32 devices in a mesh: fsdp: 8 (over z, y), tp: 4 (over x, core).
Axes of the slice: x: 2, y: 2, z: 4, core: 2. Of those that a mesh axis runs over, the one named last changes fastest.
Arguments:
- audio_states: bfloat16 [16, 1024, 1536], P('fsdp', 'tp'), may hold values from -6 to 6
- text_states: bfloat16 [16, 64, 1536], P('fsdp', 'tp'), may hold values from -6 to 6
- out_grad: bfloat16 [16, 1024, 1536], P('fsdp', 'tp'), may hold values from -6 to 6
- self_qkv: bfloat16 [3, 1536, 1536], P(None, 'fsdp', 'tp'), may hold values from -0.15625 to 0.15625
- self_out: bfloat16 [1536, 1536], P('tp', 'fsdp'), may hold values from -1.25 to 1.25
- cross_query: bfloat16 [1536, 1536], P('fsdp', 'tp'), may hold values from -0.15625 to 0.15625
- cross_kv: bfloat16 [2, 1536, 1536], P(None, 'fsdp', 'tp'), may hold values from -0.15625 to 0.15625
- cross_out: bfloat16 [1536, 1536], P('tp', 'fsdp'), may hold values from -0.625 to 0.625
- mlp_up: bfloat16 [1536, 6144], P('fsdp', 'tp'), may hold values from -0.15625 to 0.15625
- mlp_down: bfloat16 [6144, 1536], P('tp', 'fsdp'), may hold values from -0.15625 to 0.15625
- norm_gain: bfloat16 [3, 1536], P(None, 'fsdp'), may hold values from 0.099609375 to 1.8984375
- norm_bias: bfloat16 [3, 1536], P(None, 'fsdp'), may hold values from -3 to 3
Outputs:
- layer_out: bfloat16 [16, 1024, 1536], P('fsdp', 'tp')
- audio_grad: bfloat16 [16, 1024, 1536], P('fsdp', 'tp')
- text_grad: bfloat16 [16, 64, 1536], P('fsdp', 'tp')
- grad_self_qkv: float32 [3, 1536, 1536], P(None, 'fsdp', 'tp')
- grad_self_out: float32 [1536, 1536], P('tp', 'fsdp')
- grad_cross_query: float32 [1536, 1536], P('fsdp', 'tp')
- grad_cross_kv: float32 [2, 1536, 1536], P(None, 'fsdp', 'tp')
- grad_cross_out: float32 [1536, 1536], P('tp', 'fsdp')
- grad_mlp_up: float32 [1536, 6144], P('fsdp', 'tp')
- grad_mlp_down: float32 [6144, 1536], P('tp', 'fsdp')
- grad_norm_gain: float32 [3, 1536], P(None, 'fsdp')
- grad_norm_bias: float32 [3, 1536], P(None, 'fsdp')
The draws below stay inside these ranges and needn't reach their ends.
All inputs are finite; a program needn't handle non-finite values.
Results may differ from the reference program's by a relative error of at most 0.02.
Values may be sent and summed in bfloat16 or wider, within the bound.
A program may use at most 200 MiB of HBM per device.

```python
import jax
import jax.numpy as jnp
from jax import lax

D = 1536
HEAD = 64
FF = 6144
TEXT = 64
FRAMES = 1024
CLIPS = 16


def block_levels(key, shape, cuts, least, high):
    def one(axis_at, shards_of):
        heights = jax.random.uniform(jax.random.fold_in(jax.random.fold_in(key, 6), axis_at), (shards_of,), jnp.float32, least / len(cuts), high / len(cuts))
        return jnp.repeat(jnp.exp(heights), shape[axis_at] // shards_of).reshape((-1,) + (1,) * (len(shape) - axis_at - 1))

    level = one(*cuts[0])
    for cut in cuts[1:]:
        level = level * one(*cut)
    return level


def centred(own_key, extent, scale, reach, shards=(), kind=jnp.bfloat16):
    factor_of = block_levels(own_key, extent, shards, -0.22, 0.18) if shards else 1.0
    entries = jax.random.normal(own_key, extent, jnp.float32) * scale * factor_of
    return jnp.minimum(jnp.maximum(entries, -reach), reach).astype(kind)


def setup_inputs(seed: int = 0) -> dict:
    arg_keys = jax.random.split(jax.random.key(seed), 13)
    return {
        "audio_states": centred(arg_keys[0], (CLIPS, FRAMES, D), 1.0, 6.0, ((0, 8), (1, 4))),
        "text_states": centred(arg_keys[1], (CLIPS, TEXT, D), 1.0, 6.0, ((0, 8), (1, 4))),
        "out_grad": centred(arg_keys[2], (CLIPS, FRAMES, D), 1.0, 6.0, ((0, 8), (1, 4))),
        "self_qkv": centred(arg_keys[3], (3, D, D), D ** -0.5, 0.15625, ((1, 8), (2, 4))),
        "self_out": centred(arg_keys[4], (D, D), (max(D // 64, 1)) ** -0.5, 1.25, ((0, 4), (1, 8))),
        "cross_query": centred(arg_keys[5], (D, D), D ** -0.5, 0.15625, ((0, 8), (1, 4))),
        "cross_kv": centred(arg_keys[6], (2, D, D), D ** -0.5, 0.15625, ((1, 8), (2, 4))),
        "cross_out": centred(arg_keys[7], (D, D), (max(D // 16, 1)) ** -0.5, 0.625, ((0, 4), (1, 8))),
        "mlp_up": centred(arg_keys[8], (D, FF), D ** -0.5, 0.15625, ((0, 8), (1, 4))),
        "mlp_down": centred(arg_keys[9], (FF, D), (max(FF // 4, 1)) ** -0.5, 0.15625, ((0, 4), (1, 8))),
        "norm_gain": jnp.clip(1.0 + 0.18 * jax.random.normal(arg_keys[10], (3, D), jnp.float32), 0.099609375, 1.8984375).astype(jnp.bfloat16),
        "norm_bias": centred(arg_keys[11], (3, D), 0.5, 3.0, ((1, 8),)),
    }


epsilon = 1e-05

@jax.custom_vjp
def low(v):
    return lax.optimization_barrier(v.astype(jnp.bfloat16)).astype(jnp.float32)

@jax.custom_vjp
def low_back(v):
    return v

def low_keep(v):
    return (low(v), None)

def low_pass(kept, grad):
    return (grad,)

def back_keep(v):
    return (v, None)

def back_low(kept, grad):
    return (low(grad),)
low.defvjp(low_keep, low_pass)
low_back.defvjp(back_keep, back_low)

def norm_rows(stream, factor, offset):
    center = stream - lax.optimization_barrier(jnp.mean(stream, axis=-1, keepdims=True))
    spread = lax.optimization_barrier(jnp.mean(center * center, axis=-1, keepdims=True))
    return center * lax.rsqrt(spread + epsilon) * factor + offset

def attend(query_heads, key_heads, value_heads, causal):
    length = query_heads.shape[0]
    block_rows = min(512, length)
    factor = query_heads.shape[2] ** (-0.5)
    query_blocks = query_heads.reshape(length // block_rows, block_rows, query_heads.shape[1], query_heads.shape[2])
    begin_rows = jnp.arange(length // block_rows, dtype=jnp.int32) * block_rows

    def one_block(block_pair):
        piece_rows = block_pair[0]
        begin_at = block_pair[1]
        scores = jnp.einsum('qhd,khd->hqk', piece_rows, key_heads, precision=lax.Precision.HIGHEST) * factor
        scores = low_back(scores)
        if causal:
            row_at = begin_at + lax.broadcasted_iota(jnp.int32, scores.shape, 1)
            col_at = lax.broadcasted_iota(jnp.int32, scores.shape, 2)
            scores = jnp.where(row_at >= col_at, scores, -1e+30)
        attention = low(jax.nn.softmax(scores, axis=-1))
        return jnp.einsum('hqk,khd->qhd', attention, value_heads, precision=lax.Precision.HIGHEST)
    blocked = lax.map(jax.checkpoint(one_block), (query_blocks, begin_rows))
    return blocked.reshape(length, query_heads.shape[1], query_heads.shape[2])

def one_clip(stream_in, text_rows, qkv_weight, out_weight, query_weight, kv_weight, cross_weight, up_weight, down_weight, gain_rows, bias_rows):
    highest = lax.Precision.HIGHEST
    length = stream_in.shape[0]
    text_len = text_rows.shape[0]
    local_heads = qkv_weight.shape[2] // HEAD
    normed_self = low(norm_rows(stream_in, gain_rows[0], bias_rows[0]))
    qkv_rows = low_back(low(jnp.einsum('nd,cde->nce', normed_self, qkv_weight, precision=highest)))
    query_heads = qkv_rows[:, 0].reshape(length, local_heads, HEAD)
    key_heads = qkv_rows[:, 1].reshape(length, local_heads, HEAD)
    value_heads = qkv_rows[:, 2].reshape(length, local_heads, HEAD)
    self_attn = low_back(low(attend(query_heads, key_heads, value_heads, True).reshape(length, -1)))
    stream_mid = stream_in + low_back(jnp.dot(self_attn, out_weight, precision=highest))
    normed_cross = low(norm_rows(stream_mid, gain_rows[1], bias_rows[1]))
    cross_heads = low_back(low(jnp.dot(normed_cross, query_weight, precision=highest))).reshape(length, local_heads, HEAD)
    text_kv = low_back(low(jnp.einsum('td,cde->tce', text_rows, kv_weight, precision=highest)))
    text_keys = text_kv[:, 0].reshape(text_len, local_heads, HEAD)
    text_values = text_kv[:, 1].reshape(text_len, local_heads, HEAD)
    cross_attn = low_back(low(attend(cross_heads, text_keys, text_values, False).reshape(length, -1)))
    stream_late = stream_mid + low_back(jnp.dot(cross_attn, cross_weight, precision=highest))
    normed_ffn = low(norm_rows(stream_late, gain_rows[2], bias_rows[2]))
    hidden = low_back(jnp.dot(normed_ffn, up_weight, precision=highest))
    active = low(jax.nn.gelu(hidden, approximate=False))
    return stream_late + low_back(jnp.dot(active, down_weight, precision=highest))

def reference(audio_states, text_states, out_grad, self_qkv, self_out, cross_query, cross_kv, cross_out, mlp_up, mlp_down, norm_gain, norm_bias):

    def forward_all(audio_rows, text_rows, qkv_weight, out_weight, query_weight, kv_weight, cross_weight, up_weight, down_weight, gain_rows, bias_rows):

        def clip_step(clip_pair):
            return one_clip(clip_pair[0], clip_pair[1], qkv_weight, out_weight, query_weight, kv_weight, cross_weight, up_weight, down_weight, gain_rows, bias_rows)
        return lax.map(clip_step, (audio_rows, text_rows))
    primal, pullback = jax.vjp(forward_all, audio_states.astype(jnp.float32), text_states.astype(jnp.float32), self_qkv.astype(jnp.float32), self_out.astype(jnp.float32), cross_query.astype(jnp.float32), cross_kv.astype(jnp.float32), cross_out.astype(jnp.float32), mlp_up.astype(jnp.float32), mlp_down.astype(jnp.float32), norm_gain.astype(jnp.float32), norm_bias.astype(jnp.float32))
    gradients = pullback(out_grad.astype(jnp.float32))
    return (primal.astype(jnp.bfloat16), gradients[0].astype(jnp.bfloat16), gradients[1].astype(jnp.bfloat16), gradients[2], gradients[3], gradients[4], gradients[5], gradients[6], gradients[7], gradients[8], gradients[9], gradients[10])
```

```python
import functools
import math

import jax
import jax.numpy as jnp
from jax import lax
from jax.experimental import pallas as pl
from jax.experimental.pallas import tpu as pltpu
from jax.sharding import PartitionSpec as P

HEAD = 64
PAIR = 2 * HEAD
EPSILON = 1e-05
F32 = jnp.float32
BF16 = jnp.bfloat16
RATE = HEAD ** (-0.5) * math.log2(math.e)
TOKEN = (8, 128)
COST = 1000
VMEM = 44 * 2**20


def swap_chip(values):
    return lax.ppermute(values, "tp", [(t, t ^ 2) for t in range(4)])


def swap_core(values):
    return lax.ppermute(values, "tp", [(t, t ^ 1) for t in range(4)])


def place_of(share, t):
    apart = share ^ t
    return ((apart & 1) << 1) | (apart >> 1)


def gather_rows(values, swapped):
    pair = jnp.concatenate((values, swapped), axis=0)
    return pair, swap_core(pair)


def ring_of(n):
    return list(range(0, n, 2)) + list(range(n - 1, 0, -2))


def ring_place(n):
    i = lax.axis_index("fsdp")
    return jnp.where(i % 2 == 0, i // 2, n - (i + 1) // 2)


def ring_index(n, place):
    place = lax.rem(place + 2 * n, n)
    return jnp.where(place < n // 2, 2 * place, 2 * (n - place) - 1)


def send_next(values, n):
    ring = ring_of(n)
    return lax.ppermute(values, "fsdp", [(ring[k], ring[(k + 1) % n]) for k in range(n)])


def send_prev(values, n):
    ring = ring_of(n)
    return lax.ppermute(values, "fsdp", [(ring[(k + 1) % n], ring[k]) for k in range(n)])


def ring_table(n):
    return ring_index(n, ring_place(n) + jnp.arange(-(n // 2), n // 2 + 1)).astype(jnp.int32)


def place_pieces_body(n, rows, places, *refs):
    pieces, whole = refs[:-1], refs[-1]
    for piece, (step, offset) in zip(pieces, places):
        begin = ring_index(n, ring_place(n) + step) * rows + offset
        size = piece.shape[0]
        whole[pl.ds(pl.multiple_of(begin, math.gcd(rows, size)), size), :] = piece[...]


class RingGather:
    def __init__(self, shard, n):
        self.n, self.shard, self.got = n, shard, []
        self.direct = n > 16 or n % 2

    def step(self):
        if self.direct:
            return ()
        up, down = self.got[-1] if self.got else (self.shard, self.shard)
        if len(self.got) == self.n // 2 - 1:
            half = self.shard.shape[0] // 2
            up, down = up[:half], down[half:]
        self.got.append((send_next(up, self.n), send_prev(down, self.n)))
        return self.got[-1]

    def turn(self, values=(), *wait):
        if self.direct:
            return tick(list(values), *wait) if values else []
        pair = self.got[-1]
        passed = tick([*pair, *values], *wait)
        self.got[-1] = tuple(passed[:2])
        self.step()
        return passed[2:]

    def whole(self, wait=()):
        if self.direct:
            return lax.all_gather(self.shard, "fsdp", axis=0, tiled=True)
        rows, cols = self.shard.shape
        pieces, places = [self.shard], [(0, 0)]
        for k, pair in enumerate(self.got, 1):
            pieces += pair
            places += [(-k, 0), (k, 0 if k < self.n // 2 else rows // 2)]
        size = 768 if cols % 768 == 0 else cols
        return call(
            functools.partial(place_pieces_body, self.n, rows, places),
            (cols // size,),
            pieces,
            [pl.BlockSpec((v.shape[0], size), lambda i: (0, i)) for v in pieces],
            [((self.n * rows, cols), self.shard.dtype)],
            [pl.BlockSpec((self.n * rows, size), lambda i: (0, i))],
                wait=wait,
        )[0]


def ring_body(kind, rows, count, sides, *refs):
    table, wholes = refs[0], refs[1 : 1 + count]
    came = refs[1 + count : -len(sides) - count - 1]
    outs, own, sems = refs[-len(sides) - count - 1 : -count - 1], refs[-count - 1 : -1], refs[-1]
    copies = []
    for side, (entry, first, last) in enumerate(sides):
        begin = pl.multiple_of(table[entry] * rows + first, rows // 2)
        for k in range(count):
            source = wholes[k].at[pl.ds(begin, last - first), :]
            to = own[k].at[side, pl.ds(0, last - first), :]
            copies.append(pltpu.make_async_copy(source, to, sems.at[side, k]))
    for copy in copies:
        copy.start()
    for copy in copies:
        copy.wait()
    half = rows // 2
    for side, (_, first, last) in enumerate(sides):
        begin = 0
        for k in range(count):
            cols = slice(begin, begin + wholes[k].shape[1])
            begin = cols.stop
            mine = own[k][side, : last - first, :]
            if kind == "begin":
                outs[side][:, cols] = mine
            elif kind == "first":
                add = came[side][:, cols].astype(F32)
                here = slice(side * half, (side + 1) * half)
                there = slice((1 - side) * half, (2 - side) * half)
                outs[side][here, cols] = (mine[here].astype(F32) + add).astype(BF16)
                outs[side][there, cols] = mine[there]
            elif kind == "middle":
                add = came[side][:, cols].astype(F32)
                outs[side][:, cols] = (mine.astype(F32) + add).astype(BF16)
            else:
                add = came[0][:, cols].astype(F32) + came[1][:, cols].astype(F32)
                outs[side][:, cols] = mine.astype(F32) + add


class RingSum:
    def __init__(self, wholes, n, table):
        self.wholes, self.n, self.table = wholes, n, table
        self.direct = n > 16 or n % 2
        self.left = n // 2
        self.came = ()
        self.step()

    def run(self, kind, step, wait=()):
        rows = self.wholes[0].shape[0] // self.n
        half = rows // 2
        widths = [v.shape[1] for v in self.wholes]
        middle = self.n // 2
        if kind == "end":
            sides = [(middle, 0, rows)]
        elif kind == "begin":
            sides = [(middle + step, 0, half), (middle - step, half, rows)]
        else:
            sides = [(middle + step, 0, rows), (middle - step, 0, rows)]
        size = half if kind == "begin" else rows
        out = ((size, sum(widths)), F32 if kind == "end" else BF16)
        hbm = pl.BlockSpec(memory_space=pltpu.HBM)
        return call(
            functools.partial(ring_body, kind, rows, len(widths), sides),
            (1,),
            (self.table, *self.wholes, *self.came),
            [pl.BlockSpec(memory_space=pltpu.SMEM)]
            + [hbm] * len(widths)
            + [whole_spec(v.shape) for v in self.came],
            [out] * len(sides),
            [whole_spec(out[0])] * len(sides),
            [pltpu.VMEM((len(sides), rows, cols), BF16) for cols in widths]
            + [pltpu.SemaphoreType.DMA((len(sides), len(widths)))],
            wait=wait,
        )

    def step(self, wait=()):
        if self.direct or not self.left:
            return
        if self.left == self.n // 2:
            kind = "begin"
        else:
            kind = "first" if self.left == self.n // 2 - 1 else "middle"
        up, down = self.run(kind, self.left, wait)
        self.came = (send_next(up, self.n), send_prev(down, self.n))
        self.left -= 1

    def total(self):
        if self.direct:
            whole = jnp.concatenate(self.wholes, 1)
            return lax.psum_scatter(whole, "fsdp", scatter_dimension=0, tiled=True).astype(F32)
        while self.left:
            self.step()
        return self.run("end", 0)[0]


def swap_fsdp(values, n, bit):
    return lax.ppermute(values, "fsdp", [(i, i ^ bit) for i in range(n)])


def small_gather(shard, n):
    if n & (n - 1):
        return lax.all_gather(shard, "fsdp", axis=1, tiled=True)
    found = shard[None]
    bit = 1
    while bit < n:
        found = jnp.concatenate((found, swap_fsdp(found, n, bit)), axis=0)
        bit *= 2
    found = jnp.take(found, jnp.arange(n) ^ lax.axis_index("fsdp"), axis=0)
    return found.transpose(1, 0, 2).reshape(shard.shape[0], -1)


def times(rows, weight):
    return jnp.dot(rows, weight, preferred_element_type=F32)


def times_t(rows, weight):
    return lax.dot_general(rows, weight, (((1,), (1,)), ((), ())), preferred_element_type=F32)


def t_times(left, right):
    return lax.dot_general(left, right, (((0,), (0,)), ((), ())), preferred_element_type=F32)


def whole_spec(shape):
    return pl.BlockSpec(shape, lambda *_: (0,) * len(shape))


class Order:
    token = None


def call(body, grid, ins, in_specs, outs, out_specs, scratch=(), wait=(), alias=None):
    count = len(ins)
    extra = list(wait) + ([Order.token] if Order.token is not None else [])
    any_spec, hbm = (pl.BlockSpec(memory_space=space) for space in (pl.ANY, pltpu.HBM))

    def run(*refs):
        after = refs[count + len(extra) :]
        body(*refs[:count], *after[: len(outs)], *after[len(outs) + 1 :])
        after[len(outs)][...] = jnp.zeros(TOKEN, F32)

    results = pl.pallas_call(
        run,
        grid=grid,
        in_specs=list(in_specs) + [hbm] * len(wait) + [any_spec] * (len(extra) - len(wait)),
        out_specs=list(out_specs) + [whole_spec(TOKEN)],
        scratch_shapes=list(scratch),
        out_shape=[jax.ShapeDtypeStruct(s, d) for s, d in list(outs) + [(TOKEN, F32)]],
        input_output_aliases=alias or {},
        compiler_params=pltpu.CompilerParams(vmem_limit_bytes=VMEM),
        name=getattr(body, "func", body).__name__,
        cost_estimate=pl.CostEstimate(flops=COST, bytes_accessed=0, transcendentals=0),
    )(*ins, *extra)
    Order.token = results[-1]
    return results[:-1]


def head_masks(rows):
    low = lax.broadcasted_iota(jnp.int32, (rows, PAIR), 1) < HEAD
    return low, jnp.logical_not(low)


def split_heads(block, masks):
    zero = jnp.zeros_like(block)
    return [jnp.where(m, block, zero) for m in masks]


def rows_call(body, ins, outs, sums=(), wait=(), shifts=None):
    rows = outs[0][0][0]
    block = next((v for v in (128, 96) if rows % v == 0), rows)
    steps = rows // block
    shifts = shifts or [0] * len(ins)
    in_specs = []
    for v, shift in zip(ins, shifts):
        if shift is None:
            in_specs.append(whole_spec(v.shape))
        else:
            first = shift // block
            in_specs.append(
                pl.BlockSpec((block, v.shape[1]), functools.partial(lambda f, i: (i + f, 0), first))
            )
    out_specs = [pl.BlockSpec((block, shape[1]), lambda i: (i, 0)) for shape, _ in outs]
    out_specs += [whole_spec(shape) for shape, _ in sums]
    return call(
        body, (steps,), ins, in_specs, list(outs) + list(sums), out_specs, wait=wait
    )


def tick_body(*refs):
    pass


def tick(values, *wait):
    spec = pl.BlockSpec(memory_space=pl.ANY)
    count = len(values)
    return call(
        tick_body,
        (1,),
        values,
        [spec] * count,
        [(v.shape, v.dtype) for v in values],
        [spec] * count,
        wait=wait,
        alias={k: k for k in range(count)},
    )


def copy_body(from_ref, to_ref):
    to_ref[...] = from_ref[...]


def hold(values, wait=()):
    return rows_call(copy_body, (values,), [(values.shape, values.dtype)], wait=wait)[0]


def add_body(keep_ref, seen_ref, out_ref):
    out_ref[...] = (keep_ref[...] + seen_ref[...].astype(F32)).astype(BF16)


def sum_over_tp(keep, send, wait=()):
    seen = swap_core(send)
    half = keep.shape[0] // 2
    (passed,) = rows_call(
        add_body, (keep, seen), [((half, keep.shape[1]), BF16)], shifts=(half, half), wait=wait
    )
    return keep, seen, swap_chip(passed)


def total_of(refs):
    return sum(ref[...].astype(F32) for ref in refs)


def norm_forward_body(index, *refs):
    params, outs = refs[-3], refs[-2:]
    stream = total_of(refs[:-3])
    outs[0][...] = stream
    center = stream - jnp.mean(stream, axis=-1, keepdims=True)
    spread = jnp.mean(center * center, axis=-1, keepdims=True)
    gain, bias = params[index : index + 1, :], params[3 + index : 4 + index, :]
    outs[1][...] = (center * lax.rsqrt(spread + EPSILON) * gain + bias).astype(BF16)


def norm_forward(index, terms, params, rows, wait=()):
    shape = (rows, params.shape[1])
    return rows_call(
        functools.partial(norm_forward_body, index),
        (*terms, params),
        [(shape, F32), (shape, BF16)],
        shifts=[0] * len(terms) + [None],
        wait=wait,
    )


def norm_backward_body(index, count, *refs):
    stream_ref, base_ref, terms = refs[0], refs[1], refs[2 : 2 + count]
    params, outs, sums = refs[2 + count], refs[3 + count : -1], refs[-1]
    stream = stream_ref[...].astype(F32)
    center = stream - jnp.mean(stream, axis=-1, keepdims=True)
    scale = lax.rsqrt(jnp.mean(center * center, axis=-1, keepdims=True) + EPSILON)
    xhat = center * scale
    grad = total_of(terms)
    e = grad * params[index : index + 1, :]
    back = scale * (
        e - jnp.mean(e, axis=-1, keepdims=True) - xhat * jnp.mean(e * xhat, axis=-1, keepdims=True)
    )
    total = base_ref[...].astype(F32) + back
    for out in outs:
        out[...] = total.astype(out.dtype)

    @pl.when(pl.program_id(0) == 0)
    def _():
        sums[...] = jnp.zeros_like(sums)

    sums[0:1, :] += jnp.sum(grad * xhat, axis=0, keepdims=True)
    sums[1:2, :] += jnp.sum(grad, axis=0, keepdims=True)


def norm_backward(index, stream, base, terms, params, kinds):
    shape = stream.shape
    return rows_call(
        functools.partial(norm_backward_body, index, len(terms)),
        (stream, base, *terms, params),
        [(shape, kind) for kind in kinds],
        [((8, shape[1]), F32)],
        shifts=[0] * (2 + len(terms)) + [None],
    )


def sum_pair_body(left_ref, right_ref, out_ref):
    out_ref[...] = left_ref[...] + right_ref[...]


class SmallSum:
    def __init__(self, whole, n):
        self.whole, self.n = whole, n
        self.swaps = [swap_core, swap_chip]
        if n & (n - 1):
            self.whole = lax.psum(whole, "fsdp")
        else:
            bits = [2**k for k in range(n.bit_length() - 1)]
            self.swaps += [functools.partial(swap_fsdp, n=n, bit=bit) for bit in bits]
        self.came = self.swaps.pop(0)(self.whole)

    def step(self):
        if self.came is None:
            return
        shape = self.whole.shape
        (self.whole,) = call(
            sum_pair_body,
            (1,),
            (self.whole, self.came),
            [whole_spec(shape)] * 2,
            [(shape, F32)],
            [whole_spec(shape)],
        )
        self.came = self.swaps.pop(0)(self.whole) if self.swaps else None

    def total(self):
        while self.came is not None:
            self.step()
        cols = self.whole.shape[1] // self.n
        begin = lax.axis_index("fsdp") * cols
        return lax.dynamic_slice(self.whole, (0, begin), (self.whole.shape[0], cols))


def join_body(count, *refs):
    outs = refs[count]
    for k in range(count):
        outs[k] = refs[k][...]


def join(parts):
    shape, kind = parts[0].shape, parts[0].dtype
    block = 128 if shape[0] % 128 == 0 else shape[0]
    return call(
        functools.partial(join_body, len(parts)),
        (shape[0] // block,),
        parts,
        [pl.BlockSpec((block, shape[1]), lambda i: (i, 0))] * len(parts),
        [((len(parts), *shape), kind)],
        [pl.BlockSpec((len(parts), block, shape[1]), lambda i: (0, i, 0))],
    )[0]


def sum_terms_body(*refs):
    refs[-1][...] = total_of(refs[:-1]).astype(BF16)


def sum_terms(terms, shape):
    return rows_call(sum_terms_body, terms, [(shape, BF16)])[0]


def self_forward_body(
    a_ref, b_ref, w_ref, wo_ref, qkv_ref, attn_ref, lse_ref, keep_ref, send_ref, vt_ref
):
    step = pl.program_id(0)
    t = lax.axis_index("tp")
    half = a_ref.shape[0]
    share = half // 2
    qkv_ref[:half, :] = times(a_ref[...], w_ref[...]).astype(BF16)
    qkv_ref[half:, :] = times(b_ref[...], w_ref[...]).astype(BF16)
    vt_ref[...] = qkv_ref[:, 2 * PAIR :].T
    masks = head_masks(share)
    at = [pl.ds(pl.multiple_of(place_of(g, t) * share, share), share) for g in range(4)]
    seen = lax.broadcasted_iota(jnp.int32, (share, share), 0) <= lax.broadcasted_iota(
        jnp.int32, (share, share), 1
    )
    lanes = pl.ds(pl.multiple_of(step * PAIR, PAIR), PAIR)
    for g in range(4):
        queries = split_heads(qkv_ref[at[g], :PAIR], masks)
        found = []
        for e in range(2):
            scores = []
            for b in range(g + 1):
                s = times_t(qkv_ref[at[b], PAIR : 2 * PAIR], queries[e])
                scores.append(jnp.where(seen, s, -1e30) if b == g else s)
            peak = functools.reduce(
                jnp.maximum, [jnp.max(s, axis=0, keepdims=True) for s in scores]
            )
            peak = peak * RATE
            probs = [jnp.exp2(s * RATE - peak) for s in scores]
            total = sum(jnp.sum(p, axis=0, keepdims=True) for p in probs)
            rows = slice(e * HEAD, (e + 1) * HEAD)
            mixed = sum(times(vt_ref[rows, at[b]], probs[b].astype(BF16)) for b in range(g + 1))
            found.append(mixed / total)
            lse_ref[e : e + 1, at[g]] = peak + jnp.log2(total)
        attn_ref[at[g], lanes] = jnp.concatenate(found, 0).T.astype(BF16)

    @pl.when(step == pl.num_programs(0) - 1)
    def _():
        for k in range(2):
            rows = slice(k * share, (k + 1) * share)
            keep_ref[rows, :] = times_t(attn_ref[rows, :], wo_ref[...])
            late = slice(half + k * share, half + (k + 1) * share)
            send_ref[rows, :] = times_t(attn_ref[late, :], wo_ref[...]).astype(BF16)


def self_forward(a, b, weight, units):
    half, width = a.shape
    pairs = units // PAIR
    rows = 2 * half
    return call(
        self_forward_body,
        (pairs,),
        (a, b, weight, weight),
        [
            whole_spec((half, width)),
            whole_spec((half, width)),
            pl.BlockSpec((width, 3 * PAIR), lambda h: (0, h)),
            pl.BlockSpec((width, units), lambda h: (0, 3)),
        ],
        [
            ((rows, 3 * units), BF16),
            ((rows, units), BF16),
            ((8 * pairs, rows), F32),
            ((half, width), F32),
            ((half, width), BF16),
        ],
        [
            pl.BlockSpec((rows, 3 * PAIR), lambda h: (0, h)),
            whole_spec((rows, units)),
            pl.BlockSpec((8, rows), lambda h: (h, 0)),
            whole_spec((half, width)),
            whole_spec((half, width)),
        ],
        [pltpu.VMEM((PAIR, rows), BF16)],
    )


def self_backward_body(
    a_ref, b_ref, wo_ref, w_ref, qkv_ref, attn_ref, lse_ref,
    grads_ref, keep_ref, send_ref, hg_ref, kt_ref, dk_ref, dv_ref,
):
    step = pl.program_id(0)
    t = lax.axis_index("tp")
    half = a_ref.shape[0]
    share = half // 2
    hg_ref[:half, :] = times(a_ref[...], wo_ref[...]).astype(BF16)
    hg_ref[half:, :] = times(b_ref[...], wo_ref[...]).astype(BF16)
    kt_ref[...] = qkv_ref[:, PAIR : 2 * PAIR].T
    dk_ref[...] = jnp.zeros_like(dk_ref)
    dv_ref[...] = jnp.zeros_like(dv_ref)
    masks = head_masks(share)
    at = [pl.ds(pl.multiple_of(place_of(g, t) * share, share), share) for g in range(4)]
    seen = lax.broadcasted_iota(jnp.int32, (share, share), 0) <= lax.broadcasted_iota(
        jnp.int32, (share, share), 1
    )
    base = step * 3 * PAIR
    lanes = [pl.ds(pl.multiple_of(base + c * PAIR, PAIR), PAIR) for c in range(3)]
    for g in range(4):
        queries = split_heads(qkv_ref[at[g], :PAIR], masks)
        block = hg_ref[at[g], :]
        outer = split_heads(block, masks)
        inner = (block.astype(F32) * attn_ref[at[g], :].astype(F32)).T
        query_grad = []
        for e in range(2):
            rows = slice(e * HEAD, (e + 1) * HEAD)
            lse = lse_ref[e : e + 1, at[g]]
            delta = jnp.sum(inner[rows], axis=0, keepdims=True)
            total = jnp.zeros((HEAD, share), F32)
            for b in range(g + 1):
                s = times_t(qkv_ref[at[b], PAIR : 2 * PAIR], queries[e])
                probs = jnp.exp2(s * RATE - lse)
                if b == g:
                    probs = jnp.where(seen, probs, 0.0)
                grad = times_t(qkv_ref[at[b], 2 * PAIR :], outer[e])
                score_grad = (probs * (grad - delta)).astype(BF16)
                dv_ref[at[b], :] += times(probs.astype(BF16), outer[e])
                dk_ref[at[b], :] += times(score_grad, queries[e])
                total += times(kt_ref[rows, at[b]], score_grad)
            query_grad.append(total)
        query_grad = jnp.concatenate(query_grad, 0) * (HEAD ** (-0.5))
        grads_ref[at[g], lanes[0]] = query_grad.T.astype(BF16)
    grads_ref[:, lanes[1]] = (dk_ref[...] * (HEAD ** (-0.5))).astype(BF16)
    grads_ref[:, lanes[2]] = dv_ref[...].astype(BF16)

    @pl.when(step == pl.num_programs(0) - 1)
    def _():
        for k in range(2):
            rows = slice(k * share, (k + 1) * share)
            keep_ref[rows, :] = times_t(grads_ref[rows, :], w_ref[...])
            late = slice(half + k * share, half + (k + 1) * share)
            send_ref[rows, :] = times_t(grads_ref[late, :], w_ref[...]).astype(BF16)


def self_backward(a, b, weight, qkv, attn, lse):
    half, width = a.shape
    units = attn.shape[1]
    pairs = units // PAIR
    rows = 2 * half
    return call(
        self_backward_body,
        (pairs,),
        (a, b, weight, weight, qkv, attn, lse),
        [
            whole_spec((half, width)),
            whole_spec((half, width)),
            pl.BlockSpec((width, PAIR), lambda h: (0, 3 * pairs + h)),
            whole_spec((width, 3 * units)),
            pl.BlockSpec((rows, 3 * PAIR), lambda h: (0, h)),
            pl.BlockSpec((rows, PAIR), lambda h: (0, h)),
            pl.BlockSpec((8, rows), lambda h: (h, 0)),
        ],
        [
            ((rows, 3 * units), BF16),
            ((half, width), F32),
            ((half, width), BF16),
        ],
        [
            whole_spec((rows, 3 * units)),
            whole_spec((half, width)),
            whole_spec((half, width)),
        ],
        [
            pltpu.VMEM((rows, PAIR), BF16),
            pltpu.VMEM((PAIR, rows), BF16),
            pltpu.VMEM((rows, PAIR), F32),
            pltpu.VMEM((rows, PAIR), F32),
        ],
    )


def cross_weight_specs(width, units):
    return [pl.BlockSpec((width, units), functools.partial(lambda j, _: (0, j), j)) for j in (0, 2, 1, 3)]


def cross_probs(keys, queries):
    s = times_t(keys, queries)
    peak = jnp.max(s, axis=0, keepdims=True) * RATE
    probs = jnp.exp2(s * RATE - peak)
    return probs / jnp.sum(probs, axis=0, keepdims=True)


def cross_forward_body(
    a_ref, b_ref, wq0_ref, wq1_ref, wo0_ref, wo1_ref, kv0_ref, kv1_ref,
    q_ref, attn_ref, keep_ref, send_ref,
):
    share = a_ref.shape[0]
    units = wq0_ref.shape[1]
    masks = head_masks(kv0_ref.shape[0])
    keep = send = 0.0
    for j, (wq_ref, wo_ref, kv_ref) in enumerate(
        ((wq0_ref, wo0_ref, kv0_ref), (wq1_ref, wo1_ref, kv1_ref))
    ):
        cols = slice(j * units, (j + 1) * units)
        q_ref[:share, cols] = times(a_ref[...], wq_ref[...]).astype(BF16)
        q_ref[share:, cols] = times(b_ref[...], wq_ref[...]).astype(BF16)
        for begin in range(0, units, PAIR):
            lanes = slice(j * units + begin, j * units + begin + PAIR)
            queries = q_ref[:, lanes]
            keys = split_heads(kv_ref[:, begin : begin + PAIR], masks)
            values = kv_ref[:, units + begin : units + begin + PAIR].T
            mixed = [
                times(
                    values[e * HEAD : (e + 1) * HEAD],
                    cross_probs(keys[e], queries).astype(BF16),
                )
                for e in range(2)
            ]
            attn_ref[:, lanes] = jnp.concatenate(mixed, 0).T.astype(BF16)
        keep += times_t(attn_ref[:share, cols], wo_ref[...])
        send += times_t(attn_ref[share:, cols], wo_ref[...])
    keep_ref[...] = keep
    send_ref[...] = send.astype(BF16)


def cross_forward(a, b, weight, kvs):
    share, width = a.shape
    units = weight.shape[1] // 6
    ins = (a, b, *[weight] * 4, *kvs)
    outs = [
        ((2 * share, 2 * units), BF16),
        ((2 * share, 2 * units), BF16),
        ((share, width), F32),
        ((share, width), BF16),
    ]
    return call(
        cross_forward_body,
        (1,),
        ins,
        [whole_spec(v.shape) for v in ins[:2]]
        + cross_weight_specs(width, units)
        + [whole_spec(v.shape) for v in ins[6:]],
        outs,
        [whole_spec(s) for s, _ in outs],
    )


def cross_backward_body(
    a_ref, b_ref, wq0_ref, wq1_ref, wo0_ref, wo1_ref, kv0_ref, kv1_ref, q_ref,
    dq_ref, own_ref, other_ref, keep_ref, send_ref, hg_ref,
):
    share = a_ref.shape[0]
    units = wq0_ref.shape[1]
    text = kv0_ref.shape[0]
    masks = head_masks(text)
    keep = send = 0.0
    for j, (wq_ref, wo_ref, kv_ref, out_ref) in enumerate(
        ((wq0_ref, wo0_ref, kv0_ref, own_ref), (wq1_ref, wo1_ref, kv1_ref, other_ref))
    ):
        cols = slice(j * units, (j + 1) * units)
        hg_ref[:share, :] = times(a_ref[...], wo_ref[...]).astype(BF16)
        hg_ref[share:, :] = times(b_ref[...], wo_ref[...]).astype(BF16)
        for begin in range(0, units, PAIR):
            lanes = slice(j * units + begin, j * units + begin + PAIR)
            local = slice(begin, begin + PAIR)
            queries = q_ref[:, lanes]
            outer = hg_ref[:, local]
            pair_keys = kv_ref[:, local]
            keys = split_heads(pair_keys, masks)
            values = split_heads(kv_ref[:, units + begin : units + begin + PAIR], masks)
            keys_t = pair_keys.T
            query_grad, key_grad, value_grad = [], [], []
            for e in range(2):
                probs = cross_probs(keys[e], queries)
                grad = times_t(values[e], outer)
                inner = jnp.sum(probs * grad, axis=0, keepdims=True)
                score_grad = (probs * (grad - inner)).astype(BF16)
                query_grad.append(times(keys_t[e * HEAD : (e + 1) * HEAD], score_grad))
                key_grad.append(times(score_grad, queries))
                value_grad.append(times(probs.astype(BF16), outer))
            query_grad = jnp.concatenate(query_grad, 0) * (HEAD ** (-0.5))
            dq_ref[:, lanes] = query_grad.T.astype(BF16)
            key_grad = jnp.where(masks[0], *key_grad) * (HEAD ** (-0.5))
            value_grad = jnp.where(masks[0], *value_grad)
            out_ref[:, local] = key_grad.astype(out_ref.dtype)
            out_ref[:, units + begin : units + begin + PAIR] = value_grad.astype(out_ref.dtype)
        keep += times_t(dq_ref[:share, cols], wq_ref[...])
        send += times_t(dq_ref[share:, cols], wq_ref[...])
    keep_ref[...] = keep
    send_ref[...] = send.astype(BF16)


def cross_backward(a, b, weight, kvs, queries):
    share, width = a.shape
    units = weight.shape[1] // 6
    text = kvs[0].shape[0]
    ins = (a, b, *[weight] * 4, *kvs, queries)
    outs = [
        ((2 * share, 2 * units), BF16),
        ((text, 2 * units), F32),
        ((text, 2 * units), BF16),
        ((share, width), F32),
        ((share, width), BF16),
    ]
    return call(
        cross_backward_body,
        (1,),
        ins,
        [whole_spec(v.shape) for v in ins[:2]]
        + cross_weight_specs(width, units)
        + [whole_spec(v.shape) for v in ins[6:]],
        outs,
        [whole_spec(s) for s, _ in outs],
        [pltpu.VMEM((2 * share, units), BF16)],
    )


def gelu_pair(hidden):
    phi = 0.5 * (1.0 + lax.erf(hidden * (0.5**0.5)))
    density = jnp.exp(-0.5 * hidden * hidden) * 0.3989422804014327
    return hidden * phi, phi + hidden * density


def ffn_products(x, grad, up_ref, down_ref, active_ref, hidden_ref):
    units = up_ref.shape[1]
    size = units // 3 if units % (3 * 128) == 0 else units
    out = back = 0.0
    for begin in range(0, units, size):
        cols = slice(begin, begin + size)
        active, slope = gelu_pair(times(x, up_ref[:, cols]))
        active = active.astype(BF16)
        active_ref[:, cols] = active
        hidden_grad = (times(grad, down_ref[:, cols]) * slope).astype(BF16)
        hidden_ref[:, cols] = hidden_grad
        out += times_t(active, down_ref[:, cols])
        back += times_t(hidden_grad, up_ref[:, cols])
    return out, back


def ffn_first_body(
    xa_ref, xb_ref, ga_ref, gb_ref, up_ref, down_ref, active_ref, hidden_ref, out_ref, back_ref
):
    early = pl.program_id(0) < 2
    x = jnp.where(early, xa_ref[...], xb_ref[...])
    grad = jnp.where(early, ga_ref[...], gb_ref[...])
    out, back = ffn_products(x, grad, up_ref, down_ref, active_ref, hidden_ref)
    out_ref[...] = out
    back_ref[...] = back


def ffn_second_body(
    xa_ref, xb_ref, ga_ref, gb_ref, up_ref, down_ref, out_ref, back_ref,
    active_ref, hidden_ref, out_keep_ref, out_send_ref, keep_ref, send_ref,
):
    early = pl.program_id(0) < 2
    x = jnp.where(early, xa_ref[...], xb_ref[...])
    grad = jnp.where(early, ga_ref[...], gb_ref[...])
    out, back = ffn_products(x, grad, up_ref, down_ref, active_ref, hidden_ref)
    out += out_ref[...]
    back += back_ref[...]

    @pl.when(early)
    def _():
        out_keep_ref[...] = out
        keep_ref[...] = back

    @pl.when(jnp.logical_not(early))
    def _():
        out_send_ref[...] = out.astype(BF16)
        send_ref[...] = back.astype(BF16)


def ffn(x, grad, weight, partial=None):
    half, width = x[0].shape
    share = half // 2
    units = weight.shape[1] // 2
    rows = 2 * half

    def each(i):
        return (i, 0)

    def first(i):
        return (jnp.minimum(i, 1), 0)

    def second(i):
        return (jnp.maximum(i - 2, 0), 0)

    block = (share, width)
    in_specs = [
        pl.BlockSpec(block, first),
        pl.BlockSpec(block, second),
        pl.BlockSpec(block, first),
        pl.BlockSpec(block, second),
        pl.BlockSpec((width, units), lambda i: (0, 0)),
        pl.BlockSpec((width, units), lambda i: (0, 1)),
    ]
    outs = [((rows, units), BF16), ((rows, units), BF16)]
    out_specs = [pl.BlockSpec((share, units), each)] * 2
    if partial is None:
        outs += [((rows, width), F32)] * 2
        out_specs += [pl.BlockSpec(block, each)] * 2
    else:
        in_specs += [pl.BlockSpec(block, each)] * 2
        outs += [((half, width), F32), ((half, width), BF16)] * 2
        out_specs += [pl.BlockSpec(block, first), pl.BlockSpec(block, second)] * 2
    return call(
        ffn_first_body if partial is None else ffn_second_body,
        (4,),
        (*x, *grad, weight, weight, *(partial or ())),
        in_specs,
        outs,
        out_specs,
    )


def weight_grad_body(plan, lefts_count, *refs):
    lefts, rights, out = refs[:lefts_count], refs[lefts_count:-1], refs[-1]
    begin = 0
    for pairs in plan:
        cols = rights[pairs[0][1]].shape[1]
        total = 0.0
        for left, right, first in pairs:
            size = lefts[left].shape[0]
            total += t_times(lefts[left][...], rights[right][first : first + size, :])
        out[:, begin : begin + cols] = total.astype(BF16)
        begin += cols


def weight_grad(*parts):
    lefts, rights, plan = [], [], []
    for part_lefts, part_rights in parts:
        pairs = []
        right = first = 0
        for left in part_lefts:
            pairs.append((len(lefts), len(rights) + right, first))
            lefts.append(left)
            first += left.shape[0]
            if first == part_rights[right].shape[0]:
                right, first = right + 1, 0
        rights += part_rights
        plan.append(pairs)
    width = lefts[0].shape[1]
    cols = sum(part_rights[0].shape[1] for _, part_rights in parts)
    size = 256 if width % 256 == 0 else width
    return call(
        functools.partial(weight_grad_body, plan, len(lefts)),
        (width // size,),
        (*lefts, *rights),
        [pl.BlockSpec((v.shape[0], size), lambda i: (0, i)) for v in lefts]
        + [whole_spec(v.shape) for v in rights],
        [((width, cols), BF16)],
        [pl.BlockSpec((size, cols), lambda i: (i, 0))],
    )[0]


def text_project_body(text_ref, weight_ref, out_ref):
    out_ref[...] = times(text_ref[...], weight_ref[...]).astype(BF16)


def text_project(text, weight, block, cols):
    ins = (text, weight)
    specs = [whole_spec(text.shape), pl.BlockSpec((weight.shape[0], cols), lambda i: (0, block))]
    shape = (text.shape[0], cols)
    return call(text_project_body, (1,), ins, specs, [(shape, BF16)], [whole_spec(shape)])[0]


def text_back_body(half, grads_ref, weight_ref, keep_ref, send_ref):
    rows = times_t(grads_ref[...], weight_ref[...])
    for c in range(keep_ref.shape[0]):
        begin = 2 * c * half
        keep_ref[c] = rows[begin : begin + half]
        send_ref[c] = rows[begin + half : begin + 2 * half].astype(BF16)


def text_back(grads, weight, block, clips):
    width, cols = weight.shape[0], grads.shape[1]
    half = grads.shape[0] // clips // 2
    shape = (clips, half, width)
    return call(
        functools.partial(text_back_body, half),
        (1,),
        (grads, weight),
        [whole_spec(grads.shape), pl.BlockSpec((width, cols), lambda i: (0, block))],
        [(shape, F32), (shape, BF16)],
        [whole_spec(shape)] * 2,
    )


def local(
    n,
    audio_states,
    text_states,
    out_grad,
    self_qkv,
    self_out,
    cross_query,
    cross_kv,
    cross_out,
    mlp_up,
    mlp_down,
    norm_gain,
    norm_bias,
):
    clips, share, width = audio_states.shape
    units = self_out.shape[0]
    pairs = units // PAIR
    both = range(clips)

    Order.token = None
    table = ring_table(n)

    qkv_shard = self_qkv.reshape(3, -1, pairs, PAIR).transpose(1, 2, 0, 3).reshape(-1, 3 * units)
    self_ring = RingGather(jnp.concatenate((qkv_shard, self_out.T), 1), n)
    got = self_ring.step()
    params = small_gather(jnp.concatenate((norm_gain, norm_bias), 0), n).astype(F32)
    out_swapped = [swap_chip(out_grad[c]) for c in both]
    cross_own = jnp.concatenate((cross_query, cross_out.T), 1)
    cross_came = swap_chip(cross_own)
    part = mlp_up.shape[1] // 2
    ffn_shards = [
        jnp.concatenate([v[:, k * part : (k + 1) * part] for v in (mlp_up, mlp_down.T)], 1)
        for k in range(2)
    ]

    rows_in = audio_states.reshape(clips * share, width)
    cross_came, out_swapped[0] = self_ring.turn([cross_came, out_swapped[0]], params)
    cross_shard = jnp.concatenate((cross_own, cross_came, cross_kv[0], cross_kv[1]), axis=1)
    _, normed = norm_forward(0, (rows_in,), params, clips * share)
    normed = [normed[c * share : (c + 1) * share] for c in both]
    normed_swapped = [swap_chip(v) for v in normed]
    full_self = [gather_rows(normed[0], normed_swapped[0])]
    self_ring.step()
    cross_ring = RingGather(hold(cross_shard, self_ring.step()), n)
    got = cross_ring.step()
    self_w = self_ring.whole(wait=normed_swapped[1:])
    full_self += [gather_rows(normed[c], normed_swapped[c]) for c in range(1, clips)]
    seen_out = [gather_rows(out_grad[0], out_swapped[0])]
    text_pair = jnp.concatenate((text_states, swap_chip(text_states)), axis=1)
    text_full = jnp.concatenate((text_pair, swap_core(text_pair)), axis=1)
    qkv, self_attn, self_log, mid_terms = [], [], [], []
    for c in both:
        rows, attn, log, keep, send = self_forward(*full_self[c], self_w, units)
        if c == 0:
            (send,) = cross_ring.turn([send])
        else:
            keep_0, seen_0, other_0 = mid_terms[0][1:]
            send, other_0 = cross_ring.turn([send, other_0])
            mid_terms[0] = (audio_states[0], keep_0, seen_0, other_0)
        mid_terms.append((audio_states[c], *sum_over_tp(keep, send)))
        qkv.append(rows)
        self_attn.append(attn)
        self_log.append(log)
    stream_mid, cross_rows = [], []
    for c in both:
        stream, normed = norm_forward(1, mid_terms[c], params, share)
        stream_mid.append(stream)
        cross_rows.append((normed, swap_core(normed)))
    cross_ring.turn()
    early_gather = RingGather(hold(ffn_shards[0], cross_ring.got[-1] if cross_ring.got else ()), n)
    early_gather.step()
    cross_w = cross_ring.whole(wait=out_swapped[1:])
    seen_out += [gather_rows(out_grad[c], out_swapped[c]) for c in range(1, clips)]
    text_rows = text_full.reshape(-1, width)
    text_kv = text_project(text_rows, cross_w, 2, 2 * units).reshape(clips, -1, 2 * units)
    text_other = swap_chip(text_kv)
    early_gather.turn()
    cross_q, cross_attn, stream_late, full_ffn = [], [], [], []
    for c in both:
        queries, attn, keep, send = cross_forward(
            *cross_rows[c], cross_w, (text_kv[c], text_other[c])
        )
        if c:
            send, came = early_gather.turn([send, came])
            full_ffn.append(gather_rows(normed_late, came))
        cross_q.append(queries)
        cross_attn.append(attn)
        stream, normed = norm_forward(2, (stream_mid[c], keep, swap_core(send)), params, share)
        stream_late.append(stream)
        normed_late, came = normed, swap_chip(normed)
        if c == 0:
            early_gather.turn()
    late_gather = RingGather(hold(ffn_shards[1], early_gather.got[-1] if early_gather.got else ()), n)
    late_gather.step()
    early_w = early_gather.whole()

    actives, hiddens, partials = [[], []], [[], []], []
    for c in both:
        active, hidden, *partial = ffn(full_ffn[c], seen_out[c], early_w)
        if c == 0:
            active, came = late_gather.turn([active, came])
            full_ffn.append(gather_rows(normed_late, came))
        else:
            (active,) = late_gather.turn([active])
        actives[0].append(active)
        hiddens[0].append(hidden)
        partials.append(partial)
    grad = weight_grad((sum(full_ffn, ()), hiddens[0]), (sum(seen_out, ()), actives[0]))
    (grad,) = late_gather.turn([grad])
    late_w = late_gather.whole()

    def sum_clips(grad):
        return lax.psum_scatter(grad, "fsdp", scatter_dimension=0, tiled=True)

    ffn_totals = [sum_clips(grad)]
    back_terms, out_terms = [], []
    for c in both:
        active, hidden, out_keep, out_send, keep, send = ffn(
            full_ffn[c], seen_out[c], late_w, partials[c]
        )
        if c:
            (send,) = tick([send], back_terms[0][-1])
        back_terms.append(sum_over_tp(keep, send))
        out_terms.append((out_keep, out_send))
        actives[1].append(active)
        hiddens[1].append(hidden)

    norm_sums = [[], [], []]
    grad_mid, grad_in, seen_mid, seen_in = [], [], [], []
    cross_grads, own_kv, other_kv, terms, branches = [], [], [], [], []
    def late_back(c):
        grad, branch, sums = norm_backward(
            2, stream_late[c], out_grad[c], back_terms[c], params, (F32, BF16)
        )
        norm_sums[2].append(sums)
        grad_mid.append(grad)
        seen_mid.append((branch, swap_core(branch)))

    def cross_back(c):
        dq, own, other, keep, send = cross_backward(
            *seen_mid[c], cross_w, (text_kv[c], text_other[c]), cross_q[c]
        )
        cross_grads.append(dq)
        own_kv.append(own)
        other_kv.append(other)
        terms.append((keep, swap_core(send)))

    def mid_back(c):
        grad, branch, sums = norm_backward(
            1, stream_mid[c], grad_mid[c], terms[c], params, (F32, BF16)
        )
        norm_sums[1].append(sums)
        grad_in.append(grad)
        branches.append((branch, swap_chip(branch)))

    late_back(0)
    wide = weight_grad((sum(full_ffn, ()), hiddens[1]), (sum(seen_out, ()), actives[1]))
    wide, other = tick([wide, back_terms[1][-1]])
    back_terms[1] = (*back_terms[1][:-1], other)
    ffn_totals.append(sum_clips(wide))
    for c in both:
        cross_back(c)
        if c + 1 < clips:
            late_back(c + 1)
        mid_back(c)
    kv_came = swap_chip(jnp.stack(other_kv))
    wide = weight_grad((sum(cross_rows, ()), cross_grads), (sum(seen_mid, ()), cross_attn))
    wide, came = tick([wide, branches[0][1]])
    seen_in = [gather_rows(branches[0][0], came)]
    seen_in += [gather_rows(*branches[c]) for c in range(1, clips)]
    cross_shares = [
        jnp.concatenate([wide[:, k * units : (k + 1) * units] for k in (first, first + 2)], 1)
        for first in range(2)
    ]
    cross_came = swap_chip(cross_shares[1])

    self_grads, in_terms, out_sums = [], [], []
    for c in both:
        grads, keep, send = self_backward(
            *seen_in[c], self_w, qkv[c], self_attn[c], self_log[c]
        )
        if c == 0:
            send, kv_came = tick([send, kv_came])
        else:
            send, cross_came, text_came = tick([send, cross_came, text_came], *out_sum.came)
            out_sum.step()
        in_terms.append(sum_over_tp(keep, send))
        self_grads.append(grads)
        if c == 0:
            kv_grads = (jnp.stack(own_kv) + kv_came.astype(F32)).astype(BF16)
            kv_rows = kv_grads.reshape(-1, 2 * units)
            grad = weight_grad((sum(seen_in, ()), self_attn), ([text_rows], [kv_rows]))
            out_sum = RingSum([grad], n, table)
            text_keep, text_send = text_back(kv_rows, cross_w, 2, clips)
            quarter = text_keep.shape[1] // 2
            text_seen = text_keep + swap_core(text_send).astype(F32)
            text_came = swap_chip(text_seen[:, quarter:].astype(BF16))
        else:
            cross_total = sum_clips(
                (cross_shares[0].astype(F32) + cross_came.astype(F32)).astype(BF16)
            )
    text_grad = text_seen[:, :quarter] + text_came.astype(F32)
    grad = weight_grad((sum(full_self, ()), self_grads))
    qkv_sum = RingSum([grad], n, table)
    out_sum.step()
    late_terms = [sum_over_tp(*out_terms[c]) for c in both]
    audio_grad, layer_out = [], []
    for c in both:
        grad, sums = norm_backward(0, audio_states[c], grad_in[c], in_terms[c], params, (BF16,))
        norm_sums[0].append(sums)
        audio_grad.append(grad)
        if c == 0:
            qkv_sum.step()
            out_sum.step()
    norm_total = SmallSum(jnp.concatenate([sum(v) for v in norm_sums], 0), n)
    audio_grad = join(audio_grad)
    norm_total.step()
    norm_total.step()
    qkv_sum.step()
    out_total = out_sum.total()
    norm_total.step()
    layer_out.append(sum_terms((stream_late[0], *late_terms[0]), (share, width)))
    norm_total.step()
    qkv_sum.step()
    for c in range(1, clips):
        layer_out.append(sum_terms((stream_late[c], *late_terms[c]), (share, width)))
    layer_out = join(layer_out)
    norm_total = norm_total.total()
    qkv_total = qkv_sum.total()

    def cut(total, begin, count=1):
        return total[:, begin * units : (begin + count) * units]

    qkv_total = qkv_total.reshape(-1, pairs, 3, PAIR).transpose(2, 0, 1, 3)
    return (
        layer_out,
        audio_grad,
        text_grad.astype(BF16),
        qkv_total.reshape(3, -1, units),
        cut(out_total, 0).T,
        cut(cross_total, 0).astype(F32),
        jnp.stack((cut(out_total, 1), cut(out_total, 2))),
        cut(cross_total, 1).astype(F32).T,
        jnp.concatenate([v[:, :part] for v in ffn_totals], 1).astype(F32),
        jnp.concatenate([v[:, part:] for v in ffn_totals], 1).astype(F32).T,
        norm_total[0::8],
        norm_total[1::8],
    )


def solution(mesh):
    n = mesh.shape["fsdp"]

    def body(*args):
        return local(n, *args)

    return jax.shard_map(
        body,
        mesh=mesh,
        in_specs=(
            P("fsdp", "tp", None),
            P("fsdp", "tp", None),
            P("fsdp", "tp", None),
            P(None, "fsdp", "tp"),
            P("tp", "fsdp"),
            P("fsdp", "tp"),
            P(None, "fsdp", "tp"),
            P("tp", "fsdp"),
            P("fsdp", "tp"),
            P("tp", "fsdp"),
            P(None, "fsdp"),
            P(None, "fsdp"),
        ),
        out_specs=(
            P("fsdp", "tp", None),
            P("fsdp", "tp", None),
            P("fsdp", "tp", None),
            P(None, "fsdp", "tp"),
            P("tp", "fsdp"),
            P("fsdp", "tp"),
            P(None, "fsdp", "tp"),
            P("tp", "fsdp"),
            P("fsdp", "tp"),
            P("tp", "fsdp"),
            P(None, "fsdp"),
            P(None, "fsdp"),
        ),
        check_vma=False,
    )
```

```python
import functools
import math

import jax
import jax.numpy as jnp
from jax import lax
from jax.experimental import pallas as pl
from jax.experimental.pallas import tpu as pltpu
from jax.sharding import PartitionSpec as P

HEAD = 64
PAIR = 2 * HEAD
EPSILON = 1e-05
F32 = jnp.float32
BF16 = jnp.bfloat16
RATE = HEAD ** (-0.5) * math.log2(math.e)
TOKEN = (8, 128)
COST = 1000
VMEM = 52 * 2**20


def swap_chip(values):
    return lax.ppermute(values, "tp", [(t, t ^ 2) for t in range(4)])


def swap_core(values):
    return lax.ppermute(values, "tp", [(t, t ^ 1) for t in range(4)])


def place_of(share, t):
    apart = share ^ t
    return ((apart & 1) << 1) | (apart >> 1)


def gather_rows(values, swapped):
    pair = jnp.concatenate((values, swapped), axis=0)
    return pair, swap_core(pair)


def ring_of(n):
    return list(range(0, n, 2)) + list(range(n - 1, 0, -2))


def ring_place(n):
    i = lax.axis_index("fsdp")
    return jnp.where(i % 2 == 0, i // 2, n - (i + 1) // 2)


def ring_index(n, place):
    place = lax.rem(place + 2 * n, n)
    return jnp.where(place < n // 2, 2 * place, 2 * (n - place) - 1)


def send_next(values, n):
    ring = ring_of(n)
    return lax.ppermute(values, "fsdp", [(ring[k], ring[(k + 1) % n]) for k in range(n)])


def send_prev(values, n):
    ring = ring_of(n)
    return lax.ppermute(values, "fsdp", [(ring[(k + 1) % n], ring[k]) for k in range(n)])


def ring_table(n):
    return ring_index(n, ring_place(n) + jnp.arange(-(n // 2), n // 2 + 1)).astype(jnp.int32)


def place_pieces_body(n, rows, places, *refs):
    pieces, whole = refs[:-1], refs[-1]
    for piece, (step, offset) in zip(pieces, places):
        begin = ring_index(n, ring_place(n) + step) * rows + offset
        size = piece.shape[0]
        whole[pl.ds(pl.multiple_of(begin, math.gcd(rows, size)), size), :] = piece[...]


class RingGather:
    def __init__(self, shard, n):
        self.n, self.shard, self.got = n, shard, []
        self.direct = n > 16 or n % 2

    def step(self):
        if self.direct:
            return ()
        up, down = self.got[-1] if self.got else (self.shard, self.shard)
        if len(self.got) == self.n // 2 - 1:
            half = self.shard.shape[0] // 2
            up, down = up[:half], down[half:]
        self.got.append((send_next(up, self.n), send_prev(down, self.n)))
        return self.got[-1]

    def turn(self, values=(), *wait):
        if self.direct:
            return tick(list(values), *wait) if values else []
        pair = self.got[-1]
        passed = tick([*pair, *values], *wait)
        self.got[-1] = tuple(passed[:2])
        self.step()
        return passed[2:]

    def whole(self, wait=()):
        if self.direct:
            return lax.all_gather(self.shard, "fsdp", axis=0, tiled=True)
        rows, cols = self.shard.shape
        pieces, places = [self.shard], [(0, 0)]
        for k, pair in enumerate(self.got, 1):
            pieces += pair
            places += [(-k, 0), (k, 0 if k < self.n // 2 else rows // 2)]
        size = 768 if cols % 768 == 0 else cols
        return call(
            functools.partial(place_pieces_body, self.n, rows, places),
            (cols // size,),
            pieces,
            [pl.BlockSpec((v.shape[0], size), lambda i: (0, i)) for v in pieces],
            [((self.n * rows, cols), self.shard.dtype)],
            [pl.BlockSpec((self.n * rows, size), lambda i: (0, i))],
                wait=wait,
        )[0]


def ring_body(kind, rows, count, sides, split, *refs):
    table, wholes = refs[0], refs[1 : 1 + count]
    came = refs[1 + count : -len(sides) - count - 1]
    outs, own, sems = refs[-len(sides) - count - 1 : -count - 1], refs[-count - 1 : -1], refs[-1]
    copies = []
    for side, (entry, first, last) in enumerate(sides):
        begin = pl.multiple_of(table[entry] * rows + first, rows // 2)
        for k in range(count):
            source = wholes[k].at[pl.ds(begin, last - first), :]
            to = own[k].at[side, pl.ds(0, last - first), :]
            copies.append(pltpu.make_async_copy(source, to, sems.at[side, k]))
    for copy in copies:
        copy.start()
    for copy in copies:
        copy.wait()
    half = rows // 2
    for side, (_, first, last) in enumerate(sides):
        begin = 0
        for k in range(count):
            cols = slice(begin, begin + wholes[k].shape[1])
            begin = cols.stop
            mine = own[k][side, : last - first, :]
            if kind == "begin":
                outs[side][:, cols] = mine
            elif kind == "first":
                add = came[side][:, cols].astype(F32)
                here = slice(side * half, (side + 1) * half)
                there = slice((1 - side) * half, (2 - side) * half)
                outs[side][here, cols] = (mine[here].astype(F32) + add).astype(BF16)
                outs[side][there, cols] = mine[there]
            elif kind == "middle":
                add = came[side][:, cols].astype(F32)
                outs[side][:, cols] = (mine.astype(F32) + add).astype(BF16)
            else:
                total = came[0][:, cols].astype(F32) + came[1][:, cols].astype(F32)
                total += mine.astype(F32)
                if split is None:
                    outs[side][:, cols] = total
                else:
                    outer, inner = split
                    size = total.shape[1] // (outer * inner)
                    for at in range(outer * inner):
                        to = pl.ds(at // inner * size, size)
                        outs[side][at % inner, :, to] = total[:, at * size : (at + 1) * size]


class RingSum:
    def __init__(self, wholes, n, table):
        self.wholes, self.n, self.table = wholes, n, table
        self.direct = n > 16 or n % 2
        self.left = n // 2
        self.came = ()
        self.step()

    def run(self, kind, step, wait=(), split=None):
        rows = self.wholes[0].shape[0] // self.n
        half = rows // 2
        widths = [v.shape[1] for v in self.wholes]
        middle = self.n // 2
        if kind == "end":
            sides = [(middle, 0, rows)]
        elif kind == "begin":
            sides = [(middle + step, 0, half), (middle - step, half, rows)]
        else:
            sides = [(middle + step, 0, rows), (middle - step, 0, rows)]
        size = half if kind == "begin" else rows
        shape = (size, sum(widths))
        if split is not None:
            shape = (split[1], size, shape[1] // split[1])
        out = (shape, F32 if kind == "end" else BF16)
        hbm = pl.BlockSpec(memory_space=pltpu.HBM)
        return call(
            functools.partial(ring_body, kind, rows, len(widths), sides, split),
            (1,),
            (self.table, *self.wholes, *self.came),
            [pl.BlockSpec(memory_space=pltpu.SMEM)]
            + [hbm] * len(widths)
            + [whole_spec(v.shape) for v in self.came],
            [out] * len(sides),
            [whole_spec(out[0])] * len(sides),
            [pltpu.VMEM((len(sides), rows, cols), BF16) for cols in widths]
            + [pltpu.SemaphoreType.DMA((len(sides), len(widths)))],
            wait=wait,
        )

    def step(self, wait=()):
        if self.direct or not self.left:
            return
        if self.left == self.n // 2:
            kind = "begin"
        else:
            kind = "first" if self.left == self.n // 2 - 1 else "middle"
        up, down = self.run(kind, self.left, wait)
        self.came = (send_next(up, self.n), send_prev(down, self.n))
        self.left -= 1

    def total(self, split=None):
        if self.direct:
            whole = jnp.concatenate(self.wholes, 1)
            total = lax.psum_scatter(whole, "fsdp", scatter_dimension=0, tiled=True).astype(F32)
            if split is not None:
                total = total.reshape(total.shape[0], *split, -1).transpose(2, 0, 1, 3)
                total = total.reshape(*total.shape[:2], -1)
            return total
        while self.left:
            self.step()
        return self.run("end", 0, split=split)[0]


def swap_fsdp(values, n, bit):
    return lax.ppermute(values, "fsdp", [(i, i ^ bit) for i in range(n)])


def small_gather(shard, n):
    if n & (n - 1):
        return lax.all_gather(shard, "fsdp", axis=1, tiled=True)
    found = shard[None]
    bit = 1
    while bit < n:
        found = jnp.concatenate((found, swap_fsdp(found, n, bit)), axis=0)
        bit *= 2
    found = jnp.take(found, jnp.arange(n) ^ lax.axis_index("fsdp"), axis=0)
    return found.transpose(1, 0, 2).reshape(shard.shape[0], -1)


def times(rows, weight):
    return jnp.dot(rows, weight, preferred_element_type=F32)


def times_t(rows, weight):
    return lax.dot_general(rows, weight, (((1,), (1,)), ((), ())), preferred_element_type=F32)


def t_times(left, right):
    return lax.dot_general(left, right, (((0,), (0,)), ((), ())), preferred_element_type=F32)


def whole_spec(shape):
    return pl.BlockSpec(shape, lambda *_: (0,) * len(shape))


class Order:
    token = None


def call(body, grid, ins, in_specs, outs, out_specs, scratch=(), wait=(), alias=None):
    count = len(ins)
    extra = list(wait) + ([Order.token] if Order.token is not None else [])
    any_spec, hbm = (pl.BlockSpec(memory_space=space) for space in (pl.ANY, pltpu.HBM))

    def run(*refs):
        after = refs[count + len(extra) :]
        body(*refs[:count], *after[: len(outs)], *after[len(outs) + 1 :])
        after[len(outs)][...] = jnp.zeros(TOKEN, F32)

    results = pl.pallas_call(
        run,
        grid=grid,
        in_specs=list(in_specs) + [hbm] * len(wait) + [any_spec] * (len(extra) - len(wait)),
        out_specs=list(out_specs) + [whole_spec(TOKEN)],
        scratch_shapes=list(scratch),
        out_shape=[jax.ShapeDtypeStruct(s, d) for s, d in list(outs) + [(TOKEN, F32)]],
        input_output_aliases=alias or {},
        compiler_params=pltpu.CompilerParams(vmem_limit_bytes=VMEM),
        name=getattr(body, "func", body).__name__,
        cost_estimate=pl.CostEstimate(flops=COST, bytes_accessed=0, transcendentals=0),
    )(*ins, *extra)
    Order.token = results[-1]
    return results[:-1]


def head_masks(rows):
    low = lax.broadcasted_iota(jnp.int32, (rows, PAIR), 1) < HEAD
    return low, jnp.logical_not(low)


def split_heads(block, masks):
    zero = jnp.zeros_like(block)
    return [jnp.where(m, block, zero) for m in masks]


def rows_call(body, ins, outs, sums=(), wait=(), shifts=None):
    rows = outs[0][0][0]
    block = next((v for v in (128, 96) if rows % v == 0), rows)
    steps = rows // block
    shifts = shifts or [0] * len(ins)
    in_specs = []
    for v, shift in zip(ins, shifts):
        if shift is None:
            in_specs.append(whole_spec(v.shape))
        else:
            first = shift // block
            in_specs.append(
                pl.BlockSpec((block, v.shape[1]), functools.partial(lambda f, i: (i + f, 0), first))
            )
    out_specs = [pl.BlockSpec((block, shape[1]), lambda i: (i, 0)) for shape, _ in outs]
    out_specs += [whole_spec(shape) for shape, _ in sums]
    return call(
        body, (steps,), ins, in_specs, list(outs) + list(sums), out_specs, wait=wait
    )


def tick_body(*refs):
    pass


def tick(values, *wait):
    spec = pl.BlockSpec(memory_space=pl.ANY)
    count = len(values)
    return call(
        tick_body,
        (1,),
        values,
        [spec] * count,
        [(v.shape, v.dtype) for v in values],
        [spec] * count,
        wait=wait,
        alias={k: k for k in range(count)},
    )


def copy_body(from_ref, to_ref):
    to_ref[...] = from_ref[...]


def hold(values, wait=()):
    return rows_call(copy_body, (values,), [(values.shape, values.dtype)], wait=wait)[0]


def add_body(keep_ref, seen_ref, out_ref):
    out_ref[...] = (keep_ref[...] + seen_ref[...].astype(F32)).astype(BF16)


def sum_over_tp(keep, send, wait=()):
    seen = swap_core(send)
    half = keep.shape[0] // 2
    (passed,) = rows_call(
        add_body, (keep, seen), [((half, keep.shape[1]), BF16)], shifts=(half, half), wait=wait
    )
    return keep, seen, swap_chip(passed)


def total_of(refs):
    return sum(ref[...].astype(F32) for ref in refs)


def norm_forward_body(index, *refs):
    params, outs = refs[-3], refs[-2:]
    stream = total_of(refs[:-3])
    outs[0][...] = stream
    center = stream - jnp.mean(stream, axis=-1, keepdims=True)
    spread = jnp.mean(center * center, axis=-1, keepdims=True)
    gain, bias = params[index : index + 1, :], params[3 + index : 4 + index, :]
    outs[1][...] = (center * lax.rsqrt(spread + EPSILON) * gain + bias).astype(BF16)


def norm_forward(index, terms, params, rows, wait=()):
    shape = (rows, params.shape[1])
    return rows_call(
        functools.partial(norm_forward_body, index),
        (*terms, params),
        [(shape, F32), (shape, BF16)],
        shifts=[0] * len(terms) + [None],
        wait=wait,
    )


def norm_pair_body(index, left_ref, right_ref, params, *outs):
    gain, bias = params[index : index + 1, :], params[3 + index : 4 + index, :]
    for ref, out in zip((left_ref, right_ref), outs):
        stream = ref[...].astype(F32)
        center = stream - jnp.mean(stream, axis=-1, keepdims=True)
        spread = jnp.mean(center * center, axis=-1, keepdims=True)
        out[...] = (center * lax.rsqrt(spread + EPSILON) * gain + bias).astype(BF16)


def norm_pair(index, pair, params):
    return tuple(
        rows_call(
            functools.partial(norm_pair_body, index),
            (*pair, params),
            [(v.shape, BF16) for v in pair],
            shifts=[0, 0, None],
        )
    )


def norm_backward_body(index, count, *refs):
    stream_ref, base_ref, terms = refs[0], refs[1], refs[2 : 2 + count]
    params, outs, sums = refs[2 + count], refs[3 + count : -1], refs[-1]
    stream = stream_ref[...].astype(F32)
    center = stream - jnp.mean(stream, axis=-1, keepdims=True)
    scale = lax.rsqrt(jnp.mean(center * center, axis=-1, keepdims=True) + EPSILON)
    xhat = center * scale
    grad = total_of(terms)
    e = grad * params[index : index + 1, :]
    back = scale * (
        e - jnp.mean(e, axis=-1, keepdims=True) - xhat * jnp.mean(e * xhat, axis=-1, keepdims=True)
    )
    total = base_ref[...].astype(F32) + back
    for out in outs:
        out[...] = total.astype(out.dtype)

    @pl.when(pl.program_id(0) == 0)
    def _():
        sums[...] = jnp.zeros_like(sums)

    sums[0:1, :] += jnp.sum(grad * xhat, axis=0, keepdims=True)
    sums[1:2, :] += jnp.sum(grad, axis=0, keepdims=True)


def norm_backward(index, stream, base, terms, params, kinds):
    shape = stream.shape
    return rows_call(
        functools.partial(norm_backward_body, index, len(terms)),
        (stream, base, *terms, params),
        [(shape, kind) for kind in kinds],
        [((8, shape[1]), F32)],
        shifts=[0] * (2 + len(terms)) + [None],
    )


def sum_pair_body(left_ref, right_ref, out_ref):
    out_ref[...] = left_ref[...] + right_ref[...]


class SmallSum:
    def __init__(self, whole, n):
        self.whole, self.n = whole, n
        self.swaps = [swap_core, swap_chip]
        if n & (n - 1):
            self.whole = lax.psum(whole, "fsdp")
        else:
            bits = [2**k for k in range(n.bit_length() - 1)]
            self.swaps += [functools.partial(swap_fsdp, n=n, bit=bit) for bit in bits]
        self.came = self.swaps.pop(0)(self.whole)

    def step(self):
        if self.came is None:
            return
        shape = self.whole.shape
        (self.whole,) = call(
            sum_pair_body,
            (1,),
            (self.whole, self.came),
            [whole_spec(shape)] * 2,
            [(shape, F32)],
            [whole_spec(shape)],
        )
        self.came = self.swaps.pop(0)(self.whole) if self.swaps else None

    def total(self):
        while self.came is not None:
            self.step()
        cols = self.whole.shape[1] // self.n
        begin = lax.axis_index("fsdp") * cols
        return lax.dynamic_slice(self.whole, (0, begin), (self.whole.shape[0], cols))


def join_body(count, *refs):
    outs = refs[count]
    for k in range(count):
        outs[k] = refs[k][...]


def join(parts):
    shape, kind = parts[0].shape, parts[0].dtype
    block = 128 if shape[0] % 128 == 0 else shape[0]
    return call(
        functools.partial(join_body, len(parts)),
        (shape[0] // block,),
        parts,
        [pl.BlockSpec((block, shape[1]), lambda i: (i, 0))] * len(parts),
        [((len(parts), *shape), kind)],
        [pl.BlockSpec((len(parts), block, shape[1]), lambda i: (0, i, 0))],
    )[0]


def sum_terms_body(*refs):
    refs[-1][...] = total_of(refs[:-1]).astype(BF16)


def sum_terms(terms, shape):
    return rows_call(sum_terms_body, terms, [(shape, BF16)])[0]


def self_forward_body(
    a_ref, b_ref, w_ref, wo_ref, qkv_ref, attn_ref, lse_ref, keep_ref, send_ref, vt_ref
):
    step = pl.program_id(0)
    t = lax.axis_index("tp")
    half = a_ref.shape[0]
    share = half // 2
    qkv_ref[:half, :] = times(a_ref[...], w_ref[...]).astype(BF16)
    qkv_ref[half:, :] = times(b_ref[...], w_ref[...]).astype(BF16)
    vt_ref[...] = qkv_ref[:, 2 * PAIR :].T
    masks = head_masks(share)
    at = [pl.ds(pl.multiple_of(place_of(g, t) * share, share), share) for g in range(4)]
    seen = lax.broadcasted_iota(jnp.int32, (share, share), 0) <= lax.broadcasted_iota(
        jnp.int32, (share, share), 1
    )
    lanes = pl.ds(pl.multiple_of(step * PAIR, PAIR), PAIR)
    for g in range(4):
        queries = split_heads(qkv_ref[at[g], :PAIR], masks)
        found = []
        for e in range(2):
            scores = []
            for b in range(g + 1):
                s = times_t(qkv_ref[at[b], PAIR : 2 * PAIR], queries[e])
                scores.append(jnp.where(seen, s, -1e30) if b == g else s)
            peak = functools.reduce(
                jnp.maximum, [jnp.max(s, axis=0, keepdims=True) for s in scores]
            )
            peak = peak * RATE
            probs = [jnp.exp2(s * RATE - peak) for s in scores]
            total = sum(jnp.sum(p, axis=0, keepdims=True) for p in probs)
            rows = slice(e * HEAD, (e + 1) * HEAD)
            mixed = sum(times(vt_ref[rows, at[b]], probs[b].astype(BF16)) for b in range(g + 1))
            found.append(mixed / total)
            lse_ref[e : e + 1, at[g]] = peak + jnp.log2(total)
        attn_ref[at[g], lanes] = jnp.concatenate(found, 0).T.astype(BF16)

    @pl.when(step == pl.num_programs(0) - 1)
    def _():
        for k in range(2):
            rows = slice(k * share, (k + 1) * share)
            keep_ref[rows, :] = times_t(attn_ref[rows, :], wo_ref[...])
            late = slice(half + k * share, half + (k + 1) * share)
            send_ref[rows, :] = times_t(attn_ref[late, :], wo_ref[...]).astype(BF16)


def self_forward(a, b, weight, units):
    half, width = a.shape
    pairs = units // PAIR
    rows = 2 * half
    return call(
        self_forward_body,
        (pairs,),
        (a, b, weight, weight),
        [
            whole_spec((half, width)),
            whole_spec((half, width)),
            pl.BlockSpec((width, 3 * PAIR), lambda h: (0, h)),
            pl.BlockSpec((width, units), lambda h: (0, 3)),
        ],
        [
            ((rows, 3 * units), BF16),
            ((rows, units), BF16),
            ((8 * pairs, rows), F32),
            ((half, width), F32),
            ((half, width), BF16),
        ],
        [
            pl.BlockSpec((rows, 3 * PAIR), lambda h: (0, h)),
            whole_spec((rows, units)),
            pl.BlockSpec((8, rows), lambda h: (h, 0)),
            whole_spec((half, width)),
            whole_spec((half, width)),
        ],
        [pltpu.VMEM((PAIR, rows), BF16)],
    )


def self_backward_body(
    a_ref, b_ref, wo_ref, w_ref, qkv_ref, attn_ref, lse_ref,
    grads_ref, keep_ref, send_ref, hg_ref, kt_ref, dk_ref, dv_ref,
):
    step = pl.program_id(0)
    t = lax.axis_index("tp")
    half = a_ref.shape[0]
    share = half // 2
    hg_ref[:half, :] = times(a_ref[...], wo_ref[...]).astype(BF16)
    hg_ref[half:, :] = times(b_ref[...], wo_ref[...]).astype(BF16)
    kt_ref[...] = qkv_ref[:, PAIR : 2 * PAIR].T
    dk_ref[...] = jnp.zeros_like(dk_ref)
    dv_ref[...] = jnp.zeros_like(dv_ref)
    masks = head_masks(share)
    at = [pl.ds(pl.multiple_of(place_of(g, t) * share, share), share) for g in range(4)]
    seen = lax.broadcasted_iota(jnp.int32, (share, share), 0) <= lax.broadcasted_iota(
        jnp.int32, (share, share), 1
    )
    base = step * 3 * PAIR
    lanes = [pl.ds(pl.multiple_of(base + c * PAIR, PAIR), PAIR) for c in range(3)]
    for g in range(4):
        queries = split_heads(qkv_ref[at[g], :PAIR], masks)
        block = hg_ref[at[g], :]
        outer = split_heads(block, masks)
        inner = (block.astype(F32) * attn_ref[at[g], :].astype(F32)).T
        query_grad = []
        for e in range(2):
            rows = slice(e * HEAD, (e + 1) * HEAD)
            lse = lse_ref[e : e + 1, at[g]]
            delta = jnp.sum(inner[rows], axis=0, keepdims=True)
            total = jnp.zeros((HEAD, share), F32)
            for b in range(g + 1):
                s = times_t(qkv_ref[at[b], PAIR : 2 * PAIR], queries[e])
                probs = jnp.exp2(s * RATE - lse)
                if b == g:
                    probs = jnp.where(seen, probs, 0.0)
                grad = times_t(qkv_ref[at[b], 2 * PAIR :], outer[e])
                score_grad = (probs * (grad - delta)).astype(BF16)
                dv_ref[at[b], :] += times(probs.astype(BF16), outer[e])
                dk_ref[at[b], :] += times(score_grad, queries[e])
                total += times(kt_ref[rows, at[b]], score_grad)
            query_grad.append(total)
        query_grad = jnp.concatenate(query_grad, 0) * (HEAD ** (-0.5))
        grads_ref[at[g], lanes[0]] = query_grad.T.astype(BF16)
    grads_ref[:, lanes[1]] = (dk_ref[...] * (HEAD ** (-0.5))).astype(BF16)
    grads_ref[:, lanes[2]] = dv_ref[...].astype(BF16)

    @pl.when(step == pl.num_programs(0) - 1)
    def _():
        for k in range(2):
            rows = slice(k * share, (k + 1) * share)
            keep_ref[rows, :] = times_t(grads_ref[rows, :], w_ref[...])
            late = slice(half + k * share, half + (k + 1) * share)
            send_ref[rows, :] = times_t(grads_ref[late, :], w_ref[...]).astype(BF16)


def self_backward(a, b, weight, qkv, attn, lse):
    half, width = a.shape
    units = attn.shape[1]
    pairs = units // PAIR
    rows = 2 * half
    return call(
        self_backward_body,
        (pairs,),
        (a, b, weight, weight, qkv, attn, lse),
        [
            whole_spec((half, width)),
            whole_spec((half, width)),
            pl.BlockSpec((width, PAIR), lambda h: (0, 3 * pairs + h)),
            whole_spec((width, 3 * units)),
            pl.BlockSpec((rows, 3 * PAIR), lambda h: (0, h)),
            pl.BlockSpec((rows, PAIR), lambda h: (0, h)),
            pl.BlockSpec((8, rows), lambda h: (h, 0)),
        ],
        [
            ((rows, 3 * units), BF16),
            ((half, width), F32),
            ((half, width), BF16),
        ],
        [
            whole_spec((rows, 3 * units)),
            whole_spec((half, width)),
            whole_spec((half, width)),
        ],
        [
            pltpu.VMEM((rows, PAIR), BF16),
            pltpu.VMEM((PAIR, rows), BF16),
            pltpu.VMEM((rows, PAIR), F32),
            pltpu.VMEM((rows, PAIR), F32),
        ],
    )


def cross_weight_specs(width, units):
    return [pl.BlockSpec((width, units), functools.partial(lambda j, _: (0, j), j)) for j in (0, 2, 1, 3)]


def cross_probs(keys, queries):
    s = times_t(keys, queries)
    peak = jnp.max(s, axis=0, keepdims=True) * RATE
    probs = jnp.exp2(s * RATE - peak)
    return probs / jnp.sum(probs, axis=0, keepdims=True)


def cross_forward_body(
    a_ref, b_ref, wq0_ref, wq1_ref, wo0_ref, wo1_ref, kv0_ref, kv1_ref,
    q_ref, attn_ref, keep_ref, send_ref,
):
    share = a_ref.shape[0]
    units = wq0_ref.shape[1]
    masks = head_masks(kv0_ref.shape[0])
    keep = send = 0.0
    for j, (wq_ref, wo_ref, kv_ref) in enumerate(
        ((wq0_ref, wo0_ref, kv0_ref), (wq1_ref, wo1_ref, kv1_ref))
    ):
        cols = slice(j * units, (j + 1) * units)
        q_ref[:share, cols] = times(a_ref[...], wq_ref[...]).astype(BF16)
        q_ref[share:, cols] = times(b_ref[...], wq_ref[...]).astype(BF16)
        for begin in range(0, units, PAIR):
            lanes = slice(j * units + begin, j * units + begin + PAIR)
            queries = q_ref[:, lanes]
            keys = split_heads(kv_ref[:, begin : begin + PAIR], masks)
            values = kv_ref[:, units + begin : units + begin + PAIR].T
            mixed = [
                times(
                    values[e * HEAD : (e + 1) * HEAD],
                    cross_probs(keys[e], queries).astype(BF16),
                )
                for e in range(2)
            ]
            attn_ref[:, lanes] = jnp.concatenate(mixed, 0).T.astype(BF16)
        keep += times_t(attn_ref[:share, cols], wo_ref[...])
        send += times_t(attn_ref[share:, cols], wo_ref[...])
    keep_ref[...] = keep
    send_ref[...] = send.astype(BF16)


def cross_forward(a, b, weight, kvs):
    share, width = a.shape
    units = weight.shape[1] // 6
    ins = (a, b, *[weight] * 4, *kvs)
    outs = [
        ((2 * share, 2 * units), BF16),
        ((2 * share, 2 * units), BF16),
        ((share, width), F32),
        ((share, width), BF16),
    ]
    return call(
        cross_forward_body,
        (1,),
        ins,
        [whole_spec(v.shape) for v in ins[:2]]
        + cross_weight_specs(width, units)
        + [whole_spec(v.shape) for v in ins[6:]],
        outs,
        [whole_spec(s) for s, _ in outs],
    )


def cross_backward_body(
    a_ref, b_ref, wq0_ref, wq1_ref, wo0_ref, wo1_ref, kv0_ref, kv1_ref, q_ref,
    dq_ref, own_ref, other_ref, keep_ref, send_ref, hg_ref,
):
    share = a_ref.shape[0]
    units = wq0_ref.shape[1]
    text = kv0_ref.shape[0]
    masks = head_masks(text)
    keep = send = 0.0
    for j, (wq_ref, wo_ref, kv_ref, out_ref) in enumerate(
        ((wq0_ref, wo0_ref, kv0_ref, own_ref), (wq1_ref, wo1_ref, kv1_ref, other_ref))
    ):
        cols = slice(j * units, (j + 1) * units)
        hg_ref[:share, :] = times(a_ref[...], wo_ref[...]).astype(BF16)
        hg_ref[share:, :] = times(b_ref[...], wo_ref[...]).astype(BF16)
        for begin in range(0, units, PAIR):
            lanes = slice(j * units + begin, j * units + begin + PAIR)
            local = slice(begin, begin + PAIR)
            queries = q_ref[:, lanes]
            outer = hg_ref[:, local]
            pair_keys = kv_ref[:, local]
            keys = split_heads(pair_keys, masks)
            values = split_heads(kv_ref[:, units + begin : units + begin + PAIR], masks)
            keys_t = pair_keys.T
            query_grad, key_grad, value_grad = [], [], []
            for e in range(2):
                probs = cross_probs(keys[e], queries)
                grad = times_t(values[e], outer)
                inner = jnp.sum(probs * grad, axis=0, keepdims=True)
                score_grad = (probs * (grad - inner)).astype(BF16)
                query_grad.append(times(keys_t[e * HEAD : (e + 1) * HEAD], score_grad))
                key_grad.append(times(score_grad, queries))
                value_grad.append(times(probs.astype(BF16), outer))
            query_grad = jnp.concatenate(query_grad, 0) * (HEAD ** (-0.5))
            dq_ref[:, lanes] = query_grad.T.astype(BF16)
            key_grad = jnp.where(masks[0], *key_grad) * (HEAD ** (-0.5))
            value_grad = jnp.where(masks[0], *value_grad)
            out_ref[:, local] = key_grad.astype(out_ref.dtype)
            out_ref[:, units + begin : units + begin + PAIR] = value_grad.astype(out_ref.dtype)
        keep += times_t(dq_ref[:share, cols], wq_ref[...])
        send += times_t(dq_ref[share:, cols], wq_ref[...])
    keep_ref[...] = keep
    send_ref[...] = send.astype(BF16)


def cross_backward(a, b, weight, kvs, queries):
    share, width = a.shape
    units = weight.shape[1] // 6
    text = kvs[0].shape[0]
    ins = (a, b, *[weight] * 4, *kvs, queries)
    outs = [
        ((2 * share, 2 * units), BF16),
        ((text, 2 * units), F32),
        ((text, 2 * units), BF16),
        ((share, width), F32),
        ((share, width), BF16),
    ]
    return call(
        cross_backward_body,
        (1,),
        ins,
        [whole_spec(v.shape) for v in ins[:2]]
        + cross_weight_specs(width, units)
        + [whole_spec(v.shape) for v in ins[6:]],
        outs,
        [whole_spec(s) for s, _ in outs],
        [pltpu.VMEM((2 * share, units), BF16)],
    )


def gelu_pair(hidden):
    phi = 0.5 * (1.0 + lax.erf(hidden * (0.5**0.5)))
    density = jnp.exp(-0.5 * hidden * hidden) * 0.3989422804014327
    return hidden * phi, phi + hidden * density


def ffn_products(x, grad, up_ref, down_ref, active_ref, hidden_ref):
    units = up_ref.shape[1]
    size = units // 3 if units % (3 * 128) == 0 else units
    out = back = 0.0
    for begin in range(0, units, size):
        cols = slice(begin, begin + size)
        active, slope = gelu_pair(times(x, up_ref[:, cols]))
        active = active.astype(BF16)
        active_ref[:, cols] = active
        hidden_grad = (times(grad, down_ref[:, cols]) * slope).astype(BF16)
        hidden_ref[:, cols] = hidden_grad
        out += times_t(active, down_ref[:, cols])
        back += times_t(hidden_grad, up_ref[:, cols])
    return out, back


def ffn_first_body(
    xa_ref, xb_ref, ga_ref, gb_ref, up_ref, down_ref, active_ref, hidden_ref, out_ref, back_ref
):
    early = pl.program_id(0) < 2
    x = jnp.where(early, xa_ref[...], xb_ref[...])
    grad = jnp.where(early, ga_ref[...], gb_ref[...])
    out, back = ffn_products(x, grad, up_ref, down_ref, active_ref, hidden_ref)
    out_ref[...] = out
    back_ref[...] = back


def ffn_second_body(
    xa_ref, xb_ref, ga_ref, gb_ref, up_ref, down_ref, out_ref, back_ref,
    active_ref, hidden_ref, out_keep_ref, out_send_ref, keep_ref, send_ref,
):
    early = pl.program_id(0) < 2
    x = jnp.where(early, xa_ref[...], xb_ref[...])
    grad = jnp.where(early, ga_ref[...], gb_ref[...])
    out, back = ffn_products(x, grad, up_ref, down_ref, active_ref, hidden_ref)
    out += out_ref[...]
    back += back_ref[...]

    @pl.when(early)
    def _():
        out_keep_ref[...] = out
        keep_ref[...] = back

    @pl.when(jnp.logical_not(early))
    def _():
        out_send_ref[...] = out.astype(BF16)
        send_ref[...] = back.astype(BF16)


def ffn(x, grad, weight, partial=None):
    half, width = x[0].shape
    share = half // 2
    units = weight.shape[1] // 2
    rows = 2 * half

    def each(i):
        return (i, 0)

    def first(i):
        return (jnp.minimum(i, 1), 0)

    def second(i):
        return (jnp.maximum(i - 2, 0), 0)

    block = (share, width)
    in_specs = [
        pl.BlockSpec(block, first),
        pl.BlockSpec(block, second),
        pl.BlockSpec(block, first),
        pl.BlockSpec(block, second),
        pl.BlockSpec((width, units), lambda i: (0, 0)),
        pl.BlockSpec((width, units), lambda i: (0, 1)),
    ]
    outs = [((rows, units), BF16), ((rows, units), BF16)]
    out_specs = [pl.BlockSpec((share, units), each)] * 2
    if partial is None:
        outs += [((rows, width), F32)] * 2
        out_specs += [pl.BlockSpec(block, each)] * 2
    else:
        in_specs += [pl.BlockSpec(block, each)] * 2
        outs += [((half, width), F32), ((half, width), BF16)] * 2
        out_specs += [pl.BlockSpec(block, first), pl.BlockSpec(block, second)] * 2
    return call(
        ffn_first_body if partial is None else ffn_second_body,
        (4,),
        (*x, *grad, weight, weight, *(partial or ())),
        in_specs,
        outs,
        out_specs,
    )


def weight_grad_body(plan, lefts_count, rights_count, *refs):
    lefts, rights = refs[:lefts_count], refs[lefts_count : lefts_count + rights_count]
    outs = refs[lefts_count + rights_count :]
    begin = 0
    for pairs in plan:
        total = 0.0
        for left, right, first in pairs:
            size = lefts[left].shape[0]
            total += t_times(lefts[left][...], rights[right][first : first + size, :])
        cols = total.shape[1] // len(outs)
        for k, out in enumerate(outs):
            out[:, begin : begin + cols] = total[:, k * cols : (k + 1) * cols].astype(BF16)
        begin += cols


def weight_grad(*parts, split=1):
    lefts, rights, plan = [], [], []
    for part_lefts, part_rights in parts:
        pairs = []
        right = first = 0
        for left in part_lefts:
            pairs.append((len(lefts), len(rights) + right, first))
            lefts.append(left)
            first += left.shape[0]
            if first == part_rights[right].shape[0]:
                right, first = right + 1, 0
        rights += part_rights
        plan.append(pairs)
    width = lefts[0].shape[1]
    cols = sum(part_rights[0].shape[1] for _, part_rights in parts) // split
    size = 256 if width % 256 == 0 else width
    outs = call(
        functools.partial(weight_grad_body, plan, len(lefts), len(rights)),
        (width // size,),
        (*lefts, *rights),
        [pl.BlockSpec((v.shape[0], size), lambda i: (0, i)) for v in lefts]
        + [whole_spec(v.shape) for v in rights],
        [((width, cols), BF16)] * split,
        [pl.BlockSpec((size, cols), lambda i: (i, 0))] * split,
    )
    return outs[0] if split == 1 else outs


def text_project_body(text_ref, weight_ref, out_ref):
    out_ref[...] = times(text_ref[...], weight_ref[...]).astype(BF16)


def text_project(text, weight, block, cols):
    ins = (text, weight)
    specs = [whole_spec(text.shape), pl.BlockSpec((weight.shape[0], cols), lambda i: (0, block))]
    shape = (text.shape[0], cols)
    return call(text_project_body, (1,), ins, specs, [(shape, BF16)], [whole_spec(shape)])[0]


def text_back_body(half, grads_ref, weight_ref, keep_ref, send_ref):
    rows = times_t(grads_ref[...], weight_ref[...])
    for c in range(keep_ref.shape[0]):
        begin = 2 * c * half
        keep_ref[c] = rows[begin : begin + half]
        send_ref[c] = rows[begin + half : begin + 2 * half].astype(BF16)


def text_back(grads, weight, block, clips):
    width, cols = weight.shape[0], grads.shape[1]
    half = grads.shape[0] // clips // 2
    shape = (clips, half, width)
    return call(
        functools.partial(text_back_body, half),
        (1,),
        (grads, weight),
        [whole_spec(grads.shape), pl.BlockSpec((width, cols), lambda i: (0, block))],
        [(shape, F32), (shape, BF16)],
        [whole_spec(shape)] * 2,
    )


def local(
    n,
    audio_states,
    text_states,
    out_grad,
    self_qkv,
    self_out,
    cross_query,
    cross_kv,
    cross_out,
    mlp_up,
    mlp_down,
    norm_gain,
    norm_bias,
):
    clips, share, width = audio_states.shape
    units = self_out.shape[0]
    pairs = units // PAIR
    both = range(clips)

    Order.token = None
    table = ring_table(n)

    qkv_shard = self_qkv.reshape(3, -1, pairs, PAIR).transpose(1, 2, 0, 3).reshape(-1, 3 * units)
    self_ring = RingGather(jnp.concatenate((qkv_shard, self_out.T), 1), n)
    got = self_ring.step()
    params = small_gather(jnp.concatenate((norm_gain, norm_bias), 0), n).astype(F32)
    out_swapped = [swap_chip(out_grad[c]) for c in both]
    cross_own = jnp.concatenate((cross_query, cross_out.T), 1)
    cross_came = swap_chip(cross_own)
    part = mlp_up.shape[1] // 2
    ffn_shards = [
        jnp.concatenate([v[:, k * part : (k + 1) * part] for v in (mlp_up, mlp_down.T)], 1)
        for k in range(2)
    ]

    raw_swapped = [swap_chip(audio_states[c]) for c in both]
    cross_came, raw_swapped[0] = self_ring.turn([cross_came, raw_swapped[0]], params)
    cross_shard = jnp.concatenate((cross_own, cross_came, cross_kv[0], cross_kv[1]), axis=1)
    raw = gather_rows(audio_states[0], raw_swapped[0])
    full_self = [norm_pair(0, raw, params)]
    self_ring.turn()
    raw_swapped[1:] = self_ring.turn(raw_swapped[1:])
    raw = [gather_rows(audio_states[c], raw_swapped[c]) for c in range(1, clips)]
    full_self += [norm_pair(0, v, params) for v in raw]
    cross_ring = RingGather(hold(cross_shard, self_ring.got[-1] if self_ring.got else ()), n)
    cross_ring.step()
    self_w = self_ring.whole()
    text_pair = jnp.concatenate((text_states, swap_chip(text_states)), axis=1)
    text_full = jnp.concatenate((text_pair, swap_core(text_pair)), axis=1)
    qkv, self_attn, self_log, mid_terms = [], [], [], []
    for c in both:
        rows, attn, log, keep, send = self_forward(*full_self[c], self_w, units)
        if c == 0:
            send, *out_swapped = cross_ring.turn([send, *out_swapped])
            seen_out = [gather_rows(out_grad[k], out_swapped[k]) for k in both]
        else:
            keep_0, seen_0, other_0 = mid_terms[0][1:]
            send, other_0 = cross_ring.turn([send, other_0])
            mid_terms[0] = (audio_states[0], keep_0, seen_0, other_0)
        mid_terms.append((audio_states[c], *sum_over_tp(keep, send)))
        qkv.append(rows)
        self_attn.append(attn)
        self_log.append(log)
    stream_mid, cross_rows = [], []
    for c in both:
        stream, normed = norm_forward(1, mid_terms[c], params, share)
        stream_mid.append(stream)
        cross_rows.append((normed, swap_core(normed)))
        if c == 0:
            cross_ring.turn()
    early_gather = RingGather(hold(ffn_shards[0], cross_ring.got[-1] if cross_ring.got else ()), n)
    early_gather.step()
    cross_w = cross_ring.whole()
    text_rows = text_full.reshape(-1, width)
    text_kv = text_project(text_rows, cross_w, 2, 2 * units).reshape(clips, -1, 2 * units)
    (text_other,) = early_gather.turn([swap_chip(text_kv)])
    cross_q, cross_attn, stream_late, full_ffn = [], [], [], []
    for c in both:
        queries, attn, keep, send = cross_forward(
            *cross_rows[c], cross_w, (text_kv[c], text_other[c])
        )
        if c:
            send, came = early_gather.turn([send, came])
            full_ffn.append(gather_rows(normed_late, came))
        else:
            (send,) = early_gather.turn([send])
        cross_q.append(queries)
        cross_attn.append(attn)
        stream, normed = norm_forward(2, (stream_mid[c], keep, swap_core(send)), params, share)
        stream_late.append(stream)
        normed_late, came = normed, swap_chip(normed)
    late_gather = RingGather(hold(ffn_shards[1], early_gather.got[-1] if early_gather.got else ()), n)
    late_gather.step()
    early_w = early_gather.whole()

    actives, hiddens, partials = [[], []], [[], []], []
    for c in both:
        active, hidden, *partial = ffn(full_ffn[c], seen_out[c], early_w)
        if c == 0:
            (came,) = late_gather.turn([came])
            full_ffn.append(gather_rows(normed_late, came))
        else:
            late_gather.turn()
        actives[0].append(active)
        hiddens[0].append(hidden)
        partials.append(partial)
    grad = weight_grad((sum(full_ffn, ()), hiddens[0]), (sum(seen_out, ()), actives[0]))
    late_gather.turn()
    late_w = late_gather.whole()

    def sum_clips(grad):
        return lax.psum_scatter(grad, "fsdp", scatter_dimension=0, tiled=True)

    (grad,) = tick([grad])
    ffn_totals = [sum_clips(grad)]
    back_terms, out_terms = [], []
    for c in both:
        active, hidden, out_keep, out_send, keep, send = ffn(
            full_ffn[c], seen_out[c], late_w, partials[c]
        )
        if c:
            (send,) = tick([send], back_terms[0][-1])
        back_terms.append(sum_over_tp(keep, send))
        out_terms.append((out_keep, out_send))
        actives[1].append(active)
        hiddens[1].append(hidden)

    norm_sums = [[], [], []]
    grad_mid, grad_in, seen_mid, seen_in = [], [], [], []
    cross_grads, own_kv, other_kv, terms, branches = [], [], [], [], []
    def late_back(c):
        grad, branch, sums = norm_backward(
            2, stream_late[c], out_grad[c], back_terms[c], params, (F32, BF16)
        )
        norm_sums[2].append(sums)
        grad_mid.append(grad)
        seen_mid.append((branch, swap_core(branch)))

    def cross_back(c):
        dq, own, other, keep, send = cross_backward(
            *seen_mid[c], cross_w, (text_kv[c], text_other[c]), cross_q[c]
        )
        cross_grads.append(dq)
        own_kv.append(own)
        other_kv.append(other)
        terms.append((keep, swap_core(send)))

    def mid_back(c):
        grad, branch, sums = norm_backward(
            1, stream_mid[c], grad_mid[c], terms[c], params, (F32, BF16)
        )
        norm_sums[1].append(sums)
        grad_in.append(grad)
        branches.append((branch, swap_chip(branch)))

    late_back(0)
    wide = weight_grad((sum(full_ffn, ()), hiddens[1]), (sum(seen_out, ()), actives[1]))
    wide, other = tick([wide, back_terms[1][-1]])
    back_terms[1] = (*back_terms[1][:-1], other)
    ffn_totals.append(sum_clips(wide))
    for c in both:
        cross_back(c)
        if c + 1 < clips:
            late_back(c + 1)
        mid_back(c)
    kv_came = swap_chip(jnp.stack(other_kv))
    cross_shares = weight_grad(
        (sum(cross_rows, ()), cross_grads), (sum(seen_mid, ()), cross_attn), split=2
    )
    (came,) = tick([branches[0][1]])
    seen_in = [gather_rows(branches[0][0], came)]
    seen_in += [gather_rows(*branches[c]) for c in range(1, clips)]
    cross_came = swap_chip(cross_shares[1])

    self_grads, in_terms, out_sums = [], [], []
    for c in both:
        grads, keep, send = self_backward(
            *seen_in[c], self_w, qkv[c], self_attn[c], self_log[c]
        )
        if c == 0:
            send, kv_came = tick([send, kv_came])
        else:
            send, cross_came, text_came = tick([send, cross_came, text_came])
        in_terms.append(sum_over_tp(keep, send))
        self_grads.append(grads)
        if c == 0:
            kv_grads = (jnp.stack(own_kv) + kv_came.astype(F32)).astype(BF16)
            kv_rows = kv_grads.reshape(-1, 2 * units)
            grad = weight_grad((sum(seen_in, ()), self_attn), ([text_rows], [kv_rows]))
            out_total = sum_clips(grad)
            text_keep, text_send = text_back(kv_rows, cross_w, 2, clips)
            quarter = text_keep.shape[1] // 2
            text_seen = text_keep + swap_core(text_send).astype(F32)
            text_came = swap_chip(text_seen[:, quarter:].astype(BF16))
        else:
            cross_total = sum_clips(sum_terms((cross_shares[0], cross_came), cross_came.shape))
    text_grad = text_seen[:, :quarter] + text_came.astype(F32)
    grad = weight_grad((sum(full_self, ()), self_grads))
    qkv_sum = RingSum([grad], n, table)
    late_terms = [sum_over_tp(*out_terms[c]) for c in both]
    audio_grad, layer_out = [], []
    for c in both:
        grad, sums = norm_backward(0, audio_states[c], grad_in[c], in_terms[c], params, (BF16,))
        norm_sums[0].append(sums)
        audio_grad.append(grad)
        if c == 0:
            qkv_sum.step()
    norm_total = SmallSum(jnp.concatenate([sum(v)[:2] for v in norm_sums], 0), n)
    audio_grad = join(audio_grad)
    qkv_sum.step()
    norm_total.step()
    norm_total.step()
    layer_out.append(sum_terms((stream_late[0], *late_terms[0]), (share, width)))
    qkv_sum.step([out_total])
    norm_total.step()
    norm_total.step()
    for c in range(1, clips):
        layer_out.append(sum_terms((stream_late[c], *late_terms[c]), (share, width)))
    layer_out = join(layer_out)
    qkv_total = qkv_sum.total(split=(pairs, 3))
    norm_total = norm_total.total()

    def cut(total, begin, count=1):
        return total[:, begin * units : (begin + count) * units]

    return (
        layer_out,
        audio_grad,
        text_grad.astype(BF16),
        qkv_total,
        cut(out_total, 0).astype(F32).T,
        cut(cross_total, 0).astype(F32),
        jnp.stack((cut(out_total, 1), cut(out_total, 2))).astype(F32),
        cut(cross_total, 1).astype(F32).T,
        jnp.concatenate([v[:, :part] for v in ffn_totals], 1).astype(F32),
        jnp.concatenate([v[:, part:] for v in ffn_totals], 1).astype(F32).T,
        norm_total[0::2],
        norm_total[1::2],
    )


def solution(mesh):
    n = mesh.shape["fsdp"]

    def body(*args):
        return local(n, *args)

    return jax.shard_map(
        body,
        mesh=mesh,
        in_specs=(
            P("fsdp", "tp", None),
            P("fsdp", "tp", None),
            P("fsdp", "tp", None),
            P(None, "fsdp", "tp"),
            P("tp", "fsdp"),
            P("fsdp", "tp"),
            P(None, "fsdp", "tp"),
            P("tp", "fsdp"),
            P("fsdp", "tp"),
            P("tp", "fsdp"),
            P(None, "fsdp"),
            P(None, "fsdp"),
        ),
        out_specs=(
            P("fsdp", "tp", None),
            P("fsdp", "tp", None),
            P("fsdp", "tp", None),
            P(None, "fsdp", "tp"),
            P("tp", "fsdp"),
            P("fsdp", "tp"),
            P(None, "fsdp", "tp"),
            P("tp", "fsdp"),
            P("fsdp", "tp"),
            P("tp", "fsdp"),
            P(None, "fsdp"),
            P(None, "fsdp"),
        ),
        check_vma=False,
    )
```

```python
import functools
import math

import jax
import jax.numpy as jnp
from jax import lax
from jax.experimental import pallas as pl
from jax.experimental.pallas import tpu as pltpu
from jax.sharding import PartitionSpec as P

HEAD = 64
PAIR = 2 * HEAD
EPSILON = 1e-05
F32 = jnp.float32
BF16 = jnp.bfloat16
RATE = HEAD ** (-0.5) * math.log2(math.e)
TOKEN = (8, 128)
COST = 1000
VMEM = 52 * 2**20


def swap_chip(values):
    return lax.ppermute(values, "tp", [(t, t ^ 2) for t in range(4)])


def swap_core(values):
    return lax.ppermute(values, "tp", [(t, t ^ 1) for t in range(4)])


def place_of(share, t):
    apart = share ^ t
    return ((apart & 1) << 1) | (apart >> 1)


def gather_rows(values, swapped):
    pair = jnp.concatenate((values, swapped), axis=0)
    return pair, swap_core(pair)


def ring_of(n):
    return list(range(0, n, 2)) + list(range(n - 1, 0, -2))


def ring_place(n):
    i = lax.axis_index("fsdp")
    return jnp.where(i % 2 == 0, i // 2, n - (i + 1) // 2)


def ring_index(n, place):
    place = lax.rem(place + 2 * n, n)
    return jnp.where(place < n // 2, 2 * place, 2 * (n - place) - 1)


def send_next(values, n):
    ring = ring_of(n)
    return lax.ppermute(values, "fsdp", [(ring[k], ring[(k + 1) % n]) for k in range(n)])


def send_prev(values, n):
    ring = ring_of(n)
    return lax.ppermute(values, "fsdp", [(ring[(k + 1) % n], ring[k]) for k in range(n)])


def ring_table(n):
    return ring_index(n, ring_place(n) + jnp.arange(-(n // 2), n // 2 + 1)).astype(jnp.int32)


def place_pieces_body(n, rows, places, *refs):
    pieces, whole = refs[:-1], refs[-1]
    for piece, (step, offset) in zip(pieces, places):
        begin = ring_index(n, ring_place(n) + step) * rows + offset
        size = piece.shape[0]
        whole[pl.ds(pl.multiple_of(begin, math.gcd(rows, size)), size), :] = piece[...]


class RingGather:
    def __init__(self, shard, n):
        self.n, self.shard, self.got = n, shard, []
        self.direct = n > 16 or n % 2

    def step(self):
        if self.direct:
            return ()
        up, down = self.got[-1] if self.got else (self.shard, self.shard)
        if len(self.got) == self.n // 2 - 1:
            half = self.shard.shape[0] // 2
            up, down = up[:half], down[half:]
        self.got.append((send_next(up, self.n), send_prev(down, self.n)))
        return self.got[-1]

    def turn(self, values=(), *wait):
        if self.direct:
            return tick(list(values), *wait) if values else []
        pair = self.got[-1]
        passed = tick([*pair, *values], *wait)
        self.got[-1] = tuple(passed[:2])
        self.step()
        return passed[2:]

    def whole(self, wait=()):
        if self.direct:
            return lax.all_gather(self.shard, "fsdp", axis=0, tiled=True)
        rows, cols = self.shard.shape
        pieces, places = [self.shard], [(0, 0)]
        for k, pair in enumerate(self.got, 1):
            pieces += pair
            places += [(-k, 0), (k, 0 if k < self.n // 2 else rows // 2)]
        size = 768 if cols % 768 == 0 else cols
        return call(
            functools.partial(place_pieces_body, self.n, rows, places),
            (cols // size,),
            pieces,
            [pl.BlockSpec((v.shape[0], size), lambda i: (0, i)) for v in pieces],
            [((self.n * rows, cols), self.shard.dtype)],
            [pl.BlockSpec((self.n * rows, size), lambda i: (0, i))],
                wait=wait,
        )[0]


def ring_body(kind, rows, count, sides, split, *refs):
    table, wholes = refs[0], refs[1 : 1 + count]
    came = refs[1 + count : -len(sides) - count - 1]
    outs, own, sems = refs[-len(sides) - count - 1 : -count - 1], refs[-count - 1 : -1], refs[-1]
    copies = []
    for side, (entry, first, last) in enumerate(sides):
        begin = pl.multiple_of(table[entry] * rows + first, rows // 2)
        for k in range(count):
            source = wholes[k].at[pl.ds(begin, last - first), :]
            to = own[k].at[side, pl.ds(0, last - first), :]
            copies.append(pltpu.make_async_copy(source, to, sems.at[side, k]))
    for copy in copies:
        copy.start()
    for copy in copies:
        copy.wait()
    half = rows // 2
    for side, (_, first, last) in enumerate(sides):
        begin = 0
        for k in range(count):
            cols = slice(begin, begin + wholes[k].shape[1])
            begin = cols.stop
            mine = own[k][side, : last - first, :]
            if kind == "begin":
                outs[side][:, cols] = mine
            elif kind == "first":
                add = came[side][:, cols].astype(F32)
                here = slice(side * half, (side + 1) * half)
                there = slice((1 - side) * half, (2 - side) * half)
                outs[side][here, cols] = (mine[here].astype(F32) + add).astype(BF16)
                outs[side][there, cols] = mine[there]
            elif kind == "middle":
                add = came[side][:, cols].astype(F32)
                outs[side][:, cols] = (mine.astype(F32) + add).astype(BF16)
            else:
                total = came[0][:, cols].astype(F32) + came[1][:, cols].astype(F32)
                total += mine.astype(F32)
                if split is None:
                    outs[side][:, cols] = total
                else:
                    outer, inner = split
                    size = total.shape[1] // (outer * inner)
                    for at in range(outer * inner):
                        to = pl.ds(at // inner * size, size)
                        outs[side][at % inner, :, to] = total[:, at * size : (at + 1) * size]


class RingSum:
    def __init__(self, wholes, n, table):
        self.wholes, self.n, self.table = wholes, n, table
        self.direct = n > 16 or n % 2
        self.left = n // 2
        self.came = ()
        self.step()

    def run(self, kind, step, wait=(), split=None):
        rows = self.wholes[0].shape[0] // self.n
        half = rows // 2
        widths = [v.shape[1] for v in self.wholes]
        middle = self.n // 2
        if kind == "end":
            sides = [(middle, 0, rows)]
        elif kind == "begin":
            sides = [(middle + step, 0, half), (middle - step, half, rows)]
        else:
            sides = [(middle + step, 0, rows), (middle - step, 0, rows)]
        size = half if kind == "begin" else rows
        shape = (size, sum(widths))
        if split is not None:
            shape = (split[1], size, shape[1] // split[1])
        out = (shape, F32 if kind == "end" else BF16)
        hbm = pl.BlockSpec(memory_space=pltpu.HBM)
        return call(
            functools.partial(ring_body, kind, rows, len(widths), sides, split),
            (1,),
            (self.table, *self.wholes, *self.came),
            [pl.BlockSpec(memory_space=pltpu.SMEM)]
            + [hbm] * len(widths)
            + [whole_spec(v.shape) for v in self.came],
            [out] * len(sides),
            [whole_spec(out[0])] * len(sides),
            [pltpu.VMEM((len(sides), rows, cols), BF16) for cols in widths]
            + [pltpu.SemaphoreType.DMA((len(sides), len(widths)))],
            wait=wait,
        )

    def step(self, wait=()):
        if self.direct or not self.left:
            return
        if self.left == self.n // 2:
            kind = "begin"
        else:
            kind = "first" if self.left == self.n // 2 - 1 else "middle"
        up, down = self.run(kind, self.left, wait)
        self.came = (send_next(up, self.n), send_prev(down, self.n))
        self.left -= 1

    def total(self, split=None):
        if self.direct:
            whole = jnp.concatenate(self.wholes, 1)
            total = lax.psum_scatter(whole, "fsdp", scatter_dimension=0, tiled=True).astype(F32)
            if split is not None:
                total = total.reshape(total.shape[0], *split, -1).transpose(2, 0, 1, 3)
                total = total.reshape(*total.shape[:2], -1)
            return total
        while self.left:
            self.step()
        return self.run("end", 0, split=split)[0]


def swap_fsdp(values, n, bit):
    return lax.ppermute(values, "fsdp", [(i, i ^ bit) for i in range(n)])


def small_gather(shard, n):
    if n & (n - 1):
        return lax.all_gather(shard, "fsdp", axis=1, tiled=True)
    found = shard[None]
    bit = 1
    while bit < n:
        found = jnp.concatenate((found, swap_fsdp(found, n, bit)), axis=0)
        bit *= 2
    found = jnp.take(found, jnp.arange(n) ^ lax.axis_index("fsdp"), axis=0)
    return found.transpose(1, 0, 2).reshape(shard.shape[0], -1)


def times(rows, weight):
    return jnp.dot(rows, weight, preferred_element_type=F32)


def times_t(rows, weight):
    return lax.dot_general(rows, weight, (((1,), (1,)), ((), ())), preferred_element_type=F32)


def t_times(left, right):
    return lax.dot_general(left, right, (((0,), (0,)), ((), ())), preferred_element_type=F32)


def whole_spec(shape):
    return pl.BlockSpec(shape, lambda *_: (0,) * len(shape))


class Order:
    token = None


def call(body, grid, ins, in_specs, outs, out_specs, scratch=(), wait=(), alias=None):
    count = len(ins)
    extra = list(wait) + ([Order.token] if Order.token is not None else [])
    any_spec, hbm = (pl.BlockSpec(memory_space=space) for space in (pl.ANY, pltpu.HBM))

    def run(*refs):
        after = refs[count + len(extra) :]
        body(*refs[:count], *after[: len(outs)], *after[len(outs) + 1 :])
        after[len(outs)][...] = jnp.zeros(TOKEN, F32)

    results = pl.pallas_call(
        run,
        grid=grid,
        in_specs=list(in_specs) + [hbm] * len(wait) + [any_spec] * (len(extra) - len(wait)),
        out_specs=list(out_specs) + [whole_spec(TOKEN)],
        scratch_shapes=list(scratch),
        out_shape=[jax.ShapeDtypeStruct(s, d) for s, d in list(outs) + [(TOKEN, F32)]],
        input_output_aliases=alias or {},
        compiler_params=pltpu.CompilerParams(vmem_limit_bytes=VMEM),
        name=getattr(body, "func", body).__name__,
        cost_estimate=pl.CostEstimate(flops=COST, bytes_accessed=0, transcendentals=0),
    )(*ins, *extra)
    Order.token = results[-1]
    return results[:-1]


def head_masks(rows):
    low = lax.broadcasted_iota(jnp.int32, (rows, PAIR), 1) < HEAD
    return low, jnp.logical_not(low)


def split_heads(block, masks):
    zero = jnp.zeros_like(block)
    return [jnp.where(m, block, zero) for m in masks]


def rows_call(body, ins, outs, sums=(), wait=(), shifts=None, most=128):
    rows = outs[0][0][0]
    block = next((v for v in (most, 96) if rows % v == 0), rows)
    steps = rows // block
    shifts = shifts or [0] * len(ins)
    in_specs = []
    for v, shift in zip(ins, shifts):
        if shift is None:
            in_specs.append(whole_spec(v.shape))
        else:
            first = shift // block
            in_specs.append(
                pl.BlockSpec((block, v.shape[1]), functools.partial(lambda f, i: (i + f, 0), first))
            )
    out_specs = [pl.BlockSpec((block, shape[1]), lambda i: (i, 0)) for shape, _ in outs]
    out_specs += [whole_spec(shape) for shape, _ in sums]
    return call(
        body, (steps,), ins, in_specs, list(outs) + list(sums), out_specs, wait=wait
    )


def tick_body(*refs):
    pass


def tick(values, *wait):
    spec = pl.BlockSpec(memory_space=pl.ANY)
    count = len(values)
    return call(
        tick_body,
        (1,),
        values,
        [spec] * count,
        [(v.shape, v.dtype) for v in values],
        [spec] * count,
        wait=wait,
        alias={k: k for k in range(count)},
    )


def copy_body(from_ref, to_ref):
    to_ref[...] = from_ref[...]


def hold(values, wait=()):
    return rows_call(copy_body, (values,), [(values.shape, values.dtype)], wait=wait)[0]


def add_body(keep_ref, seen_ref, out_ref):
    out_ref[...] = (keep_ref[...] + seen_ref[...].astype(F32)).astype(BF16)


def sum_over_tp(keep, send, wait=()):
    seen = swap_core(send)
    half = keep.shape[0] // 2
    (passed,) = rows_call(
        add_body, (keep, seen), [((half, keep.shape[1]), BF16)], shifts=(half, half), wait=wait
    )
    return keep, seen, swap_chip(passed)


def total_of(refs):
    return sum(ref[...].astype(F32) for ref in refs)


def norm_forward_body(index, *refs):
    params, outs = refs[-3], refs[-2:]
    stream = total_of(refs[:-3])
    outs[0][...] = stream
    center = stream - jnp.mean(stream, axis=-1, keepdims=True)
    spread = jnp.mean(center * center, axis=-1, keepdims=True)
    gain, bias = params[index : index + 1, :], params[3 + index : 4 + index, :]
    outs[1][...] = (center * lax.rsqrt(spread + EPSILON) * gain + bias).astype(BF16)


def norm_forward(index, terms, params, rows, wait=()):
    shape = (rows, params.shape[1])
    return rows_call(
        functools.partial(norm_forward_body, index),
        (*terms, params),
        [(shape, F32), (shape, BF16)],
        shifts=[0] * len(terms) + [None],
        wait=wait,
    )


def norm_pair_body(index, left_ref, right_ref, params, *outs):
    gain, bias = params[index : index + 1, :], params[3 + index : 4 + index, :]
    for ref, out in zip((left_ref, right_ref), outs):
        stream = ref[...].astype(F32)
        center = stream - jnp.mean(stream, axis=-1, keepdims=True)
        spread = jnp.mean(center * center, axis=-1, keepdims=True)
        out[...] = (center * lax.rsqrt(spread + EPSILON) * gain + bias).astype(BF16)


def norm_pair(index, pair, params):
    return tuple(
        rows_call(
            functools.partial(norm_pair_body, index),
            (*pair, params),
            [(v.shape, BF16) for v in pair],
            shifts=[0, 0, None],
        )
    )


def norm_backward_body(index, count, *refs):
    stream_ref, base_ref, terms = refs[0], refs[1], refs[2 : 2 + count]
    params, outs, sums = refs[2 + count], refs[3 + count : -1], refs[-1]
    stream = stream_ref[...].astype(F32)
    center = stream - jnp.mean(stream, axis=-1, keepdims=True)
    scale = lax.rsqrt(jnp.mean(center * center, axis=-1, keepdims=True) + EPSILON)
    xhat = center * scale
    grad = total_of(terms)
    e = grad * params[index : index + 1, :]
    back = scale * (
        e - jnp.mean(e, axis=-1, keepdims=True) - xhat * jnp.mean(e * xhat, axis=-1, keepdims=True)
    )
    total = base_ref[...].astype(F32) + back
    for out in outs:
        out[...] = total.astype(out.dtype)

    @pl.when(pl.program_id(0) == 0)
    def _():
        sums[...] = jnp.zeros_like(sums)

    sums[0:1, :] += jnp.sum(grad * xhat, axis=0, keepdims=True)
    sums[1:2, :] += jnp.sum(grad, axis=0, keepdims=True)


def norm_backward(index, stream, base, terms, params, kinds):
    shape = stream.shape
    return rows_call(
        functools.partial(norm_backward_body, index, len(terms)),
        (stream, base, *terms, params),
        [(shape, kind) for kind in kinds],
        [((8, shape[1]), F32)],
        shifts=[0] * (2 + len(terms)) + [None],
    )


def sum_pair_body(left_ref, right_ref, out_ref):
    out_ref[...] = left_ref[...] + right_ref[...]


class SmallSum:
    def __init__(self, whole, n):
        self.whole, self.n = whole, n
        self.swaps = [swap_core, swap_chip]
        if n & (n - 1):
            self.whole = lax.psum(whole, "fsdp")
        else:
            bits = [2**k for k in range(n.bit_length() - 1)]
            self.swaps += [functools.partial(swap_fsdp, n=n, bit=bit) for bit in bits]
        self.came = self.swaps.pop(0)(self.whole)

    def step(self):
        if self.came is None:
            return
        shape = self.whole.shape
        (self.whole,) = call(
            sum_pair_body,
            (1,),
            (self.whole, self.came),
            [whole_spec(shape)] * 2,
            [(shape, F32)],
            [whole_spec(shape)],
        )
        self.came = self.swaps.pop(0)(self.whole) if self.swaps else None

    def total(self):
        while self.came is not None:
            self.step()
        cols = self.whole.shape[1] // self.n
        begin = lax.axis_index("fsdp") * cols
        return lax.dynamic_slice(self.whole, (0, begin), (self.whole.shape[0], cols))


def join_body(count, *refs):
    outs = refs[count]
    for k in range(count):
        outs[k] = refs[k][...]


def join(parts):
    shape, kind = parts[0].shape, parts[0].dtype
    block = 128 if shape[0] % 128 == 0 else shape[0]
    return call(
        functools.partial(join_body, len(parts)),
        (shape[0] // block,),
        parts,
        [pl.BlockSpec((block, shape[1]), lambda i: (i, 0))] * len(parts),
        [((len(parts), *shape), kind)],
        [pl.BlockSpec((len(parts), block, shape[1]), lambda i: (0, i, 0))],
    )[0]


def sum_beside_body(own_ref, *refs):
    came, last, out = refs[:-2], refs[-2], refs[-1]
    begin = 0
    for ref in came:
        cols = slice(begin, begin + ref.shape[1])
        begin = cols.stop
        out[:, cols] = (own_ref[:, cols].astype(F32) + ref[...].astype(F32)).astype(BF16)
    out[:, begin:] = last[...]


def sum_beside(own, came, last):
    shape = (own.shape[0], own.shape[1] + last.shape[1])
    return rows_call(sum_beside_body, (own, *came, last), [(shape, BF16)], most=256)[0]


def sum_terms_body(*refs):
    refs[-1][...] = total_of(refs[:-1]).astype(BF16)


def sum_terms(terms, shape):
    return rows_call(sum_terms_body, terms, [(shape, BF16)])[0]


def self_forward_body(
    a_ref, b_ref, w_ref, wo_ref, qkv_ref, attn_ref, lse_ref, keep_ref, send_ref, vt_ref
):
    step = pl.program_id(0)
    t = lax.axis_index("tp")
    half = a_ref.shape[0]
    share = half // 2
    qkv_ref[:half, :] = times(a_ref[...], w_ref[...]).astype(BF16)
    qkv_ref[half:, :] = times(b_ref[...], w_ref[...]).astype(BF16)
    vt_ref[...] = qkv_ref[:, 2 * PAIR :].T
    masks = head_masks(share)
    at = [pl.ds(pl.multiple_of(place_of(g, t) * share, share), share) for g in range(4)]
    seen = lax.broadcasted_iota(jnp.int32, (share, share), 0) <= lax.broadcasted_iota(
        jnp.int32, (share, share), 1
    )
    lanes = pl.ds(pl.multiple_of(step * PAIR, PAIR), PAIR)
    for g in range(4):
        queries = split_heads(qkv_ref[at[g], :PAIR], masks)
        found = []
        for e in range(2):
            scores = []
            for b in range(g + 1):
                s = times_t(qkv_ref[at[b], PAIR : 2 * PAIR], queries[e])
                scores.append(jnp.where(seen, s, -1e30) if b == g else s)
            peak = functools.reduce(
                jnp.maximum, [jnp.max(s, axis=0, keepdims=True) for s in scores]
            )
            peak = peak * RATE
            probs = [jnp.exp2(s * RATE - peak) for s in scores]
            total = sum(jnp.sum(p, axis=0, keepdims=True) for p in probs)
            rows = slice(e * HEAD, (e + 1) * HEAD)
            mixed = sum(times(vt_ref[rows, at[b]], probs[b].astype(BF16)) for b in range(g + 1))
            found.append(mixed / total)
            lse_ref[e : e + 1, at[g]] = peak + jnp.log2(total)
        attn_ref[at[g], lanes] = jnp.concatenate(found, 0).T.astype(BF16)

    @pl.when(step == pl.num_programs(0) - 1)
    def _():
        for k in range(2):
            rows = slice(k * share, (k + 1) * share)
            keep_ref[rows, :] = times_t(attn_ref[rows, :], wo_ref[...])
            late = slice(half + k * share, half + (k + 1) * share)
            send_ref[rows, :] = times_t(attn_ref[late, :], wo_ref[...]).astype(BF16)


def self_forward(a, b, weight, units):
    half, width = a.shape
    pairs = units // PAIR
    rows = 2 * half
    return call(
        self_forward_body,
        (pairs,),
        (a, b, weight, weight),
        [
            whole_spec((half, width)),
            whole_spec((half, width)),
            pl.BlockSpec((width, 3 * PAIR), lambda h: (0, h)),
            pl.BlockSpec((width, units), lambda h: (0, 3)),
        ],
        [
            ((rows, 3 * units), BF16),
            ((rows, units), BF16),
            ((8 * pairs, rows), F32),
            ((half, width), F32),
            ((half, width), BF16),
        ],
        [
            pl.BlockSpec((rows, 3 * PAIR), lambda h: (0, h)),
            whole_spec((rows, units)),
            pl.BlockSpec((8, rows), lambda h: (h, 0)),
            whole_spec((half, width)),
            whole_spec((half, width)),
        ],
        [pltpu.VMEM((PAIR, rows), BF16)],
    )


def self_backward_body(
    a_ref, b_ref, wo_ref, w_ref, qkv_ref, attn_ref, lse_ref,
    grads_ref, keep_ref, send_ref, hg_ref, kt_ref, dk_ref, dv_ref,
):
    step = pl.program_id(0)
    t = lax.axis_index("tp")
    half = a_ref.shape[0]
    share = half // 2
    hg_ref[:half, :] = times(a_ref[...], wo_ref[...]).astype(BF16)
    hg_ref[half:, :] = times(b_ref[...], wo_ref[...]).astype(BF16)
    kt_ref[...] = qkv_ref[:, PAIR : 2 * PAIR].T
    dk_ref[...] = jnp.zeros_like(dk_ref)
    dv_ref[...] = jnp.zeros_like(dv_ref)
    masks = head_masks(share)
    at = [pl.ds(pl.multiple_of(place_of(g, t) * share, share), share) for g in range(4)]
    seen = lax.broadcasted_iota(jnp.int32, (share, share), 0) <= lax.broadcasted_iota(
        jnp.int32, (share, share), 1
    )
    base = step * 3 * PAIR
    lanes = [pl.ds(pl.multiple_of(base + c * PAIR, PAIR), PAIR) for c in range(3)]
    for g in range(4):
        queries = split_heads(qkv_ref[at[g], :PAIR], masks)
        block = hg_ref[at[g], :]
        outer = split_heads(block, masks)
        inner = (block.astype(F32) * attn_ref[at[g], :].astype(F32)).T
        query_grad = []
        for e in range(2):
            rows = slice(e * HEAD, (e + 1) * HEAD)
            lse = lse_ref[e : e + 1, at[g]]
            delta = jnp.sum(inner[rows], axis=0, keepdims=True)
            total = jnp.zeros((HEAD, share), F32)
            for b in range(g + 1):
                s = times_t(qkv_ref[at[b], PAIR : 2 * PAIR], queries[e])
                probs = jnp.exp2(s * RATE - lse)
                if b == g:
                    probs = jnp.where(seen, probs, 0.0)
                grad = times_t(qkv_ref[at[b], 2 * PAIR :], outer[e])
                score_grad = (probs * (grad - delta)).astype(BF16)
                dv_ref[at[b], :] += times(probs.astype(BF16), outer[e])
                dk_ref[at[b], :] += times(score_grad, queries[e])
                total += times(kt_ref[rows, at[b]], score_grad)
            query_grad.append(total)
        query_grad = jnp.concatenate(query_grad, 0) * (HEAD ** (-0.5))
        grads_ref[at[g], lanes[0]] = query_grad.T.astype(BF16)
    grads_ref[:, lanes[1]] = (dk_ref[...] * (HEAD ** (-0.5))).astype(BF16)
    grads_ref[:, lanes[2]] = dv_ref[...].astype(BF16)

    @pl.when(step == pl.num_programs(0) - 1)
    def _():
        for k in range(2):
            rows = slice(k * share, (k + 1) * share)
            keep_ref[rows, :] = times_t(grads_ref[rows, :], w_ref[...])
            late = slice(half + k * share, half + (k + 1) * share)
            send_ref[rows, :] = times_t(grads_ref[late, :], w_ref[...]).astype(BF16)


def self_backward(a, b, weight, qkv, attn, lse):
    half, width = a.shape
    units = attn.shape[1]
    pairs = units // PAIR
    rows = 2 * half
    return call(
        self_backward_body,
        (pairs,),
        (a, b, weight, weight, qkv, attn, lse),
        [
            whole_spec((half, width)),
            whole_spec((half, width)),
            pl.BlockSpec((width, PAIR), lambda h: (0, 3 * pairs + h)),
            whole_spec((width, 3 * units)),
            pl.BlockSpec((rows, 3 * PAIR), lambda h: (0, h)),
            pl.BlockSpec((rows, PAIR), lambda h: (0, h)),
            pl.BlockSpec((8, rows), lambda h: (h, 0)),
        ],
        [
            ((rows, 3 * units), BF16),
            ((half, width), F32),
            ((half, width), BF16),
        ],
        [
            whole_spec((rows, 3 * units)),
            whole_spec((half, width)),
            whole_spec((half, width)),
        ],
        [
            pltpu.VMEM((rows, PAIR), BF16),
            pltpu.VMEM((PAIR, rows), BF16),
            pltpu.VMEM((rows, PAIR), F32),
            pltpu.VMEM((rows, PAIR), F32),
        ],
    )


def cross_weight_specs(width, units):
    return [pl.BlockSpec((width, units), functools.partial(lambda j, _: (0, j), j)) for j in (0, 2, 1, 3)]


def cross_probs(keys, queries):
    s = times_t(keys, queries)
    peak = jnp.max(s, axis=0, keepdims=True) * RATE
    probs = jnp.exp2(s * RATE - peak)
    return probs / jnp.sum(probs, axis=0, keepdims=True)


def cross_forward_body(
    a_ref, b_ref, wq0_ref, wq1_ref, wo0_ref, wo1_ref, kv0_ref, kv1_ref,
    q_ref, attn_ref, keep_ref, send_ref,
):
    share = a_ref.shape[0]
    units = wq0_ref.shape[1]
    masks = head_masks(kv0_ref.shape[0])
    keep = send = 0.0
    for j, (wq_ref, wo_ref, kv_ref) in enumerate(
        ((wq0_ref, wo0_ref, kv0_ref), (wq1_ref, wo1_ref, kv1_ref))
    ):
        cols = slice(j * units, (j + 1) * units)
        q_ref[:share, cols] = times(a_ref[...], wq_ref[...]).astype(BF16)
        q_ref[share:, cols] = times(b_ref[...], wq_ref[...]).astype(BF16)
        for begin in range(0, units, PAIR):
            lanes = slice(j * units + begin, j * units + begin + PAIR)
            queries = q_ref[:, lanes]
            keys = split_heads(kv_ref[:, begin : begin + PAIR], masks)
            values = kv_ref[:, units + begin : units + begin + PAIR].T
            mixed = [
                times(
                    values[e * HEAD : (e + 1) * HEAD],
                    cross_probs(keys[e], queries).astype(BF16),
                )
                for e in range(2)
            ]
            attn_ref[:, lanes] = jnp.concatenate(mixed, 0).T.astype(BF16)
        keep += times_t(attn_ref[:share, cols], wo_ref[...])
        send += times_t(attn_ref[share:, cols], wo_ref[...])
    keep_ref[...] = keep
    send_ref[...] = send.astype(BF16)


def cross_forward(a, b, weight, kvs):
    share, width = a.shape
    units = weight.shape[1] // 6
    ins = (a, b, *[weight] * 4, *kvs)
    outs = [
        ((2 * share, 2 * units), BF16),
        ((2 * share, 2 * units), BF16),
        ((share, width), F32),
        ((share, width), BF16),
    ]
    return call(
        cross_forward_body,
        (1,),
        ins,
        [whole_spec(v.shape) for v in ins[:2]]
        + cross_weight_specs(width, units)
        + [whole_spec(v.shape) for v in ins[6:]],
        outs,
        [whole_spec(s) for s, _ in outs],
    )


def cross_backward_body(
    a_ref, b_ref, wq0_ref, wq1_ref, wo0_ref, wo1_ref, kv0_ref, kv1_ref, q_ref,
    dq_ref, own_ref, other_ref, keep_ref, send_ref, hg_ref,
):
    share = a_ref.shape[0]
    units = wq0_ref.shape[1]
    text = kv0_ref.shape[0]
    masks = head_masks(text)
    keep = send = 0.0
    for j, (wq_ref, wo_ref, kv_ref, out_ref) in enumerate(
        ((wq0_ref, wo0_ref, kv0_ref, own_ref), (wq1_ref, wo1_ref, kv1_ref, other_ref))
    ):
        cols = slice(j * units, (j + 1) * units)
        hg_ref[:share, :] = times(a_ref[...], wo_ref[...]).astype(BF16)
        hg_ref[share:, :] = times(b_ref[...], wo_ref[...]).astype(BF16)
        for begin in range(0, units, PAIR):
            lanes = slice(j * units + begin, j * units + begin + PAIR)
            local = slice(begin, begin + PAIR)
            queries = q_ref[:, lanes]
            outer = hg_ref[:, local]
            pair_keys = kv_ref[:, local]
            keys = split_heads(pair_keys, masks)
            values = split_heads(kv_ref[:, units + begin : units + begin + PAIR], masks)
            keys_t = pair_keys.T
            query_grad, key_grad, value_grad = [], [], []
            for e in range(2):
                probs = cross_probs(keys[e], queries)
                grad = times_t(values[e], outer)
                inner = jnp.sum(probs * grad, axis=0, keepdims=True)
                score_grad = (probs * (grad - inner)).astype(BF16)
                query_grad.append(times(keys_t[e * HEAD : (e + 1) * HEAD], score_grad))
                key_grad.append(times(score_grad, queries))
                value_grad.append(times(probs.astype(BF16), outer))
            query_grad = jnp.concatenate(query_grad, 0) * (HEAD ** (-0.5))
            dq_ref[:, lanes] = query_grad.T.astype(BF16)
            key_grad = jnp.where(masks[0], *key_grad) * (HEAD ** (-0.5))
            value_grad = jnp.where(masks[0], *value_grad)
            out_ref[:, local] = key_grad.astype(out_ref.dtype)
            out_ref[:, units + begin : units + begin + PAIR] = value_grad.astype(out_ref.dtype)
        keep += times_t(dq_ref[:share, cols], wq_ref[...])
        send += times_t(dq_ref[share:, cols], wq_ref[...])
    keep_ref[...] = keep
    send_ref[...] = send.astype(BF16)


def cross_backward(a, b, weight, kvs, queries):
    share, width = a.shape
    units = weight.shape[1] // 6
    text = kvs[0].shape[0]
    ins = (a, b, *[weight] * 4, *kvs, queries)
    outs = [
        ((2 * share, 2 * units), BF16),
        ((text, 2 * units), F32),
        ((text, 2 * units), BF16),
        ((share, width), F32),
        ((share, width), BF16),
    ]
    return call(
        cross_backward_body,
        (1,),
        ins,
        [whole_spec(v.shape) for v in ins[:2]]
        + cross_weight_specs(width, units)
        + [whole_spec(v.shape) for v in ins[6:]],
        outs,
        [whole_spec(s) for s, _ in outs],
        [pltpu.VMEM((2 * share, units), BF16)],
    )


def gelu_pair(hidden):
    phi = 0.5 * (1.0 + lax.erf(hidden * (0.5**0.5)))
    density = jnp.exp(-0.5 * hidden * hidden) * 0.3989422804014327
    return hidden * phi, phi + hidden * density


def ffn_products(x, grad, up_ref, down_ref, active_ref, hidden_ref):
    units = up_ref.shape[1]
    size = units // 3 if units % (3 * 128) == 0 else units
    out = back = 0.0
    for begin in range(0, units, size):
        cols = slice(begin, begin + size)
        active, slope = gelu_pair(times(x, up_ref[:, cols]))
        active = active.astype(BF16)
        active_ref[:, cols] = active
        hidden_grad = (times(grad, down_ref[:, cols]) * slope).astype(BF16)
        hidden_ref[:, cols] = hidden_grad
        out += times_t(active, down_ref[:, cols])
        back += times_t(hidden_grad, up_ref[:, cols])
    return out, back


def ffn_first_body(
    xa_ref, xb_ref, ga_ref, gb_ref, up_ref, down_ref, active_ref, hidden_ref, out_ref, back_ref
):
    early = pl.program_id(0) < 2
    x = jnp.where(early, xa_ref[...], xb_ref[...])
    grad = jnp.where(early, ga_ref[...], gb_ref[...])
    out, back = ffn_products(x, grad, up_ref, down_ref, active_ref, hidden_ref)
    out_ref[...] = out
    back_ref[...] = back


def ffn_second_body(
    xa_ref, xb_ref, ga_ref, gb_ref, up_ref, down_ref, out_ref, back_ref,
    active_ref, hidden_ref, out_keep_ref, out_send_ref, keep_ref, send_ref,
):
    early = pl.program_id(0) < 2
    x = jnp.where(early, xa_ref[...], xb_ref[...])
    grad = jnp.where(early, ga_ref[...], gb_ref[...])
    out, back = ffn_products(x, grad, up_ref, down_ref, active_ref, hidden_ref)
    out += out_ref[...]
    back += back_ref[...]

    @pl.when(early)
    def _():
        out_keep_ref[...] = out
        keep_ref[...] = back

    @pl.when(jnp.logical_not(early))
    def _():
        out_send_ref[...] = out.astype(BF16)
        send_ref[...] = back.astype(BF16)


def ffn(x, grad, weight, partial=None):
    half, width = x[0].shape
    share = half // 2
    units = weight.shape[1] // 2
    rows = 2 * half

    def each(i):
        return (i, 0)

    def first(i):
        return (jnp.minimum(i, 1), 0)

    def second(i):
        return (jnp.maximum(i - 2, 0), 0)

    block = (share, width)
    in_specs = [
        pl.BlockSpec(block, first),
        pl.BlockSpec(block, second),
        pl.BlockSpec(block, first),
        pl.BlockSpec(block, second),
        pl.BlockSpec((width, units), lambda i: (0, 0)),
        pl.BlockSpec((width, units), lambda i: (0, 1)),
    ]
    outs = [((rows, units), BF16), ((rows, units), BF16)]
    out_specs = [pl.BlockSpec((share, units), each)] * 2
    if partial is None:
        outs += [((rows, width), F32)] * 2
        out_specs += [pl.BlockSpec(block, each)] * 2
    else:
        in_specs += [pl.BlockSpec(block, each)] * 2
        outs += [((half, width), F32), ((half, width), BF16)] * 2
        out_specs += [pl.BlockSpec(block, first), pl.BlockSpec(block, second)] * 2
    return call(
        ffn_first_body if partial is None else ffn_second_body,
        (4,),
        (*x, *grad, weight, weight, *(partial or ())),
        in_specs,
        outs,
        out_specs,
    )


def weight_grad_body(plan, lefts_count, rights_count, *refs):
    lefts, rights = refs[:lefts_count], refs[lefts_count : lefts_count + rights_count]
    outs = refs[lefts_count + rights_count :]
    begin = 0
    for pairs in plan:
        total = 0.0
        for left, right, first in pairs:
            size = lefts[left].shape[0]
            total += t_times(lefts[left][...], rights[right][first : first + size, :])
        cols = total.shape[1] // len(outs)
        for k, out in enumerate(outs):
            out[:, begin : begin + cols] = total[:, k * cols : (k + 1) * cols].astype(BF16)
        begin += cols


def weight_grad(*parts, split=1):
    lefts, rights, plan = [], [], []
    for part_lefts, part_rights in parts:
        pairs = []
        right = first = 0
        for left in part_lefts:
            pairs.append((len(lefts), len(rights) + right, first))
            lefts.append(left)
            first += left.shape[0]
            if first == part_rights[right].shape[0]:
                right, first = right + 1, 0
        rights += part_rights
        plan.append(pairs)
    width = lefts[0].shape[1]
    cols = sum(part_rights[0].shape[1] for _, part_rights in parts) // split
    size = 256 if width % 256 == 0 else width
    outs = call(
        functools.partial(weight_grad_body, plan, len(lefts), len(rights)),
        (width // size,),
        (*lefts, *rights),
        [pl.BlockSpec((v.shape[0], size), lambda i: (0, i)) for v in lefts]
        + [whole_spec(v.shape) for v in rights],
        [((width, cols), BF16)] * split,
        [pl.BlockSpec((size, cols), lambda i: (i, 0))] * split,
    )
    return outs[0] if split == 1 else outs


def text_project_body(text_ref, weight_ref, out_ref):
    out_ref[...] = times(text_ref[...], weight_ref[...]).astype(BF16)


def text_project(text, weight, block, cols):
    ins = (text, weight)
    specs = [whole_spec(text.shape), pl.BlockSpec((weight.shape[0], cols), lambda i: (0, block))]
    shape = (text.shape[0], cols)
    return call(text_project_body, (1,), ins, specs, [(shape, BF16)], [whole_spec(shape)])[0]


def text_back_body(half, grads_ref, weight_ref, keep_ref, send_ref):
    rows = times_t(grads_ref[...], weight_ref[...])
    for c in range(keep_ref.shape[0]):
        begin = 2 * c * half
        keep_ref[c] = rows[begin : begin + half]
        send_ref[c] = rows[begin + half : begin + 2 * half].astype(BF16)


def text_back(grads, weight, block, clips):
    width, cols = weight.shape[0], grads.shape[1]
    half = grads.shape[0] // clips // 2
    shape = (clips, half, width)
    return call(
        functools.partial(text_back_body, half),
        (1,),
        (grads, weight),
        [whole_spec(grads.shape), pl.BlockSpec((width, cols), lambda i: (0, block))],
        [(shape, F32), (shape, BF16)],
        [whole_spec(shape)] * 2,
    )


def local(
    n,
    audio_states,
    text_states,
    out_grad,
    self_qkv,
    self_out,
    cross_query,
    cross_kv,
    cross_out,
    mlp_up,
    mlp_down,
    norm_gain,
    norm_bias,
):
    clips, share, width = audio_states.shape
    units = self_out.shape[0]
    pairs = units // PAIR
    both = range(clips)

    Order.token = None
    table = ring_table(n)

    qkv_shard = self_qkv.reshape(3, -1, pairs, PAIR).transpose(1, 2, 0, 3).reshape(-1, 3 * units)
    self_ring = RingGather(jnp.concatenate((qkv_shard, self_out.T), 1), n)
    got = self_ring.step()
    params = small_gather(jnp.concatenate((norm_gain, norm_bias), 0), n).astype(F32)
    out_swapped = [swap_chip(out_grad[c]) for c in both]
    cross_own = jnp.concatenate((cross_query, cross_out.T), 1)
    cross_came = swap_chip(cross_own)
    part = mlp_up.shape[1] // 2
    ffn_shards = [
        jnp.concatenate([v[:, k * part : (k + 1) * part] for v in (mlp_up, mlp_down.T)], 1)
        for k in range(2)
    ]

    raw_swapped = [swap_chip(audio_states[c]) for c in both]
    (raw_swapped[0],) = self_ring.turn(raw_swapped[:1])
    raw = gather_rows(audio_states[0], raw_swapped[0])
    full_self = [norm_pair(0, raw, params)]
    (cross_came,) = self_ring.turn([cross_came])
    cross_shard = jnp.concatenate((cross_own, cross_came, cross_kv[0], cross_kv[1]), axis=1)
    raw_swapped[1:] = self_ring.turn(raw_swapped[1:])
    raw = [gather_rows(audio_states[c], raw_swapped[c]) for c in range(1, clips)]
    full_self += [norm_pair(0, v, params) for v in raw]
    cross_ring = RingGather(hold(cross_shard, self_ring.got[-1] if self_ring.got else ()), n)
    cross_ring.step()
    self_w = self_ring.whole()
    text_pair = jnp.concatenate((text_states, swap_chip(text_states)), axis=1)
    text_full = jnp.concatenate((text_pair, swap_core(text_pair)), axis=1)
    qkv, self_attn, self_log, mid_terms = [], [], [], []
    for c in both:
        rows, attn, log, keep, send = self_forward(*full_self[c], self_w, units)
        if c == 0:
            send, out_swapped[0] = cross_ring.turn([send, out_swapped[0]])
        else:
            keep_0, seen_0, other_0 = mid_terms[0][1:]
            send, other_0, *out_swapped[1:] = cross_ring.turn([send, other_0, *out_swapped[1:]])
            mid_terms[0] = (audio_states[0], keep_0, seen_0, other_0)
        mid_terms.append((audio_states[c], *sum_over_tp(keep, send)))
        qkv.append(rows)
        self_attn.append(attn)
        self_log.append(log)
    seen_out = [gather_rows(out_grad[c], out_swapped[c]) for c in both]
    stream_mid, cross_rows = [], []
    for c in both:
        stream, normed = norm_forward(1, mid_terms[c], params, share)
        stream_mid.append(stream)
        cross_rows.append((normed, swap_core(normed)))
        if c == 0:
            cross_ring.turn()
    early_gather = RingGather(hold(ffn_shards[0], cross_ring.got[-1] if cross_ring.got else ()), n)
    early_gather.step()
    cross_w = cross_ring.whole()
    text_rows = text_full.reshape(-1, width)
    text_kv = text_project(text_rows, cross_w, 2, 2 * units).reshape(clips, -1, 2 * units)
    (text_other,) = early_gather.turn([swap_chip(text_kv)])
    cross_q, cross_attn, stream_late, full_ffn = [], [], [], []
    for c in both:
        queries, attn, keep, send = cross_forward(
            *cross_rows[c], cross_w, (text_kv[c], text_other[c])
        )
        if c:
            send, came = early_gather.turn([send, came])
            full_ffn.append(gather_rows(normed_late, came))
        else:
            (send,) = early_gather.turn([send])
        cross_q.append(queries)
        cross_attn.append(attn)
        stream, normed = norm_forward(2, (stream_mid[c], keep, swap_core(send)), params, share)
        stream_late.append(stream)
        normed_late, came = normed, swap_chip(normed)
    late_gather = RingGather(hold(ffn_shards[1], early_gather.got[-1] if early_gather.got else ()), n)
    late_gather.step()
    early_w = early_gather.whole()

    actives, hiddens, partials = [[], []], [[], []], []
    for c in both:
        active, hidden, *partial = ffn(full_ffn[c], seen_out[c], early_w)
        if c == 0:
            (came,) = late_gather.turn([came])
            full_ffn.append(gather_rows(normed_late, came))
        else:
            late_gather.turn()
        actives[0].append(active)
        hiddens[0].append(hidden)
        partials.append(partial)
    grad = weight_grad((sum(full_ffn, ()), hiddens[0]), (sum(seen_out, ()), actives[0]))
    late_gather.turn()
    late_w = late_gather.whole()

    def sum_clips(grad):
        return lax.psum_scatter(grad, "fsdp", scatter_dimension=0, tiled=True)

    (grad,) = tick([grad])
    ffn_totals = [sum_clips(grad)]
    back_terms, out_terms = [], []
    for c in both:
        active, hidden, out_keep, out_send, keep, send = ffn(
            full_ffn[c], seen_out[c], late_w, partials[c]
        )
        if c:
            (send,) = tick([send], back_terms[0][-1])
        back_terms.append(sum_over_tp(keep, send))
        out_terms.append((out_keep, out_send))
        actives[1].append(active)
        hiddens[1].append(hidden)

    norm_sums = [[], [], []]
    grad_mid, grad_in, seen_mid, seen_in = [], [], [], []
    cross_grads, own_kv, other_kv, terms, branches = [], [], [], [], []
    def late_back(c):
        grad, branch, sums = norm_backward(
            2, stream_late[c], out_grad[c], back_terms[c], params, (F32, BF16)
        )
        norm_sums[2].append(sums)
        grad_mid.append(grad)
        seen_mid.append((branch, swap_core(branch)))

    def cross_back(c):
        dq, own, other, keep, send = cross_backward(
            *seen_mid[c], cross_w, (text_kv[c], text_other[c]), cross_q[c]
        )
        cross_grads.append(dq)
        own_kv.append(own)
        other_kv.append(other)
        terms.append((keep, swap_core(send)))

    def mid_back(c):
        grad, branch, sums = norm_backward(
            1, stream_mid[c], grad_mid[c], terms[c], params, (F32, BF16)
        )
        norm_sums[1].append(sums)
        grad_in.append(grad)
        branches.append((branch, swap_chip(branch)))

    late_back(0)
    wide = weight_grad((sum(full_ffn, ()), hiddens[1]), (sum(seen_out, ()), actives[1]))
    wide, other = tick([wide, back_terms[1][-1]])
    back_terms[1] = (*back_terms[1][:-1], other)
    ffn_totals.append(sum_clips(wide))
    for c in both:
        cross_back(c)
        if c + 1 < clips:
            late_back(c + 1)
        mid_back(c)
    kv_came = swap_chip(jnp.stack(other_kv))
    cross_shares = weight_grad(
        (sum(cross_rows, ()), cross_grads), (sum(seen_mid, ()), cross_attn), split=2
    )
    (came,) = tick([branches[0][1]])
    seen_in = [gather_rows(branches[0][0], came)]
    seen_in += [gather_rows(*branches[c]) for c in range(1, clips)]
    first = 2 * units // 3 if units % 192 == 0 else units
    cross_came = [swap_chip(cross_shares[1][:, :first]), swap_chip(cross_shares[1][:, first:])]

    self_grads, in_terms, out_sums = [], [], []
    for c in both:
        grads, keep, send = self_backward(
            *seen_in[c], self_w, qkv[c], self_attn[c], self_log[c]
        )
        if c == 0:
            send, kv_came, cross_came[0] = tick([send, kv_came, cross_came[0]])
        else:
            send, cross_came[1], text_came = tick([send, cross_came[1], text_came])
        in_terms.append(sum_over_tp(keep, send))
        self_grads.append(grads)
        if c == 0:
            kv_grads = (jnp.stack(own_kv) + kv_came.astype(F32)).astype(BF16)
            kv_rows = kv_grads.reshape(-1, 2 * units)
            grad = weight_grad((sum(seen_in, ()), self_attn), ([text_rows], [kv_rows]))
            out_wide = grad
            text_keep, text_send = text_back(kv_rows, cross_w, 2, clips)
            quarter = text_keep.shape[1] // 2
            text_seen = text_keep + swap_core(text_send).astype(F32)
            text_came = swap_chip(text_seen[:, quarter:].astype(BF16))
        else:
            mid_total = sum_clips(sum_beside(cross_shares[0], cross_came, out_wide))
    text_grad = text_seen[:, :quarter] + text_came.astype(F32)
    grad = weight_grad((sum(full_self, ()), self_grads))
    qkv_sum = RingSum([grad], n, table)
    late_terms = [sum_over_tp(*out_terms[c]) for c in both]
    audio_grad, layer_out = [], []
    for c in both:
        grad, sums = norm_backward(0, audio_states[c], grad_in[c], in_terms[c], params, (BF16,))
        norm_sums[0].append(sums)
        audio_grad.append(grad)
        if c == 0:
            qkv_sum.step()
    norm_total = SmallSum(jnp.concatenate([sum(v)[:2] for v in norm_sums], 0), n)
    audio_grad = join(audio_grad)
    qkv_sum.step()
    norm_total.step()
    norm_total.step()
    layer_out.append(sum_terms((stream_late[0], *late_terms[0]), (share, width)))
    qkv_sum.step()
    norm_total.step()
    norm_total.step()
    for c in range(1, clips):
        layer_out.append(sum_terms((stream_late[c], *late_terms[c]), (share, width)))
    layer_out = join(layer_out)
    qkv_total = qkv_sum.total(split=(pairs, 3))
    norm_total = norm_total.total()

    def cut(total, begin, count=1):
        return total[:, begin * units : (begin + count) * units]

    return (
        layer_out,
        audio_grad,
        text_grad.astype(BF16),
        qkv_total,
        cut(mid_total, 2).astype(F32).T,
        cut(mid_total, 0).astype(F32),
        jnp.stack((cut(mid_total, 3), cut(mid_total, 4))).astype(F32),
        cut(mid_total, 1).astype(F32).T,
        jnp.concatenate([v[:, :part] for v in ffn_totals], 1).astype(F32),
        jnp.concatenate([v[:, part:] for v in ffn_totals], 1).astype(F32).T,
        norm_total[0::2],
        norm_total[1::2],
    )


def solution(mesh):
    n = mesh.shape["fsdp"]

    def body(*args):
        return local(n, *args)

    return jax.shard_map(
        body,
        mesh=mesh,
        in_specs=(
            P("fsdp", "tp", None),
            P("fsdp", "tp", None),
            P("fsdp", "tp", None),
            P(None, "fsdp", "tp"),
            P("tp", "fsdp"),
            P("fsdp", "tp"),
            P(None, "fsdp", "tp"),
            P("tp", "fsdp"),
            P("fsdp", "tp"),
            P("tp", "fsdp"),
            P(None, "fsdp"),
            P(None, "fsdp"),
        ),
        out_specs=(
            P("fsdp", "tp", None),
            P("fsdp", "tp", None),
            P("fsdp", "tp", None),
            P(None, "fsdp", "tp"),
            P("tp", "fsdp"),
            P("fsdp", "tp"),
            P(None, "fsdp", "tp"),
            P("tp", "fsdp"),
            P("fsdp", "tp"),
            P("tp", "fsdp"),
            P(None, "fsdp"),
            P(None, "fsdp"),
        ),
        check_vma=False,
    )
```

```python
import functools
import math

import jax
import jax.numpy as jnp
from jax import lax
from jax.experimental import pallas as pl
from jax.experimental.pallas import tpu as pltpu
from jax.sharding import PartitionSpec as P

HEAD = 64
PAIR = 2 * HEAD
EPSILON = 1e-05
F32 = jnp.float32
BF16 = jnp.bfloat16
RATE = HEAD ** (-0.5) * math.log2(math.e)
TOKEN = (8, 128)
COST = 1000
VMEM = 52 * 2**20


def swap_chip(values):
    return lax.ppermute(values, "tp", [(t, t ^ 2) for t in range(4)])


def swap_core(values):
    return lax.ppermute(values, "tp", [(t, t ^ 1) for t in range(4)])


def place_of(share, t):
    apart = share ^ t
    return ((apart & 1) << 1) | (apart >> 1)


def gather_rows(values, swapped):
    pair = jnp.concatenate((values, swapped), axis=0)
    return pair, swap_core(pair)


def ring_of(n):
    return list(range(0, n, 2)) + list(range(n - 1, 0, -2))


def ring_place(n):
    i = lax.axis_index("fsdp")
    return jnp.where(i % 2 == 0, i // 2, n - (i + 1) // 2)


def ring_index(n, place):
    place = lax.rem(place + 2 * n, n)
    return jnp.where(place < n // 2, 2 * place, 2 * (n - place) - 1)


def send_next(values, n):
    ring = ring_of(n)
    return lax.ppermute(values, "fsdp", [(ring[k], ring[(k + 1) % n]) for k in range(n)])


def send_prev(values, n):
    ring = ring_of(n)
    return lax.ppermute(values, "fsdp", [(ring[(k + 1) % n], ring[k]) for k in range(n)])


def ring_table(n):
    return ring_index(n, ring_place(n) + jnp.arange(-(n // 2), n // 2 + 1)).astype(jnp.int32)


def place_pieces_body(n, rows, places, *refs):
    pieces, whole = refs[:-1], refs[-1]
    for piece, (step, offset) in zip(pieces, places):
        begin = ring_index(n, ring_place(n) + step) * rows + offset
        size = piece.shape[0]
        whole[pl.ds(pl.multiple_of(begin, math.gcd(rows, size)), size), :] = piece[...]


class RingGather:
    def __init__(self, shard, n):
        self.n, self.shard, self.got = n, shard, []
        self.direct = n > 16 or n % 2

    def step(self):
        if self.direct:
            return ()
        up, down = self.got[-1] if self.got else (self.shard, self.shard)
        if len(self.got) == self.n // 2 - 1:
            half = self.shard.shape[0] // 2
            up, down = up[:half], down[half:]
        self.got.append((send_next(up, self.n), send_prev(down, self.n)))
        return self.got[-1]

    def turn(self, values=(), *wait):
        if self.direct:
            return tick(list(values), *wait) if values else []
        pair = self.got[-1]
        passed = tick([*pair, *values], *wait)
        self.got[-1] = tuple(passed[:2])
        self.step()
        return passed[2:]

    def whole(self, wait=()):
        if self.direct:
            return lax.all_gather(self.shard, "fsdp", axis=0, tiled=True)
        rows, cols = self.shard.shape
        pieces, places = [self.shard], [(0, 0)]
        for k, pair in enumerate(self.got, 1):
            pieces += pair
            places += [(-k, 0), (k, 0 if k < self.n // 2 else rows // 2)]
        size = 768 if cols % 768 == 0 else cols
        return call(
            functools.partial(place_pieces_body, self.n, rows, places),
            (cols // size,),
            pieces,
            [pl.BlockSpec((v.shape[0], size), lambda i: (0, i)) for v in pieces],
            [((self.n * rows, cols), self.shard.dtype)],
            [pl.BlockSpec((self.n * rows, size), lambda i: (0, i))],
                wait=wait,
        )[0]


def ring_body(kind, rows, count, sides, split, *refs):
    table, wholes = refs[0], refs[1 : 1 + count]
    out_count = count if kind == "end" else len(sides)
    came = refs[1 + count : -out_count - count - 1]
    outs, own, sems = refs[-out_count - count - 1 : -count - 1], refs[-count - 1 : -1], refs[-1]
    copies = []
    for side, (entry, first, last) in enumerate(sides):
        begin = pl.multiple_of(table[entry] * rows + first, rows // 2)
        for k in range(count):
            source = wholes[k].at[pl.ds(begin, last - first), :]
            to = own[k].at[side, pl.ds(0, last - first), :]
            copies.append(pltpu.make_async_copy(source, to, sems.at[side, k]))
    for copy in copies:
        copy.start()
    for copy in copies:
        copy.wait()
    half = rows // 2
    for side, (_, first, last) in enumerate(sides):
        begin = 0
        for k in range(count):
            cols = slice(begin, begin + wholes[k].shape[1])
            begin = cols.stop
            mine = own[k][side, : last - first, :]
            if kind == "begin":
                outs[side][:, cols] = mine
            elif kind == "first":
                add = came[side][:, cols].astype(F32)
                here = slice(side * half, (side + 1) * half)
                there = slice((1 - side) * half, (2 - side) * half)
                outs[side][here, cols] = (mine[here].astype(F32) + add).astype(BF16)
                outs[side][there, cols] = mine[there]
            elif kind == "middle":
                add = came[side][:, cols].astype(F32)
                outs[side][:, cols] = (mine.astype(F32) + add).astype(BF16)
            else:
                total = came[0][:, cols].astype(F32) + came[1][:, cols].astype(F32)
                total += mine.astype(F32)
                if k:
                    outs[k][...] = total
                else:
                    outer, inner = split
                    size = total.shape[1] // (outer * inner)
                    for at in range(outer * inner):
                        to = pl.ds(at // inner * size, size)
                        outs[k][at % inner, :, to] = total[:, at * size : (at + 1) * size]


class RingSum:
    def __init__(self, wholes, n, table):
        self.wholes, self.n, self.table = wholes, n, table
        self.direct = n > 16 or n % 2
        self.left = n // 2
        self.came = ()
        self.step()

    def run(self, kind, step, wait=(), split=None):
        rows = self.wholes[0].shape[0] // self.n
        half = rows // 2
        widths = [v.shape[1] for v in self.wholes]
        middle = self.n // 2
        if kind == "end":
            sides = [(middle, 0, rows)]
        elif kind == "begin":
            sides = [(middle + step, 0, half), (middle - step, half, rows)]
        else:
            sides = [(middle + step, 0, rows), (middle - step, 0, rows)]
        size = half if kind == "begin" else rows
        outs = [((size, sum(widths)), BF16)] * len(sides)
        if kind == "end":
            outs = [((split[1], rows, widths[0] // split[1]), F32)]
            outs += [((rows, cols), F32) for cols in widths[1:]]
        hbm = pl.BlockSpec(memory_space=pltpu.HBM)
        return call(
            functools.partial(ring_body, kind, rows, len(widths), sides, split),
            (1,),
            (self.table, *self.wholes, *self.came),
            [pl.BlockSpec(memory_space=pltpu.SMEM)]
            + [hbm] * len(widths)
            + [whole_spec(v.shape) for v in self.came],
            outs,
            [whole_spec(shape) for shape, _ in outs],
            [pltpu.VMEM((len(sides), rows, cols), BF16) for cols in widths]
            + [pltpu.SemaphoreType.DMA((len(sides), len(widths)))],
            wait=wait,
        )

    def step(self, wait=()):
        if self.direct or not self.left:
            return
        if self.left == self.n // 2:
            kind = "begin"
        else:
            kind = "first" if self.left == self.n // 2 - 1 else "middle"
        up, down = self.run(kind, self.left, wait)
        self.came = (send_next(up, self.n), send_prev(down, self.n))
        self.left -= 1

    def totals(self, split):
        if self.direct:
            totals = [
                lax.psum_scatter(v, "fsdp", scatter_dimension=0, tiled=True).astype(F32)
                for v in self.wholes
            ]
            first = totals[0].reshape(totals[0].shape[0], *split, -1).transpose(2, 0, 1, 3)
            return [first.reshape(*first.shape[:2], -1)] + totals[1:]
        while self.left:
            self.step()
        return self.run("end", 0, split=split)


def swap_fsdp(values, n, bit):
    return lax.ppermute(values, "fsdp", [(i, i ^ bit) for i in range(n)])


def small_gather(shard, n):
    if n & (n - 1):
        return lax.all_gather(shard, "fsdp", axis=1, tiled=True)
    found = shard[None]
    bit = 1
    while bit < n:
        found = jnp.concatenate((found, swap_fsdp(found, n, bit)), axis=0)
        bit *= 2
    found = jnp.take(found, jnp.arange(n) ^ lax.axis_index("fsdp"), axis=0)
    return found.transpose(1, 0, 2).reshape(shard.shape[0], -1)


def times(rows, weight):
    return jnp.dot(rows, weight, preferred_element_type=F32)


def times_t(rows, weight):
    return lax.dot_general(rows, weight, (((1,), (1,)), ((), ())), preferred_element_type=F32)


def t_times(left, right):
    return lax.dot_general(left, right, (((0,), (0,)), ((), ())), preferred_element_type=F32)


def whole_spec(shape):
    return pl.BlockSpec(shape, lambda *_: (0,) * len(shape))


class Order:
    token = None


def call(body, grid, ins, in_specs, outs, out_specs, scratch=(), wait=(), alias=None):
    count = len(ins)
    extra = list(wait) + ([Order.token] if Order.token is not None else [])
    any_spec, hbm = (pl.BlockSpec(memory_space=space) for space in (pl.ANY, pltpu.HBM))

    def run(*refs):
        after = refs[count + len(extra) :]
        body(*refs[:count], *after[: len(outs)], *after[len(outs) + 1 :])
        after[len(outs)][...] = jnp.zeros(TOKEN, F32)

    results = pl.pallas_call(
        run,
        grid=grid,
        in_specs=list(in_specs) + [hbm] * len(wait) + [any_spec] * (len(extra) - len(wait)),
        out_specs=list(out_specs) + [whole_spec(TOKEN)],
        scratch_shapes=list(scratch),
        out_shape=[jax.ShapeDtypeStruct(s, d) for s, d in list(outs) + [(TOKEN, F32)]],
        input_output_aliases=alias or {},
        compiler_params=pltpu.CompilerParams(vmem_limit_bytes=VMEM),
        name=getattr(body, "func", body).__name__,
        cost_estimate=pl.CostEstimate(flops=COST, bytes_accessed=0, transcendentals=0),
    )(*ins, *extra)
    Order.token = results[-1]
    return results[:-1]


def head_masks(rows):
    low = lax.broadcasted_iota(jnp.int32, (rows, PAIR), 1) < HEAD
    return low, jnp.logical_not(low)


def split_heads(block, masks):
    zero = jnp.zeros_like(block)
    return [jnp.where(m, block, zero) for m in masks]


def rows_call(body, ins, outs, sums=(), wait=(), shifts=None, most=128):
    rows = outs[0][0][0]
    block = next((v for v in (most, 96) if rows % v == 0), rows)
    steps = rows // block
    shifts = shifts or [0] * len(ins)
    in_specs = []
    for v, shift in zip(ins, shifts):
        if shift is None:
            in_specs.append(whole_spec(v.shape))
        else:
            first = shift // block
            in_specs.append(
                pl.BlockSpec((block, v.shape[1]), functools.partial(lambda f, i: (i + f, 0), first))
            )
    out_specs = [pl.BlockSpec((block, shape[1]), lambda i: (i, 0)) for shape, _ in outs]
    out_specs += [whole_spec(shape) for shape, _ in sums]
    return call(
        body, (steps,), ins, in_specs, list(outs) + list(sums), out_specs, wait=wait
    )


def tick_body(*refs):
    pass


def tick(values, *wait):
    spec = pl.BlockSpec(memory_space=pl.ANY)
    count = len(values)
    return call(
        tick_body,
        (1,),
        values,
        [spec] * count,
        [(v.shape, v.dtype) for v in values],
        [spec] * count,
        wait=wait,
        alias={k: k for k in range(count)},
    )


def copy_body(from_ref, to_ref):
    to_ref[...] = from_ref[...]


def hold(values, wait=()):
    return rows_call(copy_body, (values,), [(values.shape, values.dtype)], wait=wait)[0]


def add_body(keep_ref, seen_ref, out_ref):
    out_ref[...] = (keep_ref[...] + seen_ref[...].astype(F32)).astype(BF16)


def sum_over_tp(keep, send, wait=()):
    seen = swap_core(send)
    half = keep.shape[0] // 2
    (passed,) = rows_call(
        add_body, (keep, seen), [((half, keep.shape[1]), BF16)], shifts=(half, half), wait=wait
    )
    return keep, seen, swap_chip(passed)


def total_of(refs):
    return sum(ref[...].astype(F32) for ref in refs)


def norm_forward_body(index, *refs):
    params, outs = refs[-3], refs[-2:]
    stream = total_of(refs[:-3])
    outs[0][...] = stream
    center = stream - jnp.mean(stream, axis=-1, keepdims=True)
    spread = jnp.mean(center * center, axis=-1, keepdims=True)
    gain, bias = params[index : index + 1, :], params[3 + index : 4 + index, :]
    outs[1][...] = (center * lax.rsqrt(spread + EPSILON) * gain + bias).astype(BF16)


def norm_forward(index, terms, params, rows, wait=()):
    shape = (rows, params.shape[1])
    return rows_call(
        functools.partial(norm_forward_body, index),
        (*terms, params),
        [(shape, F32), (shape, BF16)],
        shifts=[0] * len(terms) + [None],
        wait=wait,
    )


def norm_pair_body(index, left_ref, right_ref, params, *outs):
    gain, bias = params[index : index + 1, :], params[3 + index : 4 + index, :]
    for ref, out in zip((left_ref, right_ref), outs):
        stream = ref[...].astype(F32)
        center = stream - jnp.mean(stream, axis=-1, keepdims=True)
        spread = jnp.mean(center * center, axis=-1, keepdims=True)
        out[...] = (center * lax.rsqrt(spread + EPSILON) * gain + bias).astype(BF16)


def norm_pair(index, pair, params):
    return tuple(
        rows_call(
            functools.partial(norm_pair_body, index),
            (*pair, params),
            [(v.shape, BF16) for v in pair],
            shifts=[0, 0, None],
        )
    )


def norm_backward_body(index, count, *refs):
    stream_ref, base_ref, terms = refs[0], refs[1], refs[2 : 2 + count]
    params, outs, sums = refs[2 + count], refs[3 + count : -1], refs[-1]
    stream = stream_ref[...].astype(F32)
    center = stream - jnp.mean(stream, axis=-1, keepdims=True)
    scale = lax.rsqrt(jnp.mean(center * center, axis=-1, keepdims=True) + EPSILON)
    xhat = center * scale
    grad = total_of(terms)
    e = grad * params[index : index + 1, :]
    back = scale * (
        e - jnp.mean(e, axis=-1, keepdims=True) - xhat * jnp.mean(e * xhat, axis=-1, keepdims=True)
    )
    total = base_ref[...].astype(F32) + back
    for out in outs:
        out[...] = total.astype(out.dtype)

    @pl.when(pl.program_id(0) == 0)
    def _():
        sums[...] = jnp.zeros_like(sums)

    sums[0:1, :] += jnp.sum(grad * xhat, axis=0, keepdims=True)
    sums[1:2, :] += jnp.sum(grad, axis=0, keepdims=True)


def norm_backward(index, stream, base, terms, params, kinds):
    shape = stream.shape
    return rows_call(
        functools.partial(norm_backward_body, index, len(terms)),
        (stream, base, *terms, params),
        [(shape, kind) for kind in kinds],
        [((8, shape[1]), F32)],
        shifts=[0] * (2 + len(terms)) + [None],
    )


def sum_pair_body(left_ref, right_ref, out_ref):
    out_ref[...] = left_ref[...] + right_ref[...]


class SmallSum:
    def __init__(self, whole, n):
        self.whole, self.n = whole, n
        self.swaps = [swap_core, swap_chip]
        if n & (n - 1):
            self.whole = lax.psum(whole, "fsdp")
        else:
            bits = [2**k for k in range(n.bit_length() - 1)]
            self.swaps += [functools.partial(swap_fsdp, n=n, bit=bit) for bit in bits]
        self.came = self.swaps.pop(0)(self.whole)

    def step(self):
        if self.came is None:
            return
        shape = self.whole.shape
        (self.whole,) = call(
            sum_pair_body,
            (1,),
            (self.whole, self.came),
            [whole_spec(shape)] * 2,
            [(shape, F32)],
            [whole_spec(shape)],
        )
        self.came = self.swaps.pop(0)(self.whole) if self.swaps else None

    def total(self):
        while self.came is not None:
            self.step()
        cols = self.whole.shape[1] // self.n
        begin = lax.axis_index("fsdp") * cols
        return lax.dynamic_slice(self.whole, (0, begin), (self.whole.shape[0], cols))


def join_body(count, *refs):
    outs = refs[count]
    for k in range(count):
        outs[k] = refs[k][...]


def join(parts):
    shape, kind = parts[0].shape, parts[0].dtype
    block = 128 if shape[0] % 128 == 0 else shape[0]
    return call(
        functools.partial(join_body, len(parts)),
        (shape[0] // block,),
        parts,
        [pl.BlockSpec((block, shape[1]), lambda i: (i, 0))] * len(parts),
        [((len(parts), *shape), kind)],
        [pl.BlockSpec((len(parts), block, shape[1]), lambda i: (0, i, 0))],
    )[0]


def sum_terms_body(*refs):
    refs[-1][...] = total_of(refs[:-1]).astype(BF16)


def sum_terms(terms, shape, most=128):
    return rows_call(sum_terms_body, terms, [(shape, BF16)], most=most)[0]


def self_forward_body(
    a_ref, b_ref, w_ref, wo_ref, qkv_ref, attn_ref, lse_ref, keep_ref, send_ref, vt_ref
):
    step = pl.program_id(0)
    t = lax.axis_index("tp")
    half = a_ref.shape[0]
    share = half // 2
    qkv_ref[:half, :] = times(a_ref[...], w_ref[...]).astype(BF16)
    qkv_ref[half:, :] = times(b_ref[...], w_ref[...]).astype(BF16)
    vt_ref[...] = qkv_ref[:, 2 * PAIR :].T
    masks = head_masks(share)
    at = [pl.ds(pl.multiple_of(place_of(g, t) * share, share), share) for g in range(4)]
    seen = lax.broadcasted_iota(jnp.int32, (share, share), 0) <= lax.broadcasted_iota(
        jnp.int32, (share, share), 1
    )
    lanes = pl.ds(pl.multiple_of(step * PAIR, PAIR), PAIR)
    for g in range(4):
        queries = split_heads(qkv_ref[at[g], :PAIR], masks)
        found = []
        for e in range(2):
            scores = []
            for b in range(g + 1):
                s = times_t(qkv_ref[at[b], PAIR : 2 * PAIR], queries[e])
                scores.append(jnp.where(seen, s, -1e30) if b == g else s)
            peak = functools.reduce(
                jnp.maximum, [jnp.max(s, axis=0, keepdims=True) for s in scores]
            )
            peak = peak * RATE
            probs = [jnp.exp2(s * RATE - peak) for s in scores]
            total = sum(jnp.sum(p, axis=0, keepdims=True) for p in probs)
            rows = slice(e * HEAD, (e + 1) * HEAD)
            mixed = sum(times(vt_ref[rows, at[b]], probs[b].astype(BF16)) for b in range(g + 1))
            found.append(mixed / total)
            lse_ref[e : e + 1, at[g]] = peak + jnp.log2(total)
        attn_ref[at[g], lanes] = jnp.concatenate(found, 0).T.astype(BF16)

    @pl.when(step == pl.num_programs(0) - 1)
    def _():
        for k in range(2):
            rows = slice(k * share, (k + 1) * share)
            keep_ref[rows, :] = times_t(attn_ref[rows, :], wo_ref[...])
            late = slice(half + k * share, half + (k + 1) * share)
            send_ref[rows, :] = times_t(attn_ref[late, :], wo_ref[...]).astype(BF16)


def self_forward(a, b, weight, units):
    half, width = a.shape
    pairs = units // PAIR
    rows = 2 * half
    return call(
        self_forward_body,
        (pairs,),
        (a, b, weight, weight),
        [
            whole_spec((half, width)),
            whole_spec((half, width)),
            pl.BlockSpec((width, 3 * PAIR), lambda h: (0, h)),
            pl.BlockSpec((width, units), lambda h: (0, 3)),
        ],
        [
            ((rows, 3 * units), BF16),
            ((rows, units), BF16),
            ((8 * pairs, rows), F32),
            ((half, width), F32),
            ((half, width), BF16),
        ],
        [
            pl.BlockSpec((rows, 3 * PAIR), lambda h: (0, h)),
            whole_spec((rows, units)),
            pl.BlockSpec((8, rows), lambda h: (h, 0)),
            whole_spec((half, width)),
            whole_spec((half, width)),
        ],
        [pltpu.VMEM((PAIR, rows), BF16)],
    )


def self_backward_body(
    a_ref, b_ref, wo_ref, w_ref, qkv_ref, attn_ref, lse_ref,
    grads_ref, keep_ref, send_ref, hg_ref, kt_ref, dk_ref, dv_ref,
):
    step = pl.program_id(0)
    t = lax.axis_index("tp")
    half = a_ref.shape[0]
    share = half // 2
    hg_ref[:half, :] = times(a_ref[...], wo_ref[...]).astype(BF16)
    hg_ref[half:, :] = times(b_ref[...], wo_ref[...]).astype(BF16)
    kt_ref[...] = qkv_ref[:, PAIR : 2 * PAIR].T
    dk_ref[...] = jnp.zeros_like(dk_ref)
    dv_ref[...] = jnp.zeros_like(dv_ref)
    masks = head_masks(share)
    at = [pl.ds(pl.multiple_of(place_of(g, t) * share, share), share) for g in range(4)]
    seen = lax.broadcasted_iota(jnp.int32, (share, share), 0) <= lax.broadcasted_iota(
        jnp.int32, (share, share), 1
    )
    base = step * 3 * PAIR
    lanes = [pl.ds(pl.multiple_of(base + c * PAIR, PAIR), PAIR) for c in range(3)]
    for g in range(4):
        queries = split_heads(qkv_ref[at[g], :PAIR], masks)
        block = hg_ref[at[g], :]
        outer = split_heads(block, masks)
        inner = (block.astype(F32) * attn_ref[at[g], :].astype(F32)).T
        query_grad = []
        for e in range(2):
            rows = slice(e * HEAD, (e + 1) * HEAD)
            lse = lse_ref[e : e + 1, at[g]]
            delta = jnp.sum(inner[rows], axis=0, keepdims=True)
            total = jnp.zeros((HEAD, share), F32)
            for b in range(g + 1):
                s = times_t(qkv_ref[at[b], PAIR : 2 * PAIR], queries[e])
                probs = jnp.exp2(s * RATE - lse)
                if b == g:
                    probs = jnp.where(seen, probs, 0.0)
                grad = times_t(qkv_ref[at[b], 2 * PAIR :], outer[e])
                score_grad = (probs * (grad - delta)).astype(BF16)
                dv_ref[at[b], :] += times(probs.astype(BF16), outer[e])
                dk_ref[at[b], :] += times(score_grad, queries[e])
                total += times(kt_ref[rows, at[b]], score_grad)
            query_grad.append(total)
        query_grad = jnp.concatenate(query_grad, 0) * (HEAD ** (-0.5))
        grads_ref[at[g], lanes[0]] = query_grad.T.astype(BF16)
    grads_ref[:, lanes[1]] = (dk_ref[...] * (HEAD ** (-0.5))).astype(BF16)
    grads_ref[:, lanes[2]] = dv_ref[...].astype(BF16)

    @pl.when(step == pl.num_programs(0) - 1)
    def _():
        for k in range(2):
            rows = slice(k * share, (k + 1) * share)
            keep_ref[rows, :] = times_t(grads_ref[rows, :], w_ref[...])
            late = slice(half + k * share, half + (k + 1) * share)
            send_ref[rows, :] = times_t(grads_ref[late, :], w_ref[...]).astype(BF16)


def self_backward(a, b, weight, qkv, attn, lse):
    half, width = a.shape
    units = attn.shape[1]
    pairs = units // PAIR
    rows = 2 * half
    return call(
        self_backward_body,
        (pairs,),
        (a, b, weight, weight, qkv, attn, lse),
        [
            whole_spec((half, width)),
            whole_spec((half, width)),
            pl.BlockSpec((width, PAIR), lambda h: (0, 3 * pairs + h)),
            whole_spec((width, 3 * units)),
            pl.BlockSpec((rows, 3 * PAIR), lambda h: (0, h)),
            pl.BlockSpec((rows, PAIR), lambda h: (0, h)),
            pl.BlockSpec((8, rows), lambda h: (h, 0)),
        ],
        [
            ((rows, 3 * units), BF16),
            ((half, width), F32),
            ((half, width), BF16),
        ],
        [
            whole_spec((rows, 3 * units)),
            whole_spec((half, width)),
            whole_spec((half, width)),
        ],
        [
            pltpu.VMEM((rows, PAIR), BF16),
            pltpu.VMEM((PAIR, rows), BF16),
            pltpu.VMEM((rows, PAIR), F32),
            pltpu.VMEM((rows, PAIR), F32),
        ],
    )


def cross_weight_specs(width, units):
    return [pl.BlockSpec((width, units), functools.partial(lambda j, _: (0, j), j)) for j in (0, 2, 1, 3)]


def cross_probs(keys, queries):
    s = times_t(keys, queries)
    peak = jnp.max(s, axis=0, keepdims=True) * RATE
    probs = jnp.exp2(s * RATE - peak)
    return probs / jnp.sum(probs, axis=0, keepdims=True)


def cross_forward_body(
    a_ref, b_ref, wq0_ref, wq1_ref, wo0_ref, wo1_ref, kv0_ref, kv1_ref,
    q_ref, attn_ref, keep_ref, send_ref,
):
    share = a_ref.shape[0]
    units = wq0_ref.shape[1]
    masks = head_masks(kv0_ref.shape[0])
    keep = send = 0.0
    for j, (wq_ref, wo_ref, kv_ref) in enumerate(
        ((wq0_ref, wo0_ref, kv0_ref), (wq1_ref, wo1_ref, kv1_ref))
    ):
        cols = slice(j * units, (j + 1) * units)
        q_ref[:share, cols] = times(a_ref[...], wq_ref[...]).astype(BF16)
        q_ref[share:, cols] = times(b_ref[...], wq_ref[...]).astype(BF16)
        for begin in range(0, units, PAIR):
            lanes = slice(j * units + begin, j * units + begin + PAIR)
            queries = q_ref[:, lanes]
            keys = split_heads(kv_ref[:, begin : begin + PAIR], masks)
            values = kv_ref[:, units + begin : units + begin + PAIR].T
            mixed = [
                times(
                    values[e * HEAD : (e + 1) * HEAD],
                    cross_probs(keys[e], queries).astype(BF16),
                )
                for e in range(2)
            ]
            attn_ref[:, lanes] = jnp.concatenate(mixed, 0).T.astype(BF16)
        keep += times_t(attn_ref[:share, cols], wo_ref[...])
        send += times_t(attn_ref[share:, cols], wo_ref[...])
    keep_ref[...] = keep
    send_ref[...] = send.astype(BF16)


def cross_forward(a, b, weight, kvs):
    share, width = a.shape
    units = weight.shape[1] // 6
    ins = (a, b, *[weight] * 4, *kvs)
    outs = [
        ((2 * share, 2 * units), BF16),
        ((2 * share, 2 * units), BF16),
        ((share, width), F32),
        ((share, width), BF16),
    ]
    return call(
        cross_forward_body,
        (1,),
        ins,
        [whole_spec(v.shape) for v in ins[:2]]
        + cross_weight_specs(width, units)
        + [whole_spec(v.shape) for v in ins[6:]],
        outs,
        [whole_spec(s) for s, _ in outs],
    )


def cross_backward_body(
    a_ref, b_ref, wq0_ref, wq1_ref, wo0_ref, wo1_ref, kv0_ref, kv1_ref, q_ref,
    dq_ref, own_ref, other_ref, keep_ref, send_ref, hg_ref,
):
    share = a_ref.shape[0]
    units = wq0_ref.shape[1]
    text = kv0_ref.shape[0]
    masks = head_masks(text)
    keep = send = 0.0
    for j, (wq_ref, wo_ref, kv_ref, out_ref) in enumerate(
        ((wq0_ref, wo0_ref, kv0_ref, own_ref), (wq1_ref, wo1_ref, kv1_ref, other_ref))
    ):
        cols = slice(j * units, (j + 1) * units)
        hg_ref[:share, :] = times(a_ref[...], wo_ref[...]).astype(BF16)
        hg_ref[share:, :] = times(b_ref[...], wo_ref[...]).astype(BF16)
        for begin in range(0, units, PAIR):
            lanes = slice(j * units + begin, j * units + begin + PAIR)
            local = slice(begin, begin + PAIR)
            queries = q_ref[:, lanes]
            outer = hg_ref[:, local]
            pair_keys = kv_ref[:, local]
            keys = split_heads(pair_keys, masks)
            values = split_heads(kv_ref[:, units + begin : units + begin + PAIR], masks)
            keys_t = pair_keys.T
            query_grad, key_grad, value_grad = [], [], []
            for e in range(2):
                probs = cross_probs(keys[e], queries)
                grad = times_t(values[e], outer)
                inner = jnp.sum(probs * grad, axis=0, keepdims=True)
                score_grad = (probs * (grad - inner)).astype(BF16)
                query_grad.append(times(keys_t[e * HEAD : (e + 1) * HEAD], score_grad))
                key_grad.append(times(score_grad, queries))
                value_grad.append(times(probs.astype(BF16), outer))
            query_grad = jnp.concatenate(query_grad, 0) * (HEAD ** (-0.5))
            dq_ref[:, lanes] = query_grad.T.astype(BF16)
            key_grad = jnp.where(masks[0], *key_grad) * (HEAD ** (-0.5))
            value_grad = jnp.where(masks[0], *value_grad)
            out_ref[:, local] = key_grad.astype(out_ref.dtype)
            out_ref[:, units + begin : units + begin + PAIR] = value_grad.astype(out_ref.dtype)
        keep += times_t(dq_ref[:share, cols], wq_ref[...])
        send += times_t(dq_ref[share:, cols], wq_ref[...])
    keep_ref[...] = keep
    send_ref[...] = send.astype(BF16)


def cross_backward(a, b, weight, kvs, queries):
    share, width = a.shape
    units = weight.shape[1] // 6
    text = kvs[0].shape[0]
    ins = (a, b, *[weight] * 4, *kvs, queries)
    outs = [
        ((2 * share, 2 * units), BF16),
        ((text, 2 * units), F32),
        ((text, 2 * units), BF16),
        ((share, width), F32),
        ((share, width), BF16),
    ]
    return call(
        cross_backward_body,
        (1,),
        ins,
        [whole_spec(v.shape) for v in ins[:2]]
        + cross_weight_specs(width, units)
        + [whole_spec(v.shape) for v in ins[6:]],
        outs,
        [whole_spec(s) for s, _ in outs],
        [pltpu.VMEM((2 * share, units), BF16)],
    )


def gelu_pair(hidden):
    phi = 0.5 * (1.0 + lax.erf(hidden * (0.5**0.5)))
    density = jnp.exp(-0.5 * hidden * hidden) * 0.3989422804014327
    return hidden * phi, phi + hidden * density


def ffn_products(x, grad, up_ref, down_ref, active_ref, hidden_ref):
    units = up_ref.shape[1]
    size = units // 3 if units % (3 * 128) == 0 else units
    out = back = 0.0
    for begin in range(0, units, size):
        cols = slice(begin, begin + size)
        active, slope = gelu_pair(times(x, up_ref[:, cols]))
        active = active.astype(BF16)
        active_ref[:, cols] = active
        hidden_grad = (times(grad, down_ref[:, cols]) * slope).astype(BF16)
        hidden_ref[:, cols] = hidden_grad
        out += times_t(active, down_ref[:, cols])
        back += times_t(hidden_grad, up_ref[:, cols])
    return out, back


def ffn_first_body(
    xa_ref, xb_ref, ga_ref, gb_ref, up_ref, down_ref, active_ref, hidden_ref, out_ref, back_ref
):
    early = pl.program_id(0) < 2
    x = jnp.where(early, xa_ref[...], xb_ref[...])
    grad = jnp.where(early, ga_ref[...], gb_ref[...])
    out, back = ffn_products(x, grad, up_ref, down_ref, active_ref, hidden_ref)
    out_ref[...] = out
    back_ref[...] = back


def ffn_second_body(
    xa_ref, xb_ref, ga_ref, gb_ref, up_ref, down_ref, out_ref, back_ref,
    active_ref, hidden_ref, out_keep_ref, out_send_ref, keep_ref, send_ref,
):
    early = pl.program_id(0) < 2
    x = jnp.where(early, xa_ref[...], xb_ref[...])
    grad = jnp.where(early, ga_ref[...], gb_ref[...])
    out, back = ffn_products(x, grad, up_ref, down_ref, active_ref, hidden_ref)
    out += out_ref[...]
    back += back_ref[...]

    @pl.when(early)
    def _():
        out_keep_ref[...] = out
        keep_ref[...] = back

    @pl.when(jnp.logical_not(early))
    def _():
        out_send_ref[...] = out.astype(BF16)
        send_ref[...] = back.astype(BF16)


def ffn(x, grad, weight, partial=None):
    half, width = x[0].shape
    share = half // 2
    units = weight.shape[1] // 2
    rows = 2 * half

    def each(i):
        return (i, 0)

    def first(i):
        return (jnp.minimum(i, 1), 0)

    def second(i):
        return (jnp.maximum(i - 2, 0), 0)

    block = (share, width)
    in_specs = [
        pl.BlockSpec(block, first),
        pl.BlockSpec(block, second),
        pl.BlockSpec(block, first),
        pl.BlockSpec(block, second),
        pl.BlockSpec((width, units), lambda i: (0, 0)),
        pl.BlockSpec((width, units), lambda i: (0, 1)),
    ]
    outs = [((rows, units), BF16), ((rows, units), BF16)]
    out_specs = [pl.BlockSpec((share, units), each)] * 2
    if partial is None:
        outs += [((rows, width), F32)] * 2
        out_specs += [pl.BlockSpec(block, each)] * 2
    else:
        in_specs += [pl.BlockSpec(block, each)] * 2
        outs += [((half, width), F32), ((half, width), BF16)] * 2
        out_specs += [pl.BlockSpec(block, first), pl.BlockSpec(block, second)] * 2
    return call(
        ffn_first_body if partial is None else ffn_second_body,
        (4,),
        (*x, *grad, weight, weight, *(partial or ())),
        in_specs,
        outs,
        out_specs,
    )


def weight_grad_body(plan, lefts_count, rights_count, *refs):
    lefts, rights = refs[:lefts_count], refs[lefts_count : lefts_count + rights_count]
    outs = refs[lefts_count + rights_count :]
    begin = 0
    for pairs in plan:
        total = 0.0
        for left, right, first in pairs:
            size = lefts[left].shape[0]
            total += t_times(lefts[left][...], rights[right][first : first + size, :])
        cols = total.shape[1] // len(outs)
        for k, out in enumerate(outs):
            out[:, begin : begin + cols] = total[:, k * cols : (k + 1) * cols].astype(BF16)
        begin += cols


def weight_grad(*parts, split=1):
    lefts, rights, plan = [], [], []
    for part_lefts, part_rights in parts:
        pairs = []
        right = first = 0
        for left in part_lefts:
            pairs.append((len(lefts), len(rights) + right, first))
            lefts.append(left)
            first += left.shape[0]
            if first == part_rights[right].shape[0]:
                right, first = right + 1, 0
        rights += part_rights
        plan.append(pairs)
    width = lefts[0].shape[1]
    cols = sum(part_rights[0].shape[1] for _, part_rights in parts) // split
    size = 256 if width % 256 == 0 else width
    outs = call(
        functools.partial(weight_grad_body, plan, len(lefts), len(rights)),
        (width // size,),
        (*lefts, *rights),
        [pl.BlockSpec((v.shape[0], size), lambda i: (0, i)) for v in lefts]
        + [whole_spec(v.shape) for v in rights],
        [((width, cols), BF16)] * split,
        [pl.BlockSpec((size, cols), lambda i: (i, 0))] * split,
    )
    return outs[0] if split == 1 else outs


def text_project_body(text_ref, weight_ref, out_ref):
    out_ref[...] = times(text_ref[...], weight_ref[...]).astype(BF16)


def text_project(text, weight, block, cols):
    ins = (text, weight)
    specs = [whole_spec(text.shape), pl.BlockSpec((weight.shape[0], cols), lambda i: (0, block))]
    shape = (text.shape[0], cols)
    return call(text_project_body, (1,), ins, specs, [(shape, BF16)], [whole_spec(shape)])[0]


def text_back_body(half, grads_ref, weight_ref, keep_ref, send_ref):
    rows = times_t(grads_ref[...], weight_ref[...])
    for c in range(keep_ref.shape[0]):
        begin = 2 * c * half
        keep_ref[c] = rows[begin : begin + half]
        send_ref[c] = rows[begin + half : begin + 2 * half].astype(BF16)


def text_back(grads, weight, block, clips):
    width, cols = weight.shape[0], grads.shape[1]
    half = grads.shape[0] // clips // 2
    shape = (clips, half, width)
    return call(
        functools.partial(text_back_body, half),
        (1,),
        (grads, weight),
        [whole_spec(grads.shape), pl.BlockSpec((width, cols), lambda i: (0, block))],
        [(shape, F32), (shape, BF16)],
        [whole_spec(shape)] * 2,
    )


def local(
    n,
    audio_states,
    text_states,
    out_grad,
    self_qkv,
    self_out,
    cross_query,
    cross_kv,
    cross_out,
    mlp_up,
    mlp_down,
    norm_gain,
    norm_bias,
):
    clips, share, width = audio_states.shape
    units = self_out.shape[0]
    pairs = units // PAIR
    both = range(clips)

    Order.token = None
    table = ring_table(n)

    qkv_shard = self_qkv.reshape(3, -1, pairs, PAIR).transpose(1, 2, 0, 3).reshape(-1, 3 * units)
    self_ring = RingGather(jnp.concatenate((qkv_shard, self_out.T), 1), n)
    got = self_ring.step()
    params = small_gather(jnp.concatenate((norm_gain, norm_bias), 0), n).astype(F32)
    out_swapped = [swap_chip(out_grad[c]) for c in both]
    cross_own = jnp.concatenate((cross_query, cross_out.T), 1)
    cross_came = swap_chip(cross_own)
    part = mlp_up.shape[1] // 2
    ffn_shards = [
        jnp.concatenate([v[:, k * part : (k + 1) * part] for v in (mlp_up, mlp_down.T)], 1)
        for k in range(2)
    ]

    raw_swapped = [swap_chip(audio_states[c]) for c in both]
    cross_came, raw_swapped[0] = self_ring.turn([cross_came, raw_swapped[0]])
    cross_shard = jnp.concatenate((cross_own, cross_came, cross_kv[0], cross_kv[1]), axis=1)
    raw = gather_rows(audio_states[0], raw_swapped[0])
    self_ring.turn()
    full_self = [norm_pair(0, raw, params)]
    raw_swapped[1:] = self_ring.turn(raw_swapped[1:])
    raw = [gather_rows(audio_states[c], raw_swapped[c]) for c in range(1, clips)]
    full_self += [norm_pair(0, v, params) for v in raw]
    cross_ring = RingGather(hold(cross_shard, self_ring.got[-1] if self_ring.got else ()), n)
    cross_ring.step()
    self_w = self_ring.whole()
    text_pair = jnp.concatenate((text_states, swap_chip(text_states)), axis=1)
    text_full = jnp.concatenate((text_pair, swap_core(text_pair)), axis=1)
    qkv, self_attn, self_log, mid_terms = [], [], [], []
    for c in both:
        rows, attn, log, keep, send = self_forward(*full_self[c], self_w, units)
        if c == 0:
            send, out_swapped[0] = cross_ring.turn([send, out_swapped[0]])
            seen_out = [gather_rows(out_grad[0], out_swapped[0])]
        else:
            keep_0, seen_0, other_0 = mid_terms[0][1:]
            send, other_0 = cross_ring.turn([send, other_0])
            mid_terms[0] = (audio_states[0], keep_0, seen_0, other_0)
        mid_terms.append((audio_states[c], *sum_over_tp(keep, send)))
        qkv.append(rows)
        self_attn.append(attn)
        self_log.append(log)
    stream_mid, cross_rows = [], []
    for c in both:
        stream, normed = norm_forward(1, mid_terms[c], params, share)
        stream_mid.append(stream)
        cross_rows.append((normed, swap_core(normed)))
        if c == 0:
            cross_ring.turn()
    early_gather = RingGather(hold(ffn_shards[0], cross_ring.got[-1] if cross_ring.got else ()), n)
    early_gather.step()
    cross_w = cross_ring.whole()
    text_rows = text_full.reshape(-1, width)
    text_kv = text_project(text_rows, cross_w, 2, 2 * units).reshape(clips, -1, 2 * units)
    (text_other,) = early_gather.turn([swap_chip(text_kv)])
    cross_q, cross_attn, stream_late, full_ffn = [], [], [], []
    for c in both:
        queries, attn, keep, send = cross_forward(
            *cross_rows[c], cross_w, (text_kv[c], text_other[c])
        )
        if c:
            send, came = early_gather.turn([send, came])
            full_ffn.append(gather_rows(normed_late, came))
        else:
            send, *out_swapped[1:] = early_gather.turn([send, *out_swapped[1:]])
            seen_out += [gather_rows(out_grad[k], out_swapped[k]) for k in range(1, clips)]
        cross_q.append(queries)
        cross_attn.append(attn)
        stream, normed = norm_forward(2, (stream_mid[c], keep, swap_core(send)), params, share)
        stream_late.append(stream)
        normed_late, came = normed, swap_chip(normed)
    late_gather = RingGather(hold(ffn_shards[1], early_gather.got[-1] if early_gather.got else ()), n)
    late_gather.step()
    early_w = early_gather.whole()

    actives, hiddens, partials = [[], []], [[], []], []
    for c in both:
        active, hidden, *partial = ffn(full_ffn[c], seen_out[c], early_w)
        if c == 0:
            (came,) = late_gather.turn([came])
            full_ffn.append(gather_rows(normed_late, came))
        else:
            late_gather.turn()
        actives[0].append(active)
        hiddens[0].append(hidden)
        partials.append(partial)
    grad = weight_grad((sum(full_ffn, ()), hiddens[0]), (sum(seen_out, ()), actives[0]))
    late_gather.turn()
    late_w = late_gather.whole()

    def sum_clips(grad):
        return lax.psum_scatter(grad, "fsdp", scatter_dimension=0, tiled=True)

    (grad,) = tick([grad])
    ffn_totals = [sum_clips(grad)]
    back_terms, out_terms = [], []
    for c in both:
        active, hidden, out_keep, out_send, keep, send = ffn(
            full_ffn[c], seen_out[c], late_w, partials[c]
        )
        if c:
            (send,) = tick([send], back_terms[0][-1])
        back_terms.append(sum_over_tp(keep, send))
        out_terms.append((out_keep, out_send))
        actives[1].append(active)
        hiddens[1].append(hidden)

    norm_sums = [[], [], []]
    grad_mid, grad_in, seen_mid, seen_in = [], [], [], []
    cross_grads, own_kv, other_kv, terms, branches = [], [], [], [], []
    def late_back(c):
        grad, branch, sums = norm_backward(
            2, stream_late[c], out_grad[c], back_terms[c], params, (F32, BF16)
        )
        norm_sums[2].append(sums)
        grad_mid.append(grad)
        seen_mid.append((branch, swap_core(branch)))

    def cross_back(c):
        dq, own, other, keep, send = cross_backward(
            *seen_mid[c], cross_w, (text_kv[c], text_other[c]), cross_q[c]
        )
        cross_grads.append(dq)
        own_kv.append(own)
        other_kv.append(other)
        terms.append((keep, swap_core(send)))

    def mid_back(c):
        grad, branch, sums = norm_backward(
            1, stream_mid[c], grad_mid[c], terms[c], params, (F32, BF16)
        )
        norm_sums[1].append(sums)
        grad_in.append(grad)
        branches.append((branch, swap_chip(branch)))

    late_back(0)
    wide = weight_grad((sum(full_ffn, ()), hiddens[1]), (sum(seen_out, ()), actives[1]))
    wide, other = tick([wide, back_terms[1][-1]])
    back_terms[1] = (*back_terms[1][:-1], other)
    ffn_totals.append(sum_clips(wide))
    for c in both:
        cross_back(c)
        if c + 1 < clips:
            late_back(c + 1)
        mid_back(c)
    kv_came = swap_chip(jnp.stack(other_kv))
    cross_shares = weight_grad(
        (sum(cross_rows, ()), cross_grads), (sum(seen_mid, ()), cross_attn), split=2
    )
    (came,) = tick([branches[0][1]])
    seen_in = [gather_rows(branches[0][0], came)]
    seen_in += [gather_rows(*branches[c]) for c in range(1, clips)]
    cross_came = swap_chip(cross_shares[1])

    self_grads, in_terms, out_sums = [], [], []
    for c in both:
        grads, keep, send = self_backward(
            *seen_in[c], self_w, qkv[c], self_attn[c], self_log[c]
        )
        if c == 0:
            send, kv_came = tick([send, kv_came])
        else:
            send, text_came = tick([send, text_came])
        in_terms.append(sum_over_tp(keep, send))
        self_grads.append(grads)
        if c == 0:
            kv_grads = (jnp.stack(own_kv) + kv_came.astype(F32)).astype(BF16)
            kv_rows = kv_grads.reshape(-1, 2 * units)
            grad = weight_grad((sum(seen_in, ()), self_attn), ([text_rows], [kv_rows]))
            out_total = sum_clips(grad)
            text_keep, text_send = text_back(kv_rows, cross_w, 2, clips)
            quarter = text_keep.shape[1] // 2
            text_seen = text_keep + swap_core(text_send).astype(F32)
            text_came = swap_chip(text_seen[:, quarter:].astype(BF16))
    text_grad = text_seen[:, :quarter] + text_came.astype(F32)
    grad = weight_grad((sum(full_self, ()), self_grads))
    cross_g = sum_terms((cross_shares[0], cross_came), cross_came.shape, most=256)
    ring = RingSum([grad, cross_g], n, table)
    late_terms = [sum_over_tp(*out_terms[c]) for c in both]
    audio_grad, layer_out = [], []
    for c in both:
        grad, sums = norm_backward(0, audio_states[c], grad_in[c], in_terms[c], params, (BF16,))
        norm_sums[0].append(sums)
        audio_grad.append(grad)
        if c == 0:
            ring.step()
    norm_total = SmallSum(jnp.concatenate([sum(v)[:2] for v in norm_sums], 0), n)
    audio_grad = join(audio_grad)
    ring.step()
    norm_total.step()
    layer_out.append(sum_terms((stream_late[0], *late_terms[0]), (share, width)))
    norm_total.step()
    ring.step()
    norm_total.step()
    for c in range(1, clips):
        layer_out.append(sum_terms((stream_late[c], *late_terms[c]), (share, width)))
    norm_total.step()
    layer_out = join(layer_out)
    qkv_total, cross_total = ring.totals((pairs, 3))
    norm_total = norm_total.total()

    def cut(total, begin, count=1):
        return total[:, begin * units : (begin + count) * units]

    return (
        layer_out,
        audio_grad,
        text_grad.astype(BF16),
        qkv_total,
        cut(out_total, 0).astype(F32).T,
        cut(cross_total, 0),
        jnp.stack((cut(out_total, 1), cut(out_total, 2))).astype(F32),
        cut(cross_total, 1).T,
        jnp.concatenate([v[:, :part] for v in ffn_totals], 1).astype(F32),
        jnp.concatenate([v[:, part:] for v in ffn_totals], 1).astype(F32).T,
        norm_total[0::2],
        norm_total[1::2],
    )


def solution(mesh):
    n = mesh.shape["fsdp"]

    def body(*args):
        return local(n, *args)

    return jax.shard_map(
        body,
        mesh=mesh,
        in_specs=(
            P("fsdp", "tp", None),
            P("fsdp", "tp", None),
            P("fsdp", "tp", None),
            P(None, "fsdp", "tp"),
            P("tp", "fsdp"),
            P("fsdp", "tp"),
            P(None, "fsdp", "tp"),
            P("tp", "fsdp"),
            P("fsdp", "tp"),
            P("tp", "fsdp"),
            P(None, "fsdp"),
            P(None, "fsdp"),
        ),
        out_specs=(
            P("fsdp", "tp", None),
            P("fsdp", "tp", None),
            P("fsdp", "tp", None),
            P(None, "fsdp", "tp"),
            P("tp", "fsdp"),
            P("fsdp", "tp"),
            P(None, "fsdp", "tp"),
            P("tp", "fsdp"),
            P("fsdp", "tp"),
            P("tp", "fsdp"),
            P(None, "fsdp"),
            P(None, "fsdp"),
        ),
        check_vma=False,
    )
```

```python
import functools
import math

import jax
import jax.numpy as jnp
from jax import lax
from jax.experimental import pallas as pl
from jax.experimental.pallas import tpu as pltpu
from jax.sharding import PartitionSpec as P

HEAD = 64
PAIR = 2 * HEAD
EPSILON = 1e-05
F32 = jnp.float32
BF16 = jnp.bfloat16
RATE = HEAD ** (-0.5) * math.log2(math.e)
TOKEN = (8, 128)
COST = 1000
VMEM = 52 * 2**20


def swap_chip(values):
    return lax.ppermute(values, "tp", [(t, t ^ 2) for t in range(4)])


def swap_core(values):
    return lax.ppermute(values, "tp", [(t, t ^ 1) for t in range(4)])


def place_of(share, t):
    apart = share ^ t
    return ((apart & 1) << 1) | (apart >> 1)


def gather_rows(values, swapped):
    pair = jnp.concatenate((values, swapped), axis=0)
    return pair, swap_core(pair)


def ring_of(n):
    return list(range(0, n, 2)) + list(range(n - 1, 0, -2))


def ring_place(n):
    i = lax.axis_index("fsdp")
    return jnp.where(i % 2 == 0, i // 2, n - (i + 1) // 2)


def ring_index(n, place):
    place = lax.rem(place + 2 * n, n)
    return jnp.where(place < n // 2, 2 * place, 2 * (n - place) - 1)


def send_next(values, n):
    ring = ring_of(n)
    return lax.ppermute(values, "fsdp", [(ring[k], ring[(k + 1) % n]) for k in range(n)])


def send_prev(values, n):
    ring = ring_of(n)
    return lax.ppermute(values, "fsdp", [(ring[(k + 1) % n], ring[k]) for k in range(n)])


def ring_table(n):
    return ring_index(n, ring_place(n) + jnp.arange(-(n // 2), n // 2 + 1)).astype(jnp.int32)


def place_pieces_body(n, rows, places, *refs):
    pieces, whole = refs[:-1], refs[-1]
    for piece, (step, offset) in zip(pieces, places):
        begin = ring_index(n, ring_place(n) + step) * rows + offset
        size = piece.shape[0]
        whole[pl.ds(pl.multiple_of(begin, math.gcd(rows, size)), size), :] = piece[...]


class RingGather:
    def __init__(self, shard, n):
        self.n, self.shard, self.got = n, shard, []
        self.direct = n > 16 or n % 2

    def step(self):
        if self.direct:
            return ()
        up, down = self.got[-1] if self.got else (self.shard, self.shard)
        if len(self.got) == self.n // 2 - 1:
            half = self.shard.shape[0] // 2
            up, down = up[:half], down[half:]
        self.got.append((send_next(up, self.n), send_prev(down, self.n)))
        return self.got[-1]

    def turn(self, values=(), *wait):
        if self.direct:
            return tick(list(values), *wait) if values else []
        pair = self.got[-1]
        passed = tick([*pair, *values], *wait)
        self.got[-1] = tuple(passed[:2])
        self.step()
        return passed[2:]

    def whole(self, wait=()):
        if self.direct:
            return lax.all_gather(self.shard, "fsdp", axis=0, tiled=True)
        rows, cols = self.shard.shape
        pieces, places = [self.shard], [(0, 0)]
        for k, pair in enumerate(self.got, 1):
            pieces += pair
            places += [(-k, 0), (k, 0 if k < self.n // 2 else rows // 2)]
        size = 768 if cols % 768 == 0 else cols
        return call(
            functools.partial(place_pieces_body, self.n, rows, places),
            (cols // size,),
            pieces,
            [pl.BlockSpec((v.shape[0], size), lambda i: (0, i)) for v in pieces],
            [((self.n * rows, cols), self.shard.dtype)],
            [pl.BlockSpec((self.n * rows, size), lambda i: (0, i))],
                wait=wait,
        )[0]


def ring_body(kind, rows, count, sides, split, *refs):
    table, wholes = refs[0], refs[1 : 1 + count]
    out_count = count if kind == "end" else len(sides)
    came = refs[1 + count : -out_count - count - 1]
    outs, own, sems = refs[-out_count - count - 1 : -count - 1], refs[-count - 1 : -1], refs[-1]
    copies = []
    for side, (entry, first, last) in enumerate(sides):
        begin = pl.multiple_of(table[entry] * rows + first, rows // 2)
        for k in range(count):
            source = wholes[k].at[pl.ds(begin, last - first), :]
            to = own[k].at[side, pl.ds(0, last - first), :]
            copies.append(pltpu.make_async_copy(source, to, sems.at[side, k]))
    for copy in copies:
        copy.start()
    for copy in copies:
        copy.wait()
    half = rows // 2
    for side, (_, first, last) in enumerate(sides):
        begin = 0
        for k in range(count):
            cols = slice(begin, begin + wholes[k].shape[1])
            begin = cols.stop
            mine = own[k][side, : last - first, :]
            if kind == "begin":
                outs[side][:, cols] = mine
            elif kind == "first":
                add = came[side][:, cols].astype(F32)
                here = slice(side * half, (side + 1) * half)
                there = slice((1 - side) * half, (2 - side) * half)
                outs[side][here, cols] = (mine[here].astype(F32) + add).astype(BF16)
                outs[side][there, cols] = mine[there]
            elif kind == "middle":
                add = came[side][:, cols].astype(F32)
                outs[side][:, cols] = (mine.astype(F32) + add).astype(BF16)
            else:
                total = came[0][:, cols].astype(F32) + came[1][:, cols].astype(F32)
                total += mine.astype(F32)
                if k:
                    outs[k][...] = total
                else:
                    outer, inner = split
                    size = total.shape[1] // (outer * inner)
                    for at in range(outer * inner):
                        to = pl.ds(at // inner * size, size)
                        outs[k][at % inner, :, to] = total[:, at * size : (at + 1) * size]


class RingSum:
    def __init__(self, wholes, n, table):
        self.wholes, self.n, self.table = wholes, n, table
        self.direct = n > 16 or n % 2
        self.left = n // 2
        self.came = ()
        self.step()

    def run(self, kind, step, wait=(), split=None):
        rows = self.wholes[0].shape[0] // self.n
        half = rows // 2
        widths = [v.shape[1] for v in self.wholes]
        middle = self.n // 2
        if kind == "end":
            sides = [(middle, 0, rows)]
        elif kind == "begin":
            sides = [(middle + step, 0, half), (middle - step, half, rows)]
        else:
            sides = [(middle + step, 0, rows), (middle - step, 0, rows)]
        size = half if kind == "begin" else rows
        outs = [((size, sum(widths)), BF16)] * len(sides)
        if kind == "end":
            outs = [((split[1], rows, widths[0] // split[1]), F32)]
            outs += [((rows, cols), F32) for cols in widths[1:]]
        hbm = pl.BlockSpec(memory_space=pltpu.HBM)
        return call(
            functools.partial(ring_body, kind, rows, len(widths), sides, split),
            (1,),
            (self.table, *self.wholes, *self.came),
            [pl.BlockSpec(memory_space=pltpu.SMEM)]
            + [hbm] * len(widths)
            + [whole_spec(v.shape) for v in self.came],
            outs,
            [whole_spec(shape) for shape, _ in outs],
            [pltpu.VMEM((len(sides), rows, cols), BF16) for cols in widths]
            + [pltpu.SemaphoreType.DMA((len(sides), len(widths)))],
            wait=wait,
        )

    def step(self, wait=()):
        if self.direct or not self.left:
            return
        if self.left == self.n // 2:
            kind = "begin"
        else:
            kind = "first" if self.left == self.n // 2 - 1 else "middle"
        up, down = self.run(kind, self.left, wait)
        self.came = (send_next(up, self.n), send_prev(down, self.n))
        self.left -= 1

    def totals(self, split):
        if self.direct:
            totals = [
                lax.psum_scatter(v, "fsdp", scatter_dimension=0, tiled=True).astype(F32)
                for v in self.wholes
            ]
            first = totals[0].reshape(totals[0].shape[0], *split, -1).transpose(2, 0, 1, 3)
            return [first.reshape(*first.shape[:2], -1)] + totals[1:]
        while self.left:
            self.step()
        return self.run("end", 0, split=split)


def swap_fsdp(values, n, bit):
    return lax.ppermute(values, "fsdp", [(i, i ^ bit) for i in range(n)])


def small_gather(shard, n):
    if n & (n - 1):
        return lax.all_gather(shard, "fsdp", axis=1, tiled=True)
    found = shard[None]
    bit = 1
    while bit < n:
        found = jnp.concatenate((found, swap_fsdp(found, n, bit)), axis=0)
        bit *= 2
    found = jnp.take(found, jnp.arange(n) ^ lax.axis_index("fsdp"), axis=0)
    return found.transpose(1, 0, 2).reshape(shard.shape[0], -1)


def times(rows, weight):
    return jnp.dot(rows, weight, preferred_element_type=F32)


def times_t(rows, weight):
    return lax.dot_general(rows, weight, (((1,), (1,)), ((), ())), preferred_element_type=F32)


def t_times(left, right):
    return lax.dot_general(left, right, (((0,), (0,)), ((), ())), preferred_element_type=F32)


def whole_spec(shape):
    return pl.BlockSpec(shape, lambda *_: (0,) * len(shape))


class Order:
    token = None


def call(body, grid, ins, in_specs, outs, out_specs, scratch=(), wait=(), alias=None):
    count = len(ins)
    extra = list(wait) + ([Order.token] if Order.token is not None else [])
    any_spec, hbm = (pl.BlockSpec(memory_space=space) for space in (pl.ANY, pltpu.HBM))

    def run(*refs):
        after = refs[count + len(extra) :]
        body(*refs[:count], *after[: len(outs)], *after[len(outs) + 1 :])
        after[len(outs)][...] = jnp.zeros(TOKEN, F32)

    results = pl.pallas_call(
        run,
        grid=grid,
        in_specs=list(in_specs) + [hbm] * len(wait) + [any_spec] * (len(extra) - len(wait)),
        out_specs=list(out_specs) + [whole_spec(TOKEN)],
        scratch_shapes=list(scratch),
        out_shape=[jax.ShapeDtypeStruct(s, d) for s, d in list(outs) + [(TOKEN, F32)]],
        input_output_aliases=alias or {},
        compiler_params=pltpu.CompilerParams(vmem_limit_bytes=VMEM),
        name=getattr(body, "func", body).__name__,
        cost_estimate=pl.CostEstimate(flops=COST, bytes_accessed=0, transcendentals=0),
    )(*ins, *extra)
    Order.token = results[-1]
    return results[:-1]


def head_masks(rows):
    low = lax.broadcasted_iota(jnp.int32, (rows, PAIR), 1) < HEAD
    return low, jnp.logical_not(low)


def split_heads(block, masks):
    zero = jnp.zeros_like(block)
    return [jnp.where(m, block, zero) for m in masks]


def rows_call(body, ins, outs, sums=(), wait=(), shifts=None, most=128):
    rows = outs[0][0][0]
    block = next((v for v in (most, 96) if rows % v == 0), rows)
    steps = rows // block
    shifts = shifts or [0] * len(ins)
    in_specs = []
    for v, shift in zip(ins, shifts):
        if shift is None:
            in_specs.append(whole_spec(v.shape))
        else:
            first = shift // block
            in_specs.append(
                pl.BlockSpec((block, v.shape[1]), functools.partial(lambda f, i: (i + f, 0), first))
            )
    out_specs = [pl.BlockSpec((block, shape[1]), lambda i: (i, 0)) for shape, _ in outs]
    out_specs += [whole_spec(shape) for shape, _ in sums]
    return call(
        body, (steps,), ins, in_specs, list(outs) + list(sums), out_specs, wait=wait
    )


def tick_body(*refs):
    pass


def tick(values, *wait):
    spec = pl.BlockSpec(memory_space=pl.ANY)
    count = len(values)
    return call(
        tick_body,
        (1,),
        values,
        [spec] * count,
        [(v.shape, v.dtype) for v in values],
        [spec] * count,
        wait=wait,
        alias={k: k for k in range(count)},
    )


def copy_body(from_ref, to_ref):
    to_ref[...] = from_ref[...]


def hold(values, wait=()):
    return rows_call(copy_body, (values,), [(values.shape, values.dtype)], wait=wait)[0]


def add_body(keep_ref, seen_ref, out_ref):
    out_ref[...] = (keep_ref[...] + seen_ref[...].astype(F32)).astype(BF16)


def sum_over_tp(keep, send, wait=()):
    seen = swap_core(send)
    half = keep.shape[0] // 2
    (passed,) = rows_call(
        add_body, (keep, seen), [((half, keep.shape[1]), BF16)], shifts=(half, half), wait=wait
    )
    return keep, seen, swap_chip(passed)


def total_of(refs):
    return sum(ref[...].astype(F32) for ref in refs)


def norm_forward_body(index, *refs):
    params, outs = refs[-3], refs[-2:]
    stream = total_of(refs[:-3])
    outs[0][...] = stream
    center = stream - jnp.mean(stream, axis=-1, keepdims=True)
    spread = jnp.mean(center * center, axis=-1, keepdims=True)
    gain, bias = params[index : index + 1, :], params[3 + index : 4 + index, :]
    outs[1][...] = (center * lax.rsqrt(spread + EPSILON) * gain + bias).astype(BF16)


def norm_forward(index, terms, params, rows, wait=()):
    shape = (rows, params.shape[1])
    return rows_call(
        functools.partial(norm_forward_body, index),
        (*terms, params),
        [(shape, F32), (shape, BF16)],
        shifts=[0] * len(terms) + [None],
        wait=wait,
    )


def norm_pair_body(index, left_ref, right_ref, params, *outs):
    gain, bias = params[index : index + 1, :], params[3 + index : 4 + index, :]
    for ref, out in zip((left_ref, right_ref), outs):
        stream = ref[...].astype(F32)
        center = stream - jnp.mean(stream, axis=-1, keepdims=True)
        spread = jnp.mean(center * center, axis=-1, keepdims=True)
        out[...] = (center * lax.rsqrt(spread + EPSILON) * gain + bias).astype(BF16)


def norm_pair(index, pair, params):
    return tuple(
        rows_call(
            functools.partial(norm_pair_body, index),
            (*pair, params),
            [(v.shape, BF16) for v in pair],
            shifts=[0, 0, None],
        )
    )


def norm_backward_body(index, count, *refs):
    stream_ref, base_ref, terms = refs[0], refs[1], refs[2 : 2 + count]
    params, outs, sums = refs[2 + count], refs[3 + count : -1], refs[-1]
    stream = stream_ref[...].astype(F32)
    center = stream - jnp.mean(stream, axis=-1, keepdims=True)
    scale = lax.rsqrt(jnp.mean(center * center, axis=-1, keepdims=True) + EPSILON)
    xhat = center * scale
    grad = total_of(terms)
    e = grad * params[index : index + 1, :]
    back = scale * (
        e - jnp.mean(e, axis=-1, keepdims=True) - xhat * jnp.mean(e * xhat, axis=-1, keepdims=True)
    )
    total = base_ref[...].astype(F32) + back
    for out in outs:
        out[...] = total.astype(out.dtype)

    @pl.when(pl.program_id(0) == 0)
    def _():
        sums[...] = jnp.zeros_like(sums)

    sums[0:1, :] += jnp.sum(grad * xhat, axis=0, keepdims=True)
    sums[1:2, :] += jnp.sum(grad, axis=0, keepdims=True)


def norm_backward(index, stream, base, terms, params, kinds):
    shape = stream.shape
    return rows_call(
        functools.partial(norm_backward_body, index, len(terms)),
        (stream, base, *terms, params),
        [(shape, kind) for kind in kinds],
        [((8, shape[1]), F32)],
        shifts=[0] * (2 + len(terms)) + [None],
    )


def sum_pair_body(left_ref, right_ref, out_ref):
    out_ref[...] = left_ref[...] + right_ref[...]


class SmallSum:
    def __init__(self, whole, n):
        self.whole, self.n = whole, n
        self.swaps = [swap_core, swap_chip]
        if n & (n - 1):
            self.whole = lax.psum(whole, "fsdp")
        else:
            bits = [2**k for k in range(n.bit_length() - 1)]
            self.swaps += [functools.partial(swap_fsdp, n=n, bit=bit) for bit in bits]
        self.came = self.swaps.pop(0)(self.whole)

    def step(self):
        if self.came is None:
            return
        shape = self.whole.shape
        (self.whole,) = call(
            sum_pair_body,
            (1,),
            (self.whole, self.came),
            [whole_spec(shape)] * 2,
            [(shape, F32)],
            [whole_spec(shape)],
        )
        self.came = self.swaps.pop(0)(self.whole) if self.swaps else None

    def total(self):
        while self.came is not None:
            self.step()
        cols = self.whole.shape[1] // self.n
        begin = lax.axis_index("fsdp") * cols
        return lax.dynamic_slice(self.whole, (0, begin), (self.whole.shape[0], cols))


def join_body(count, *refs):
    outs = refs[count]
    for k in range(count):
        outs[k] = refs[k][...]


def join(parts):
    shape, kind = parts[0].shape, parts[0].dtype
    block = 128 if shape[0] % 128 == 0 else shape[0]
    return call(
        functools.partial(join_body, len(parts)),
        (shape[0] // block,),
        parts,
        [pl.BlockSpec((block, shape[1]), lambda i: (i, 0))] * len(parts),
        [((len(parts), *shape), kind)],
        [pl.BlockSpec((len(parts), block, shape[1]), lambda i: (0, i, 0))],
    )[0]


def sum_terms_body(*refs):
    refs[-1][...] = total_of(refs[:-1]).astype(BF16)


def sum_terms(terms, shape, most=128):
    return rows_call(sum_terms_body, terms, [(shape, BF16)], most=most)[0]


def self_forward_body(
    a_ref, b_ref, w_ref, wo_ref, qkv_ref, attn_ref, lse_ref, keep_ref, send_ref, vt_ref
):
    step = pl.program_id(0)
    t = lax.axis_index("tp")
    half = a_ref.shape[0]
    share = half // 2
    qkv_ref[:half, :] = times(a_ref[...], w_ref[...]).astype(BF16)
    qkv_ref[half:, :] = times(b_ref[...], w_ref[...]).astype(BF16)
    vt_ref[...] = qkv_ref[:, 2 * PAIR :].T
    masks = head_masks(share)
    at = [pl.ds(pl.multiple_of(place_of(g, t) * share, share), share) for g in range(4)]
    seen = lax.broadcasted_iota(jnp.int32, (share, share), 0) <= lax.broadcasted_iota(
        jnp.int32, (share, share), 1
    )
    lanes = pl.ds(pl.multiple_of(step * PAIR, PAIR), PAIR)
    for g in range(4):
        queries = split_heads(qkv_ref[at[g], :PAIR], masks)
        found = []
        for e in range(2):
            scores = []
            for b in range(g + 1):
                s = times_t(qkv_ref[at[b], PAIR : 2 * PAIR], queries[e])
                scores.append(jnp.where(seen, s, -1e30) if b == g else s)
            peak = functools.reduce(
                jnp.maximum, [jnp.max(s, axis=0, keepdims=True) for s in scores]
            )
            peak = peak * RATE
            probs = [jnp.exp2(s * RATE - peak) for s in scores]
            total = sum(jnp.sum(p, axis=0, keepdims=True) for p in probs)
            rows = slice(e * HEAD, (e + 1) * HEAD)
            mixed = sum(times(vt_ref[rows, at[b]], probs[b].astype(BF16)) for b in range(g + 1))
            found.append(mixed / total)
            lse_ref[e : e + 1, at[g]] = peak + jnp.log2(total)
        attn_ref[at[g], lanes] = jnp.concatenate(found, 0).T.astype(BF16)

    @pl.when(step == pl.num_programs(0) - 1)
    def _():
        for k in range(2):
            rows = slice(k * share, (k + 1) * share)
            keep_ref[rows, :] = times_t(attn_ref[rows, :], wo_ref[...])
            late = slice(half + k * share, half + (k + 1) * share)
            send_ref[rows, :] = times_t(attn_ref[late, :], wo_ref[...]).astype(BF16)


def self_forward(a, b, weight, units):
    half, width = a.shape
    pairs = units // PAIR
    rows = 2 * half
    return call(
        self_forward_body,
        (pairs,),
        (a, b, weight, weight),
        [
            whole_spec((half, width)),
            whole_spec((half, width)),
            pl.BlockSpec((width, 3 * PAIR), lambda h: (0, h)),
            pl.BlockSpec((width, units), lambda h: (0, 3)),
        ],
        [
            ((rows, 3 * units), BF16),
            ((rows, units), BF16),
            ((8 * pairs, rows), F32),
            ((half, width), F32),
            ((half, width), BF16),
        ],
        [
            pl.BlockSpec((rows, 3 * PAIR), lambda h: (0, h)),
            whole_spec((rows, units)),
            pl.BlockSpec((8, rows), lambda h: (h, 0)),
            whole_spec((half, width)),
            whole_spec((half, width)),
        ],
        [pltpu.VMEM((PAIR, rows), BF16)],
    )


def self_backward_body(
    a_ref, b_ref, wo_ref, w_ref, qkv_ref, attn_ref, lse_ref,
    grads_ref, keep_ref, send_ref, hg_ref, kt_ref, dk_ref, dv_ref,
):
    step = pl.program_id(0)
    t = lax.axis_index("tp")
    half = a_ref.shape[0]
    share = half // 2
    hg_ref[:half, :] = times(a_ref[...], wo_ref[...]).astype(BF16)
    hg_ref[half:, :] = times(b_ref[...], wo_ref[...]).astype(BF16)
    kt_ref[...] = qkv_ref[:, PAIR : 2 * PAIR].T
    dk_ref[...] = jnp.zeros_like(dk_ref)
    dv_ref[...] = jnp.zeros_like(dv_ref)
    masks = head_masks(share)
    at = [pl.ds(pl.multiple_of(place_of(g, t) * share, share), share) for g in range(4)]
    seen = lax.broadcasted_iota(jnp.int32, (share, share), 0) <= lax.broadcasted_iota(
        jnp.int32, (share, share), 1
    )
    base = step * 3 * PAIR
    lanes = [pl.ds(pl.multiple_of(base + c * PAIR, PAIR), PAIR) for c in range(3)]
    for g in range(4):
        queries = split_heads(qkv_ref[at[g], :PAIR], masks)
        block = hg_ref[at[g], :]
        outer = split_heads(block, masks)
        inner = (block.astype(F32) * attn_ref[at[g], :].astype(F32)).T
        query_grad = []
        for e in range(2):
            rows = slice(e * HEAD, (e + 1) * HEAD)
            lse = lse_ref[e : e + 1, at[g]]
            delta = jnp.sum(inner[rows], axis=0, keepdims=True)
            total = jnp.zeros((HEAD, share), F32)
            for b in range(g + 1):
                s = times_t(qkv_ref[at[b], PAIR : 2 * PAIR], queries[e])
                probs = jnp.exp2(s * RATE - lse)
                if b == g:
                    probs = jnp.where(seen, probs, 0.0)
                grad = times_t(qkv_ref[at[b], 2 * PAIR :], outer[e])
                score_grad = (probs * (grad - delta)).astype(BF16)
                dv_ref[at[b], :] += times(probs.astype(BF16), outer[e])
                dk_ref[at[b], :] += times(score_grad, queries[e])
                total += times(kt_ref[rows, at[b]], score_grad)
            query_grad.append(total)
        query_grad = jnp.concatenate(query_grad, 0) * (HEAD ** (-0.5))
        grads_ref[at[g], lanes[0]] = query_grad.T.astype(BF16)
    grads_ref[:, lanes[1]] = (dk_ref[...] * (HEAD ** (-0.5))).astype(BF16)
    grads_ref[:, lanes[2]] = dv_ref[...].astype(BF16)

    @pl.when(step == pl.num_programs(0) - 1)
    def _():
        for k in range(2):
            rows = slice(k * share, (k + 1) * share)
            keep_ref[rows, :] = times_t(grads_ref[rows, :], w_ref[...])
            late = slice(half + k * share, half + (k + 1) * share)
            send_ref[rows, :] = times_t(grads_ref[late, :], w_ref[...]).astype(BF16)


def self_backward(a, b, weight, qkv, attn, lse):
    half, width = a.shape
    units = attn.shape[1]
    pairs = units // PAIR
    rows = 2 * half
    return call(
        self_backward_body,
        (pairs,),
        (a, b, weight, weight, qkv, attn, lse),
        [
            whole_spec((half, width)),
            whole_spec((half, width)),
            pl.BlockSpec((width, PAIR), lambda h: (0, 3 * pairs + h)),
            whole_spec((width, 3 * units)),
            pl.BlockSpec((rows, 3 * PAIR), lambda h: (0, h)),
            pl.BlockSpec((rows, PAIR), lambda h: (0, h)),
            pl.BlockSpec((8, rows), lambda h: (h, 0)),
        ],
        [
            ((rows, 3 * units), BF16),
            ((half, width), F32),
            ((half, width), BF16),
        ],
        [
            whole_spec((rows, 3 * units)),
            whole_spec((half, width)),
            whole_spec((half, width)),
        ],
        [
            pltpu.VMEM((rows, PAIR), BF16),
            pltpu.VMEM((PAIR, rows), BF16),
            pltpu.VMEM((rows, PAIR), F32),
            pltpu.VMEM((rows, PAIR), F32),
        ],
    )


def cross_weight_specs(width, units):
    return [pl.BlockSpec((width, units), functools.partial(lambda j, _: (0, j), j)) for j in (0, 2, 1, 3)]


def cross_probs(keys, queries):
    s = times_t(keys, queries)
    peak = jnp.max(s, axis=0, keepdims=True) * RATE
    probs = jnp.exp2(s * RATE - peak)
    return probs / jnp.sum(probs, axis=0, keepdims=True)


def cross_forward_body(
    a_ref, b_ref, wq0_ref, wq1_ref, wo0_ref, wo1_ref, kv0_ref, kv1_ref,
    q_ref, attn_ref, keep_ref, send_ref,
):
    share = a_ref.shape[0]
    units = wq0_ref.shape[1]
    masks = head_masks(kv0_ref.shape[0])
    keep = send = 0.0
    for j, (wq_ref, wo_ref, kv_ref) in enumerate(
        ((wq0_ref, wo0_ref, kv0_ref), (wq1_ref, wo1_ref, kv1_ref))
    ):
        cols = slice(j * units, (j + 1) * units)
        q_ref[:share, cols] = times(a_ref[...], wq_ref[...]).astype(BF16)
        q_ref[share:, cols] = times(b_ref[...], wq_ref[...]).astype(BF16)
        for begin in range(0, units, PAIR):
            lanes = slice(j * units + begin, j * units + begin + PAIR)
            queries = q_ref[:, lanes]
            keys = split_heads(kv_ref[:, begin : begin + PAIR], masks)
            values = kv_ref[:, units + begin : units + begin + PAIR].T
            mixed = [
                times(
                    values[e * HEAD : (e + 1) * HEAD],
                    cross_probs(keys[e], queries).astype(BF16),
                )
                for e in range(2)
            ]
            attn_ref[:, lanes] = jnp.concatenate(mixed, 0).T.astype(BF16)
        keep += times_t(attn_ref[:share, cols], wo_ref[...])
        send += times_t(attn_ref[share:, cols], wo_ref[...])
    keep_ref[...] = keep
    send_ref[...] = send.astype(BF16)


def cross_forward(a, b, weight, kvs):
    share, width = a.shape
    units = weight.shape[1] // 6
    ins = (a, b, *[weight] * 4, *kvs)
    outs = [
        ((2 * share, 2 * units), BF16),
        ((2 * share, 2 * units), BF16),
        ((share, width), F32),
        ((share, width), BF16),
    ]
    return call(
        cross_forward_body,
        (1,),
        ins,
        [whole_spec(v.shape) for v in ins[:2]]
        + cross_weight_specs(width, units)
        + [whole_spec(v.shape) for v in ins[6:]],
        outs,
        [whole_spec(s) for s, _ in outs],
    )


def cross_backward_body(
    a_ref, b_ref, wq0_ref, wq1_ref, wo0_ref, wo1_ref, kv0_ref, kv1_ref, q_ref,
    dq_ref, own_ref, other_ref, keep_ref, send_ref, hg_ref,
):
    share = a_ref.shape[0]
    units = wq0_ref.shape[1]
    text = kv0_ref.shape[0]
    masks = head_masks(text)
    keep = send = 0.0
    for j, (wq_ref, wo_ref, kv_ref, out_ref) in enumerate(
        ((wq0_ref, wo0_ref, kv0_ref, own_ref), (wq1_ref, wo1_ref, kv1_ref, other_ref))
    ):
        cols = slice(j * units, (j + 1) * units)
        hg_ref[:share, :] = times(a_ref[...], wo_ref[...]).astype(BF16)
        hg_ref[share:, :] = times(b_ref[...], wo_ref[...]).astype(BF16)
        for begin in range(0, units, PAIR):
            lanes = slice(j * units + begin, j * units + begin + PAIR)
            local = slice(begin, begin + PAIR)
            queries = q_ref[:, lanes]
            outer = hg_ref[:, local]
            pair_keys = kv_ref[:, local]
            keys = split_heads(pair_keys, masks)
            values = split_heads(kv_ref[:, units + begin : units + begin + PAIR], masks)
            keys_t = pair_keys.T
            query_grad, key_grad, value_grad = [], [], []
            for e in range(2):
                probs = cross_probs(keys[e], queries)
                grad = times_t(values[e], outer)
                inner = jnp.sum(probs * grad, axis=0, keepdims=True)
                score_grad = (probs * (grad - inner)).astype(BF16)
                query_grad.append(times(keys_t[e * HEAD : (e + 1) * HEAD], score_grad))
                key_grad.append(times(score_grad, queries))
                value_grad.append(times(probs.astype(BF16), outer))
            query_grad = jnp.concatenate(query_grad, 0) * (HEAD ** (-0.5))
            dq_ref[:, lanes] = query_grad.T.astype(BF16)
            key_grad = jnp.where(masks[0], *key_grad) * (HEAD ** (-0.5))
            value_grad = jnp.where(masks[0], *value_grad)
            out_ref[:, local] = key_grad.astype(out_ref.dtype)
            out_ref[:, units + begin : units + begin + PAIR] = value_grad.astype(out_ref.dtype)
        keep += times_t(dq_ref[:share, cols], wq_ref[...])
        send += times_t(dq_ref[share:, cols], wq_ref[...])
    keep_ref[...] = keep
    send_ref[...] = send.astype(BF16)


def cross_backward(a, b, weight, kvs, queries):
    share, width = a.shape
    units = weight.shape[1] // 6
    text = kvs[0].shape[0]
    ins = (a, b, *[weight] * 4, *kvs, queries)
    outs = [
        ((2 * share, 2 * units), BF16),
        ((text, 2 * units), F32),
        ((text, 2 * units), BF16),
        ((share, width), F32),
        ((share, width), BF16),
    ]
    return call(
        cross_backward_body,
        (1,),
        ins,
        [whole_spec(v.shape) for v in ins[:2]]
        + cross_weight_specs(width, units)
        + [whole_spec(v.shape) for v in ins[6:]],
        outs,
        [whole_spec(s) for s, _ in outs],
        [pltpu.VMEM((2 * share, units), BF16)],
    )


def gelu_pair(hidden):
    phi = 0.5 * (1.0 + lax.erf(hidden * (0.5**0.5)))
    density = jnp.exp(-0.5 * hidden * hidden) * 0.3989422804014327
    return hidden * phi, phi + hidden * density


def ffn_products(x, grad, up_ref, down_ref, active_ref, hidden_ref):
    units = up_ref.shape[1]
    size = units // 2 if units % (2 * 128) == 0 else units
    out = back = 0.0
    for begin in range(0, units, size):
        cols = slice(begin, begin + size)
        active, slope = gelu_pair(times(x, up_ref[:, cols]))
        active = active.astype(BF16)
        active_ref[:, cols] = active
        hidden_grad = (times(grad, down_ref[:, cols]) * slope).astype(BF16)
        hidden_ref[:, cols] = hidden_grad
        out += times_t(active, down_ref[:, cols])
        back += times_t(hidden_grad, up_ref[:, cols])
    return out, back


def ffn_first_body(
    xa_ref, xb_ref, ga_ref, gb_ref, up_ref, down_ref, active_ref, hidden_ref, out_ref, back_ref
):
    early = pl.program_id(0) < 2
    x = jnp.where(early, xa_ref[...], xb_ref[...])
    grad = jnp.where(early, ga_ref[...], gb_ref[...])
    out, back = ffn_products(x, grad, up_ref, down_ref, active_ref, hidden_ref)
    out_ref[...] = out
    back_ref[...] = back


def ffn_second_body(
    xa_ref, xb_ref, ga_ref, gb_ref, up_ref, down_ref, out_ref, back_ref,
    active_ref, hidden_ref, out_keep_ref, out_send_ref, keep_ref, send_ref,
):
    early = pl.program_id(0) < 2
    x = jnp.where(early, xa_ref[...], xb_ref[...])
    grad = jnp.where(early, ga_ref[...], gb_ref[...])
    out, back = ffn_products(x, grad, up_ref, down_ref, active_ref, hidden_ref)
    out += out_ref[...]
    back += back_ref[...]

    @pl.when(early)
    def _():
        out_keep_ref[...] = out
        keep_ref[...] = back

    @pl.when(jnp.logical_not(early))
    def _():
        out_send_ref[...] = out.astype(BF16)
        send_ref[...] = back.astype(BF16)


def ffn(x, grad, weight, partial=None):
    half, width = x[0].shape
    share = half // 2
    units = weight.shape[1] // 2
    rows = 2 * half

    def each(i):
        return (i, 0)

    def first(i):
        return (jnp.minimum(i, 1), 0)

    def second(i):
        return (jnp.maximum(i - 2, 0), 0)

    block = (share, width)
    in_specs = [
        pl.BlockSpec(block, first),
        pl.BlockSpec(block, second),
        pl.BlockSpec(block, first),
        pl.BlockSpec(block, second),
        pl.BlockSpec((width, units), lambda i: (0, 0)),
        pl.BlockSpec((width, units), lambda i: (0, 1)),
    ]
    outs = [((rows, units), BF16), ((rows, units), BF16)]
    out_specs = [pl.BlockSpec((share, units), each)] * 2
    if partial is None:
        outs += [((rows, width), F32)] * 2
        out_specs += [pl.BlockSpec(block, each)] * 2
    else:
        in_specs += [pl.BlockSpec(block, each)] * 2
        outs += [((half, width), F32), ((half, width), BF16)] * 2
        out_specs += [pl.BlockSpec(block, first), pl.BlockSpec(block, second)] * 2
    return call(
        ffn_first_body if partial is None else ffn_second_body,
        (4,),
        (*x, *grad, weight, weight, *(partial or ())),
        in_specs,
        outs,
        out_specs,
    )


def weight_grad_body(plan, lefts_count, rights_count, *refs):
    lefts, rights = refs[:lefts_count], refs[lefts_count : lefts_count + rights_count]
    outs = refs[lefts_count + rights_count :]
    begin = 0
    for pairs in plan:
        total = 0.0
        for left, right, first in pairs:
            size = lefts[left].shape[0]
            total += t_times(lefts[left][...], rights[right][first : first + size, :])
        cols = total.shape[1] // len(outs)
        for k, out in enumerate(outs):
            out[:, begin : begin + cols] = total[:, k * cols : (k + 1) * cols].astype(BF16)
        begin += cols


def weight_grad(*parts, split=1):
    lefts, rights, plan = [], [], []
    for part_lefts, part_rights in parts:
        pairs = []
        right = first = 0
        for left in part_lefts:
            pairs.append((len(lefts), len(rights) + right, first))
            lefts.append(left)
            first += left.shape[0]
            if first == part_rights[right].shape[0]:
                right, first = right + 1, 0
        rights += part_rights
        plan.append(pairs)
    width = lefts[0].shape[1]
    cols = sum(part_rights[0].shape[1] for _, part_rights in parts) // split
    size = 256 if width % 256 == 0 else width
    outs = call(
        functools.partial(weight_grad_body, plan, len(lefts), len(rights)),
        (width // size,),
        (*lefts, *rights),
        [pl.BlockSpec((v.shape[0], size), lambda i: (0, i)) for v in lefts]
        + [whole_spec(v.shape) for v in rights],
        [((width, cols), BF16)] * split,
        [pl.BlockSpec((size, cols), lambda i: (i, 0))] * split,
    )
    return outs[0] if split == 1 else outs


def finish_body(early_ref, late_ref, out_ref, up_ref, down_ref, mixed_ref, kv_ref):
    half = early_ref.shape[1] // 2
    for k, ref in enumerate((early_ref, late_ref)):
        cols = slice(k * half, (k + 1) * half)
        up_ref[:, cols] = ref[:, :half].astype(F32)
        down_ref[:, cols] = ref[:, half:].astype(F32)
    units = out_ref.shape[1] // 3
    mixed_ref[...] = out_ref[:, :units].astype(F32)
    for k in range(2):
        kv_ref[k] = out_ref[:, (k + 1) * units : (k + 2) * units].astype(F32)


def finish(early, late, out):
    rows, wide = early.shape
    units = out.shape[1] // 3
    ins = (early, late, out)
    outs = [((rows, wide), F32), ((rows, wide), F32), ((rows, units), F32), ((2, rows, units), F32)]
    specs = [whole_spec(v.shape) for v in ins]
    return call(finish_body, (1,), ins, specs, outs, [whole_spec(s) for s, _ in outs])


def text_project_body(text_ref, weight_ref, out_ref):
    out_ref[...] = times(text_ref[...], weight_ref[...]).astype(BF16)


def text_project(text, weight, block, cols):
    ins = (text, weight)
    specs = [whole_spec(text.shape), pl.BlockSpec((weight.shape[0], cols), lambda i: (0, block))]
    shape = (text.shape[0], cols)
    return call(text_project_body, (1,), ins, specs, [(shape, BF16)], [whole_spec(shape)])[0]


def text_back_body(half, grads_ref, weight_ref, keep_ref, send_ref):
    rows = times_t(grads_ref[...], weight_ref[...])
    for c in range(keep_ref.shape[0]):
        begin = 2 * c * half
        keep_ref[c] = rows[begin : begin + half]
        send_ref[c] = rows[begin + half : begin + 2 * half].astype(BF16)


def text_back(grads, weight, block, clips):
    width, cols = weight.shape[0], grads.shape[1]
    half = grads.shape[0] // clips // 2
    shape = (clips, half, width)
    return call(
        functools.partial(text_back_body, half),
        (1,),
        (grads, weight),
        [whole_spec(grads.shape), pl.BlockSpec((width, cols), lambda i: (0, block))],
        [(shape, F32), (shape, BF16)],
        [whole_spec(shape)] * 2,
    )


def local(
    n,
    audio_states,
    text_states,
    out_grad,
    self_qkv,
    self_out,
    cross_query,
    cross_kv,
    cross_out,
    mlp_up,
    mlp_down,
    norm_gain,
    norm_bias,
):
    clips, share, width = audio_states.shape
    units = self_out.shape[0]
    pairs = units // PAIR
    both = range(clips)

    Order.token = None
    table = ring_table(n)

    qkv_shard = self_qkv.reshape(3, -1, pairs, PAIR).transpose(1, 2, 0, 3).reshape(-1, 3 * units)
    self_ring = RingGather(jnp.concatenate((qkv_shard, self_out.T), 1), n)
    got = self_ring.step()
    params = small_gather(jnp.concatenate((norm_gain, norm_bias), 0), n).astype(F32)
    out_swapped = [swap_chip(out_grad[c]) for c in both]
    cross_own = jnp.concatenate((cross_query, cross_out.T), 1)
    cross_came = swap_chip(cross_own)
    part = mlp_up.shape[1] // 2
    ffn_shards = [
        jnp.concatenate([v[:, k * part : (k + 1) * part] for v in (mlp_up, mlp_down.T)], 1)
        for k in range(2)
    ]

    raw_swapped = [swap_chip(audio_states[c]) for c in both]
    (raw_swapped[0],) = self_ring.turn(raw_swapped[:1], params)
    raw = gather_rows(audio_states[0], raw_swapped[0])
    full_self = [norm_pair(0, raw, params)]
    (cross_came,) = self_ring.turn([cross_came])
    cross_shard = jnp.concatenate((cross_own, cross_came, cross_kv[0], cross_kv[1]), axis=1)
    raw_swapped[1:] = self_ring.turn(raw_swapped[1:])
    raw = [gather_rows(audio_states[c], raw_swapped[c]) for c in range(1, clips)]
    full_self += [norm_pair(0, v, params) for v in raw]
    cross_ring = RingGather(hold(cross_shard, self_ring.got[-1] if self_ring.got else ()), n)
    cross_ring.step()
    self_w = self_ring.whole()
    text_pair = jnp.concatenate((text_states, swap_chip(text_states)), axis=1)
    text_full = jnp.concatenate((text_pair, swap_core(text_pair)), axis=1)
    qkv, self_attn, self_log, mid_terms = [], [], [], []
    for c in both:
        rows, attn, log, keep, send = self_forward(*full_self[c], self_w, units)
        if c == 0:
            send, out_swapped[0] = cross_ring.turn([send, out_swapped[0]])
            seen_out = [gather_rows(out_grad[0], out_swapped[0])]
        else:
            keep_0, seen_0, other_0 = mid_terms[0][1:]
            send, other_0 = cross_ring.turn([send, other_0])
            mid_terms[0] = (audio_states[0], keep_0, seen_0, other_0)
        mid_terms.append((audio_states[c], *sum_over_tp(keep, send)))
        qkv.append(rows)
        self_attn.append(attn)
        self_log.append(log)
    stream_mid, cross_rows = [], []
    for c in both:
        stream, normed = norm_forward(1, mid_terms[c], params, share)
        stream_mid.append(stream)
        cross_rows.append((normed, swap_core(normed)))
        if c == 0:
            cross_ring.turn()
    early_gather = RingGather(hold(ffn_shards[0], cross_ring.got[-1] if cross_ring.got else ()), n)
    early_gather.step()
    cross_w = cross_ring.whole()
    text_rows = text_full.reshape(-1, width)
    text_kv = text_project(text_rows, cross_w, 2, 2 * units).reshape(clips, -1, 2 * units)
    (text_other,) = early_gather.turn([swap_chip(text_kv)])
    cross_q, cross_attn, stream_late, full_ffn = [], [], [], []
    for c in both:
        queries, attn, keep, send = cross_forward(
            *cross_rows[c], cross_w, (text_kv[c], text_other[c])
        )
        if c:
            send, came = early_gather.turn([send, came])
            full_ffn.append(gather_rows(normed_late, came))
        else:
            send, *out_swapped[1:] = early_gather.turn([send, *out_swapped[1:]])
            seen_out += [gather_rows(out_grad[k], out_swapped[k]) for k in range(1, clips)]
        cross_q.append(queries)
        cross_attn.append(attn)
        stream, normed = norm_forward(2, (stream_mid[c], keep, swap_core(send)), params, share)
        stream_late.append(stream)
        normed_late, came = normed, swap_chip(normed)
    late_gather = RingGather(hold(ffn_shards[1], early_gather.got[-1] if early_gather.got else ()), n)
    late_gather.step()
    early_w = early_gather.whole()

    actives, hiddens, partials = [[], []], [[], []], []
    for c in both:
        active, hidden, *partial = ffn(full_ffn[c], seen_out[c], early_w)
        if c == 0:
            (came,) = late_gather.turn([came])
            full_ffn.append(gather_rows(normed_late, came))
        else:
            late_gather.turn()
        actives[0].append(active)
        hiddens[0].append(hidden)
        partials.append(partial)
    grad = weight_grad((sum(full_ffn, ()), hiddens[0]), (sum(seen_out, ()), actives[0]))
    late_gather.turn()
    late_w = late_gather.whole()

    def sum_clips(grad):
        return lax.psum_scatter(grad, "fsdp", scatter_dimension=0, tiled=True)

    (grad,) = tick([grad])
    ffn_totals = [sum_clips(grad)]
    back_terms, out_terms = [], []
    for c in both:
        active, hidden, out_keep, out_send, keep, send = ffn(
            full_ffn[c], seen_out[c], late_w, partials[c]
        )
        if c:
            (send,) = tick([send], back_terms[0][-1])
        back_terms.append(sum_over_tp(keep, send))
        out_terms.append((out_keep, out_send))
        actives[1].append(active)
        hiddens[1].append(hidden)

    norm_sums = [[], [], []]
    grad_mid, grad_in, seen_mid, seen_in = [], [], [], []
    cross_grads, own_kv, other_kv, terms, branches = [], [], [], [], []
    def late_back(c):
        grad, branch, sums = norm_backward(
            2, stream_late[c], out_grad[c], back_terms[c], params, (F32, BF16)
        )
        norm_sums[2].append(sums)
        grad_mid.append(grad)
        seen_mid.append((branch, swap_core(branch)))

    def cross_back(c):
        dq, own, other, keep, send = cross_backward(
            *seen_mid[c], cross_w, (text_kv[c], text_other[c]), cross_q[c]
        )
        cross_grads.append(dq)
        own_kv.append(own)
        other_kv.append(other)
        terms.append((keep, swap_core(send)))

    def mid_back(c):
        grad, branch, sums = norm_backward(
            1, stream_mid[c], grad_mid[c], terms[c], params, (F32, BF16)
        )
        norm_sums[1].append(sums)
        grad_in.append(grad)
        branches.append((branch, swap_chip(branch)))

    late_back(0)
    wide = weight_grad((sum(full_ffn, ()), hiddens[1]), (sum(seen_out, ()), actives[1]))
    wide, other = tick([wide, back_terms[1][-1]])
    back_terms[1] = (*back_terms[1][:-1], other)
    ffn_totals.append(sum_clips(wide))
    for c in both:
        cross_back(c)
        if c + 1 < clips:
            late_back(c + 1)
        mid_back(c)
    kv_came = swap_chip(jnp.stack(other_kv))
    cross_shares = weight_grad(
        (sum(cross_rows, ()), cross_grads), (sum(seen_mid, ()), cross_attn), split=2
    )
    (came,) = tick([branches[0][1]])
    seen_in = [gather_rows(branches[0][0], came)]
    seen_in += [gather_rows(*branches[c]) for c in range(1, clips)]
    cross_came = swap_chip(cross_shares[1])

    self_grads, in_terms, out_sums = [], [], []
    for c in both:
        grads, keep, send = self_backward(
            *seen_in[c], self_w, qkv[c], self_attn[c], self_log[c]
        )
        if c == 0:
            send, kv_came = tick([send, kv_came])
        else:
            (send,) = tick([send])
        in_terms.append(sum_over_tp(keep, send))
        self_grads.append(grads)
        if c == 0:
            kv_grads = (jnp.stack(own_kv) + kv_came.astype(F32)).astype(BF16)
            kv_rows = kv_grads.reshape(-1, 2 * units)
            grad = weight_grad((sum(seen_in, ()), self_attn), ([text_rows], [kv_rows]))
            out_total = sum_clips(grad)
            text_keep, text_send = text_back(kv_rows, cross_w, 2, clips)
            quarter = text_keep.shape[1] // 2
            text_seen = text_keep + swap_core(text_send).astype(F32)
            text_came = swap_chip(text_seen[:, quarter:].astype(BF16))
    grad = weight_grad((sum(full_self, ()), self_grads))
    cross_g = sum_terms((cross_shares[0], cross_came), cross_came.shape, most=256)
    ring = RingSum([grad, cross_g], n, table)
    (text_came,) = tick([text_came])
    text_grad = text_seen[:, :quarter] + text_came.astype(F32)
    late_terms = [sum_over_tp(*out_terms[c]) for c in both]
    audio_grad, layer_out = [], []
    for c in both:
        grad, sums = norm_backward(0, audio_states[c], grad_in[c], in_terms[c], params, (BF16,))
        norm_sums[0].append(sums)
        audio_grad.append(grad)
        if c == 0:
            ring.step()
    norm_total = SmallSum(jnp.concatenate([sum(v)[:2] for v in norm_sums], 0), n)
    audio_grad = join(audio_grad)
    ring.step()
    norm_total.step()
    layer_out.append(sum_terms((stream_late[0], *late_terms[0]), (share, width)))
    norm_total.step()
    ring.step()
    norm_total.step()
    for c in range(1, clips):
        layer_out.append(sum_terms((stream_late[c], *late_terms[c]), (share, width)))
    norm_total.step()
    layer_out = join(layer_out)
    finished = finish(*ffn_totals, out_total)
    qkv_total, cross_total = ring.totals((pairs, 3))
    norm_total = norm_total.total()

    def cut(total, begin, count=1):
        return total[:, begin * units : (begin + count) * units]

    return (
        layer_out,
        audio_grad,
        text_grad.astype(BF16),
        qkv_total,
        finished[2].T,
        cut(cross_total, 0),
        finished[3],
        cut(cross_total, 1).T,
        finished[0],
        finished[1].T,
        norm_total[0::2],
        norm_total[1::2],
    )


def solution(mesh):
    n = mesh.shape["fsdp"]

    def body(*args):
        return local(n, *args)

    return jax.shard_map(
        body,
        mesh=mesh,
        in_specs=(
            P("fsdp", "tp", None),
            P("fsdp", "tp", None),
            P("fsdp", "tp", None),
            P(None, "fsdp", "tp"),
            P("tp", "fsdp"),
            P("fsdp", "tp"),
            P(None, "fsdp", "tp"),
            P("tp", "fsdp"),
            P("fsdp", "tp"),
            P("tp", "fsdp"),
            P(None, "fsdp"),
            P(None, "fsdp"),
        ),
        out_specs=(
            P("fsdp", "tp", None),
            P("fsdp", "tp", None),
            P("fsdp", "tp", None),
            P(None, "fsdp", "tp"),
            P("tp", "fsdp"),
            P("fsdp", "tp"),
            P(None, "fsdp", "tp"),
            P("tp", "fsdp"),
            P("fsdp", "tp"),
            P("tp", "fsdp"),
            P(None, "fsdp"),
            P(None, "fsdp"),
        ),
        check_vma=False,
    )
```
